32 devices in a mesh: section: 2 (over core), dp: 16 (over z, y, x).
Axes of the slice: x: 2, y: 2, z: 4, core: 2. Of those that a mesh axis runs over, the one named last changes fastest.
Arguments:
- ends_in: bfloat16 [2, 8192, 768], P('section', 'dp'), may hold values from -6 to 6
- lengths: int32 [32, 4], P('dp'), may hold values from 0 to 256, as said below
- qkv_weight: bfloat16 [2, 768, 2304], P('section', 'dp'), may hold values from -0.21875 to 0.21875
- qkv_bias: bfloat16 [2, 2304], P('section', 'dp'), may hold values from -1.796875 to 1.796875
- out_weight: bfloat16 [2, 768, 768], P('section', 'dp'), may hold values from -1.75 to 1.75
- up_weight: bfloat16 [2, 768, 3072], P('section', 'dp'), may hold values from -0.21875 to 0.21875
- up_bias: bfloat16 [2, 3072], P('section', 'dp'), may hold values from -1.796875 to 1.796875
- down_weight: bfloat16 [2, 3072, 768], P('section', 'dp'), may hold values from -0.109375 to 0.109375
- out_biases: bfloat16 [2, 2, 768], P('section', None, 'dp'), may hold values from -1.796875 to 1.796875
- norm_gains: bfloat16 [2, 2, 768], P('section', None, 'dp'), may hold values from 0.25 to 1.75
- norm_biases: bfloat16 [2, 2, 768], P('section', None, 'dp'), may hold values from -1.796875 to 1.796875
Outputs:
- ends_out: float32 [2, 8192, 768], P('section', 'dp')
- qkv_weight_grad: float32 [2, 768, 2304], P('section', 'dp')
- qkv_bias_grad: float32 [2, 2304], P('section', 'dp')
- out_weight_grad: float32 [2, 768, 768], P('section', 'dp')
- up_weight_grad: float32 [2, 768, 3072], P('section', 'dp')
- up_bias_grad: float32 [2, 3072], P('section', 'dp')
- down_weight_grad: float32 [2, 3072, 768], P('section', 'dp')
- out_biases_grad: float32 [2, 2, 768], P('section', None, 'dp')
- norm_gains_grad: float32 [2, 2, 768], P('section', None, 'dp')
- norm_biases_grad: float32 [2, 2, 768], P('section', None, 'dp')
The draws below stay inside these ranges and needn't reach their ends.
Inputs may be any that keep to these rules, and one draw needn't show every extreme that they name: `lengths`: row r describes micro-batch r % 2 of data device r // 2: its sequences fill the block's slots in order from slot 0; each row sums to 256 or less, and some row holds a single sequence of 256 tokens.
All inputs are finite; a program needn't handle non-finite values.
Results may differ from the reference program's by a relative error of at most 0.01.
Values may be sent and summed in bfloat16 or wider, within the bound.
No kernel may reach another device: no remote copies, remote signals or barrier semaphores. Data moves between devices by JAX's collectives and lax.ppermute only.
A program may use at most 320 MiB of HBM per device.

```python
import math
import jax
import jax.numpy as jnp
from jax import lax

D = 768
HEADS = 12
HD = 64
ROT = 16
FF = 3072
SLOTS = 256
MICRO = 2
NSEQ = 4
TOKENS = 8192
N_DP = 16


def draw_lengths(key, part):
    key = jax.random.fold_in(key, 7)
    key_filled, key_cuts, key_full = jax.random.split(key, 3)
    blocks = N_DP * MICRO
    filled = jax.random.randint(key_filled, (blocks, 1), SLOTS // 2, SLOTS + 1, dtype=jnp.int32)
    cut_points = jax.random.randint(key_cuts, (blocks, NSEQ - 1), 0, SLOTS + 1, dtype=jnp.int32)
    cut_points = jnp.sort(jnp.minimum(cut_points, filled), axis=1)
    bounds = jnp.concatenate([jnp.zeros((blocks, 1), jnp.int32), cut_points, filled], axis=1)
    pieces = bounds[:, 1:] - bounds[:, :-1]
    chosen = jax.random.randint(key_full, (), 0, blocks, dtype=jnp.int32)
    single = jnp.zeros((NSEQ,), jnp.int32).at[0].set(SLOTS)
    row_index = jnp.arange(blocks, dtype=jnp.int32)[:, None]
    return jnp.where(row_index == chosen, single[None, :], pieces).astype(jnp.int32)


def with_spikes(values, rng, source, target, blocks, factor):
    def block_of(axis_at):
        return (jnp.arange(values.shape[axis_at]) // (values.shape[axis_at] // blocks)).reshape((-1,) + (1,) * (values.ndim - 1 - axis_at))

    first = jax.random.permutation(rng, blocks)[block_of(target)]
    far = (block_of(target) + blocks // 2) % blocks
    return jnp.where((block_of(source) == first) | (block_of(source) == far), factor * values, values)


def level_of(own_key, dims, cuts, smallest, high):
    def one(dim, parts):
        steps = jax.random.uniform(jax.random.fold_in(jax.random.fold_in(own_key, 6), dim), (parts,), jnp.float32, smallest / len(cuts), high / len(cuts))
        return jnp.repeat(jnp.exp(steps), dims[dim] // parts).reshape((-1,) + (1,) * (len(dims) - dim - 1))

    level = one(*cuts[0])
    for cut in cuts[1:]:
        level = level * one(*cut)
    return level


def gaussian(rng, shape, scale, bound, cuts=(), held_as=jnp.bfloat16):
    array = scale * jax.random.normal(rng, shape, jnp.float32)
    if cuts:
        array = array * level_of(rng, shape, cuts, -0.22, 0.18)
    return jnp.clip(array, -bound, bound).astype(held_as)


def bell_draw_with(rng, dims, scale, limit, cuts, heavy, kind=jnp.bfloat16):
    array = scale * jax.random.normal(rng, dims, jnp.float32)
    if cuts:
        array = array * level_of(rng, dims, cuts, -0.22, 0.18)
    return jnp.clip(with_spikes(array, jax.random.fold_in(rng, 3), *heavy), -limit, limit).astype(kind)


def setup_inputs(seed: int = 0) -> dict:
    seeds = jax.random.split(jax.random.key(seed), 12)
    ends_in = bell_draw_with(seeds[0], (2, TOKENS, D), 1.0, 6.0, ((0, 2), (1, 16)), (1, 2, 16, 2.0))
    lengths = draw_lengths(jax.random.fold_in(seeds[11], 71), 0)
    qkv_weight = gaussian(seeds[2], (2, D, 3 * D), D ** -0.5, 0.21875, ((0, 2), (1, 16)))
    qkv_bias = gaussian(seeds[3], (2, 3 * D), 0.3, 1.796875, ((0, 2), (1, 16)))
    out_weight = gaussian(seeds[4], (2, D, D), (D // 64) ** -0.5, 1.75, ((0, 2), (1, 16)))
    up_weight = gaussian(seeds[5], (2, D, FF), D ** -0.5, 0.21875, ((0, 2), (1, 16)))
    up_bias = gaussian(seeds[6], (2, FF), 0.3, 1.796875, ((0, 2), (1, 16)))
    down_weight = gaussian(seeds[7], (2, FF, D), FF ** -0.5, 0.109375, ((0, 2), (1, 16)))
    out_biases = gaussian(seeds[8], (2, 2, D), 0.3, 1.796875, ((0, 2), (2, 16)))
    norm_gains = jnp.clip(1.0 + 0.15 * jax.random.normal(seeds[9], (2, 2, D), jnp.float32), 0.25, 1.75).astype(jnp.bfloat16)
    norm_biases = gaussian(seeds[10], (2, 2, D), 0.3, 1.796875, ((0, 2), (2, 16)))
    return dict(ends_in=ends_in, lengths=lengths, qkv_weight=qkv_weight, qkv_bias=qkv_bias, out_weight=out_weight, up_weight=up_weight, up_bias=up_bias, down_weight=down_weight, out_biases=out_biases, norm_gains=norm_gains, norm_biases=norm_biases)


@jax.custom_vjp
def low(v):
    return lax.optimization_barrier(v.astype(jnp.bfloat16)).astype(jnp.float32)

@jax.custom_vjp
def low_back(v):
    return v

def low_keep(v):
    return (low(v), None)

def low_pass(kept, grad):
    return (grad,)

def back_keep(v):
    return (v, None)

def back_low(kept, grad):
    return (low(grad),)
low.defvjp(low_keep, low_pass)
low_back.defvjp(back_keep, back_low)
eps = 1e-05
masked_score = -1e+30

def product(left, right):
    return jnp.dot(left, right, precision=lax.Precision.HIGHEST)

def block_layout(row_lengths):
    ends_at = jnp.cumsum(row_lengths).astype(jnp.int32)
    indices = jnp.arange(SLOTS, dtype=jnp.int32)
    passed = indices[:, None] >= ends_at[None, :]
    segment = lax.optimization_barrier(jnp.sum(passed.astype(jnp.int32), axis=1)).astype(jnp.int32)
    starts = lax.optimization_barrier(jnp.sum(jnp.where(passed, row_lengths[None, :], 0), axis=1)).astype(jnp.int32)
    return (segment, indices - starts)

def rotary_tables(positions):
    freqs = 10000.0 ** (-2.0 * jnp.arange(ROT // 2, dtype=jnp.float32) / ROT)
    angles = positions.astype(jnp.float32)[..., None] * freqs
    angles = jnp.concatenate([angles, angles], axis=-1)
    return (jnp.cos(angles), jnp.sin(angles))

def rotate(values, cosine, sine_table):
    head_part = values[..., :ROT]
    rest_part = values[..., ROT:]
    half = ROT // 2
    turned = jnp.concatenate([-head_part[..., half:], head_part[..., :half]], axis=-1)
    return jnp.concatenate([head_part * cosine + turned * sine_table, rest_part], axis=-1)

def normalize(residual, gains, shifts):
    centre = lax.optimization_barrier(jnp.mean(residual, axis=-1, keepdims=True))
    centred = residual - centre
    spread = lax.optimization_barrier(jnp.mean(centred * centred, axis=-1, keepdims=True))
    unit_rows = centred * lax.rsqrt(spread + eps)
    return (unit_rows * gains[0] + shifts[0], unit_rows * gains[1] + shifts[1])

def attend_block(item):
    queries, keys_r, values_r, segment = item
    indices = jnp.arange(SLOTS, dtype=jnp.int32)
    allowed = (segment[:, None] == segment[None, :]) & (indices[None, :] <= indices[:, None])
    scores = jnp.einsum('qhd,khd->hqk', queries, keys_r, precision=lax.Precision.HIGHEST) * (1.0 / math.sqrt(HD))
    scores = low_back(scores)
    scores = jnp.where(allowed[None], scores, masked_score)
    row_peak = lax.optimization_barrier(jnp.max(scores, axis=-1, keepdims=True))
    raised = jnp.exp(scores - row_peak)
    probabilities = low(raised / lax.optimization_barrier(jnp.sum(raised, axis=-1, keepdims=True)))
    return jnp.einsum('hqk,khd->qhd', probabilities, values_r, precision=lax.Precision.HIGHEST)

def layer(layer_params, residual, segment, positions):
    weight_qkv, bias_qkv, weight_out, weight_up, bias_up, weight_down, bias_out, gains, shifts = layer_params
    normed_attn, normed_mlp = normalize(residual, gains, shifts)
    normed_attn = low(normed_attn)
    normed_mlp = low(normed_mlp)
    count = residual.shape[0]
    projected = low_back(product(normed_attn.reshape(count * SLOTS, D), weight_qkv) + bias_qkv)
    projected = projected.reshape(count, SLOTS, 3, HEADS, HD)
    cosine, sine_table = rotary_tables(positions)
    cosine = cosine[:, :, None, :]
    sine_table = sine_table[:, :, None, :]
    queries = low(rotate(projected[:, :, 0], cosine, sine_table))
    keys_r = low(rotate(projected[:, :, 1], cosine, sine_table))
    values_r = low(projected[:, :, 2])
    attended = lax.map(jax.checkpoint(attend_block), (queries, keys_r, values_r, segment))
    attended = low_back(low(attended.reshape(count * SLOTS, D)))
    attn_out = product(attended, weight_out) + bias_out[0]
    hidden = low_back(product(normed_mlp.reshape(count * SLOTS, D), weight_up) + bias_up)
    activated = low(jax.nn.gelu(hidden, approximate=False))
    mlp_out = product(activated, weight_down) + bias_out[1]
    return residual + (attn_out + mlp_out).reshape(count, SLOTS, D)

def reference(ends_in, lengths, qkv_weight, qkv_bias, out_weight, up_weight, up_bias, down_weight, out_biases, norm_gains, norm_biases):
    params = tuple((stacked.astype(jnp.float32) for stacked in (qkv_weight, qkv_bias, out_weight, up_weight, up_bias, down_weight, out_biases, norm_gains, norm_biases)))
    blocks = N_DP * MICRO
    group = math.gcd(blocks, max(1, 4096 // SLOTS))
    rounds = blocks // group
    segments, positions = jax.vmap(block_layout)(lengths)
    segments = segments.reshape(rounds, group, SLOTS)
    positions = positions.reshape(rounds, group, SLOTS)
    inputs = ends_in[0].astype(jnp.float32).reshape(rounds, group, SLOTS, D)
    cotangent = ends_in[1].astype(jnp.float32).reshape(rounds, group, SLOTS, D)

    def model(layer_params, rows_in, segment, position_ids):
        lower = jax.tree.map(lambda stacked: stacked[0], layer_params)
        upper = jax.tree.map(lambda stacked: stacked[1], layer_params)
        handed = low_back(low(layer(lower, rows_in, segment, position_ids)))
        return layer(upper, handed, segment, position_ids)

    def accumulate(totals, item):
        rows_in, cot_rows, segment, position_ids = item
        outputs, backward = jax.vjp(lambda layer_params, given_rows: model(layer_params, given_rows, segment, position_ids), params, rows_in)
        grads_params, grads_rows = backward(cot_rows)
        totals = jax.tree.map(jnp.add, totals, grads_params)
        return (totals, (outputs, grads_rows))
    starting = jax.tree.map(jnp.zeros_like, params)
    totals, (outputs, grads_rows) = lax.scan(accumulate, starting, (inputs, cotangent, segments, positions))
    ends_out = jnp.stack([grads_rows.reshape(TOKENS, D), outputs.reshape(TOKENS, D)])
    return (ends_out, totals[0], totals[1], totals[2], totals[3], totals[4], totals[5], totals[6], totals[7], totals[8])
```

```python
from functools import partial
import math

import jax
import jax.numpy as jnp
from jax import lax
from jax.experimental import pallas as pl
from jax.experimental.pallas import tpu as pltpu
from jax.sharding import PartitionSpec as P

HD = 64
ROT = 16


eps = 1e-05
masked_score = -1e30


def product_plain(left, right):
    return jnp.dot(left, right, preferred_element_type=jnp.float32)


def product_transposed(left, right):
    return lax.dot_general(
        left, right, (((1,), (1,)), ((), ())), preferred_element_type=jnp.float32
    )


def product_leftwise(left, right):
    return lax.dot_general(
        left, right, (((0,), (0,)), ((), ())), preferred_element_type=jnp.float32
    )


def layouts(lengths, slot_count):
    ends_at = jnp.cumsum(lengths, axis=1)
    indices = jnp.arange(slot_count, dtype=jnp.int32)
    passed = indices[None, :, None] >= ends_at[:, None, :]
    segments = jnp.sum(passed.astype(jnp.int32), axis=2)
    starts = jnp.sum(jnp.where(passed, lengths[:, None, :], 0), axis=2)
    return (segments, indices[None, :] - starts)


def rotary_tables(positions):
    freqs = 10000.0 ** (-2.0 * jnp.arange(ROT // 2, dtype=jnp.float32) / ROT)
    angles = positions.astype(jnp.float32)[:, None] * freqs[None, :]
    angles = jnp.concatenate([angles, angles], axis=1)
    return (jnp.cos(angles)[:, None, :], jnp.sin(angles)[:, None, :])


def rotate(values, cosine, sine_table):
    head_part = values[..., :ROT]
    half = ROT // 2
    turned = jnp.concatenate([-head_part[..., half:], head_part[..., :half]], axis=-1)
    return jnp.concatenate([head_part * cosine + turned * sine_table, values[..., ROT:]], axis=-1)


def unrotate(grads, cosine, sine_table):
    head_part = grads[..., :ROT]
    half = ROT // 2
    turned = head_part * sine_table
    back_part = jnp.concatenate([turned[..., half:], -turned[..., :half]], axis=-1)
    return jnp.concatenate([head_part * cosine + back_part, grads[..., ROT:]], axis=-1)


def normalize(residual, gains, shifts):
    centre = jnp.mean(residual, axis=-1, keepdims=True)
    centred = residual - centre
    spread = jnp.mean(centred * centred, axis=-1, keepdims=True)
    unit_rows = centred * lax.rsqrt(spread + eps)
    return (unit_rows * gains[0] + shifts[0], unit_rows * gains[1] + shifts[1])


def allowed_mask(segment):
    indices = jnp.arange(segment.shape[0], dtype=jnp.int32)
    return (segment[:, None] == segment[None, :]) & (indices[None, :] <= indices[:, None])


def score_block(query_rows, keys_r, allowed_rows):
    scores = jnp.einsum("qhd,khd->hqk", query_rows, keys_r, preferred_element_type=jnp.float32) * (
        1.0 / math.sqrt(HD)
    )
    return jnp.where(allowed_rows[None], scores, masked_score)


def layer_forward(entry, segment, positions, weights):
    weight_qkv, bias_qkv, weight_out, weight_up, bias_up, weight_down, bias_out, gains, shifts = (
        weights
    )
    residual = entry.astype(jnp.float32)
    normed_attn, normed_mlp = normalize(
        residual, gains.astype(jnp.float32), shifts.astype(jnp.float32)
    )
    length = residual.shape[0]
    features = residual.shape[1]
    head_count = features // HD
    projected = (
        product_plain(normed_attn.astype(jnp.bfloat16), weight_qkv) + bias_qkv.astype(jnp.float32)
    ).reshape(length, 3, head_count, HD)
    cosine, sine_table = rotary_tables(positions)
    queries = rotate(projected[:, 0], cosine, sine_table).astype(jnp.bfloat16)
    keys_r = rotate(projected[:, 1], cosine, sine_table).astype(jnp.bfloat16)
    values_r = projected[:, 2].astype(jnp.bfloat16)
    allowed = allowed_mask(segment)
    scores = score_block(queries, keys_r, allowed)
    row_peak = jnp.max(scores, axis=-1, keepdims=True)
    raised = jnp.exp(scores - row_peak)
    row_total = jnp.sum(raised, axis=-1, keepdims=True)
    probabilities = (raised / row_total).astype(jnp.bfloat16)
    pieces = [
        jnp.einsum("hqk,khd->qhd", probabilities, values_r, preferred_element_type=jnp.float32)
    ]
    log_parts = [(row_peak + jnp.log(row_total))[..., 0]]
    attended = jnp.concatenate(pieces, axis=0).reshape(length, features).astype(jnp.bfloat16)
    log_totals = jnp.concatenate(log_parts, axis=1)
    attn_out = product_plain(attended, weight_out) + bias_out[0].astype(jnp.float32)
    hidden = product_plain(normed_mlp.astype(jnp.bfloat16), weight_up) + bias_up.astype(jnp.float32)
    activated = jax.nn.gelu(hidden, approximate=False).astype(jnp.bfloat16)
    mlp_out = product_plain(activated, weight_down) + bias_out[1].astype(jnp.float32)
    produced = residual + attn_out + mlp_out
    return (produced, (queries, keys_r, values_r, log_totals, attended, hidden, activated))


def mlp_part(grad_in, normed_mlp_r, saved, weights):
    weight_qkv, bias_qkv, weight_out, weight_up, bias_up, weight_down, bias_out, gains, shifts = (
        weights
    )
    queries, keys_r, values_r, log_totals, attended, hidden, activated = saved
    grad_rows = grad_in.astype(jnp.float32)
    column_sum = jnp.sum(grad_rows, axis=0)
    grad_bias_out = jnp.stack([column_sum, column_sum])
    grad_weight_down = product_leftwise(activated, grad_in)
    grad_activated = product_transposed(grad_in, weight_down)
    gelu_value, gelu_back = jax.vjp(partial(jax.nn.gelu, approximate=False), hidden)
    grad_hidden = gelu_back(grad_activated)[0].astype(jnp.bfloat16)
    grad_weight_up = product_leftwise(normed_mlp_r, grad_hidden)
    grad_bias_up = jnp.sum(grad_hidden.astype(jnp.float32), axis=0)
    grad_normed_mlp = product_transposed(grad_hidden, weight_up)
    grad_weight_out = product_leftwise(attended, grad_in)
    return (
        grad_normed_mlp,
        (grad_weight_out, grad_weight_up, grad_bias_up, grad_weight_down, grad_bias_out),
    )


def attn_part(grad_in, normed_attn_r, segment, positions, saved, weights):
    weight_qkv, bias_qkv, weight_out, weight_up, bias_up, weight_down, bias_out, gains, shifts = (
        weights
    )
    queries, keys_r, values_r, log_totals, attended, hidden, activated = saved
    length = grad_in.shape[0]
    features = grad_in.shape[1]
    head_count = features // HD
    scale_factor = 1.0 / math.sqrt(HD)
    grad_attended = (
        product_transposed(grad_in, weight_out).astype(jnp.bfloat16).reshape(length, head_count, HD)
    )
    allowed = allowed_mask(segment)
    cosine, sine_table = rotary_tables(positions)
    scores = score_block(queries, keys_r, allowed)
    probabilities = jnp.exp(scores - log_totals[..., None])
    grad_values = jnp.einsum(
        "hqk,qhd->khd",
        probabilities.astype(jnp.bfloat16),
        grad_attended,
        preferred_element_type=jnp.float32,
    )
    grad_probs = jnp.einsum(
        "qhd,khd->hqk", grad_attended, values_r, preferred_element_type=jnp.float32
    )
    inner_sum = jnp.sum(grad_probs * probabilities, axis=-1, keepdims=True)
    grad_scores = (probabilities * (grad_probs - inner_sum)).astype(jnp.bfloat16)
    query_parts = [
        jnp.einsum("hqk,khd->qhd", grad_scores, keys_r, preferred_element_type=jnp.float32)
        * scale_factor
    ]
    grad_keys = (
        jnp.einsum("hqk,qhd->khd", grad_scores, queries, preferred_element_type=jnp.float32)
        * scale_factor
    )
    grad_queries = unrotate(jnp.concatenate(query_parts, axis=0), cosine, sine_table)
    grad_keys = unrotate(grad_keys, cosine, sine_table)
    grad_projected = (
        jnp.stack([grad_queries, grad_keys, grad_values], axis=1)
        .reshape(length, 3 * features)
        .astype(jnp.bfloat16)
    )
    grad_weight_qkv = product_leftwise(normed_attn_r, grad_projected)
    grad_bias_qkv = jnp.sum(grad_projected.astype(jnp.float32), axis=0)
    grad_normed_attn = product_transposed(grad_projected, weight_qkv)
    return (grad_normed_attn, (grad_weight_qkv, grad_bias_qkv))


def layer_backward(grad_in, entry, segment, positions, saved, weights):
    gains = weights[7]
    shifts = weights[8]
    residual = entry.astype(jnp.float32)
    (normed_attn, normed_mlp), norm_back = jax.vjp(
        normalize, residual, gains.astype(jnp.float32), shifts.astype(jnp.float32)
    )
    grad_normed_mlp, mlp_grads = mlp_part(grad_in, normed_mlp.astype(jnp.bfloat16), saved, weights)
    grad_normed_attn, attn_grads = attn_part(
        grad_in, normed_attn.astype(jnp.bfloat16), segment, positions, saved, weights
    )
    grad_residual, grad_gains, grad_shifts = norm_back((grad_normed_attn, grad_normed_mlp))
    grads_layer = (
        attn_grads[0],
        attn_grads[1],
        mlp_grads[0],
        mlp_grads[1],
        mlp_grads[2],
        mlp_grads[3],
        mlp_grads[4],
        grad_gains,
        grad_shifts,
    )
    return (grad_in.astype(jnp.float32) + grad_residual, grads_layer)


SQUARE = 4
RING = 4


def swap_cores(value):
    return lax.ppermute(value, "section", [(0, 1), (1, 0)])


def swap_square(value, bit):
    count = lax.axis_size("dp")
    return lax.ppermute(value, "dp", [(i, i ^ bit) for i in range(count)])


def ring_on(value):
    count = lax.axis_size("dp")
    return lax.ppermute(value, "dp", [(i, (i + SQUARE) % count) for i in range(count)])


def small_slice():
    return lax.axis_size("dp") == SQUARE * RING


def place_kernel(spot_ref, own, first, second, far_low, far_high, out, sems):
    spot = spot_ref[0]
    half = RING // 2
    copies = [
        pltpu.make_async_copy(own, out.at[:, spot], sems.at[0]),
        pltpu.make_async_copy(first, out.at[:, spot ^ 1], sems.at[1]),
        pltpu.make_async_copy(second, out.at[:, spot ^ 2], sems.at[2]),
        pltpu.make_async_copy(far_low, out.at[pl.ds(0, half), spot ^ 3], sems.at[3]),
        pltpu.make_async_copy(far_high, out.at[pl.ds(half, half), spot ^ 3], sems.at[4]),
    ]
    for copy in copies:
        copy.start()
    for copy in copies:
        copy.wait()


def place_blocks(spot, blocks):
    _, rows, columns = blocks[0].shape
    any_space = pl.BlockSpec(memory_space=pl.ANY)
    return pl.pallas_call(
        place_kernel,
        out_shape=jax.ShapeDtypeStruct((RING, SQUARE, rows, columns), blocks[0].dtype),
        in_specs=[pl.BlockSpec(memory_space=pltpu.SMEM)] + [any_space] * 5,
        out_specs=any_space,
        scratch_shapes=[pltpu.SemaphoreType.DMA((5,))],
        name="place_blocks",
    )(spot, *blocks)


def gather_rows(piece):
    rows, columns = piece.shape
    if not small_slice():
        return lax.all_gather(piece, "dp", axis=0, tiled=True)
    place = lax.axis_index("dp")
    level = place // SQUARE
    spot = (place % SQUARE).astype(jnp.int32).reshape(1)
    held = [piece]
    for _ in range(RING - 1):
        held.append(ring_on(held[-1]))
    doubled = jnp.stack([held[3], held[2], held[1], held[0], held[3], held[2], held[1]])
    column = lax.dynamic_slice_in_dim(doubled, RING - 1 - level, RING, 0)
    first = swap_square(column, 1)
    second = swap_square(column, 2)
    half = RING // 2
    far_low = swap_square(first[:half], 2)
    far_high = swap_square(second[half:], 1)
    whole = place_blocks(spot, (column, first, second, far_low, far_high))
    return whole.reshape(RING * SQUARE * rows, columns)


def scatter_rows(summed):
    rows = summed.shape[0] // lax.axis_size("dp")
    columns = summed.shape[1]
    if not small_slice():
        return lax.psum_scatter(summed, "dp", scatter_dimension=0, tiled=True)
    place = lax.axis_index("dp")
    level = place // SQUARE
    spot = place % SQUARE
    blocks = summed.reshape(RING, SQUARE, rows, columns)

    def block(index):
        return lax.dynamic_index_in_dim(blocks, index, 1, keepdims=False)

    half = RING // 2
    wire = jnp.bfloat16
    far = block(spot ^ 3).astype(wire)
    far_low = swap_square(far[:half], 1)
    far_high = swap_square(far[half:], 2)
    first = block(spot ^ 1)
    second = block(spot ^ 2)
    first = jnp.concatenate([first[:half], first[half:] + far_high.astype(jnp.float32)])
    second = jnp.concatenate([second[:half] + far_low.astype(jnp.float32), second[half:]])
    from_first = swap_square(first.astype(wire), 1)
    from_second = swap_square(second.astype(wire), 2)
    column = block(spot) + from_first.astype(jnp.float32) + from_second.astype(jnp.float32)

    def rung(back):
        return lax.dynamic_index_in_dim(column, (level - back) % RING, 0, keepdims=False)

    travelling = rung(1)
    for step in range(1, RING):
        travelling = ring_on(travelling.astype(wire)).astype(jnp.float32) + rung(step + 1)
    return travelling


def halves_joined(is_first, mine, other):
    return jnp.where(
        is_first, jnp.concatenate([mine, other], axis=1), jnp.concatenate([other, mine], axis=1)
    )


def half_of(array, which):
    width = array.shape[1] // 2
    return lax.dynamic_slice_in_dim(array, which * width, width, 1)


def half_slots(array, which):
    length = array.shape[0] // 2
    return lax.dynamic_slice_in_dim(array, which * length, length, 0)


def on_device(
    ends_in,
    lengths,
    qkv_weight,
    qkv_bias,
    out_weight,
    up_weight,
    up_bias,
    down_weight,
    out_biases,
    norm_gains,
    norm_biases,
):
    section_index = lax.axis_index("section")
    is_first = section_index == 0
    features = ends_in.shape[2]
    count = lax.axis_size("dp")
    own_rows = ends_in[0]
    slot_count = own_rows.shape[0] // 2
    kept_rows = half_slots(own_rows, section_index)
    other_rows = swap_cores(half_slots(own_rows, 1 - section_index))
    entry = jnp.where(is_first, kept_rows, other_rows)
    cotangent = jnp.where(is_first, other_rows, kept_rows)
    segments, positions = layouts(lengths, slot_count)
    segment = lax.dynamic_index_in_dim(segments, section_index, 0, keepdims=False)
    position = lax.dynamic_index_in_dim(positions, section_index, 0, keepdims=False)

    def both(shard):
        kept = half_of(shard, section_index)
        other = swap_cores(half_of(shard, 1 - section_index))
        return (jnp.where(is_first, kept, other), jnp.where(is_first, other, kept))

    small_shapes = [
        (qkv_bias.shape[1],),
        (up_bias.shape[1],),
        out_biases.shape[1:],
        norm_gains.shape[1:],
        norm_biases.shape[1:],
    ]
    small_own = jnp.concatenate(
        [a[0].reshape(-1) for a in (qkv_bias, up_bias, out_biases, norm_gains, norm_biases)]
    )
    small_other = swap_cores(small_own)
    small_both = jnp.where(
        is_first,
        jnp.concatenate([small_own, small_other]),
        jnp.concatenate([small_other, small_own]),
    )
    small_full = gather_rows(small_both[None])
    small_full = small_full.reshape(count, 2, small_own.shape[0])

    def small_of(layer):
        rows = small_full[:, layer]
        found = []
        at = 0
        for shape in small_shapes:
            size = math.prod(shape)
            part = rows[:, at : at + size].reshape((count,) + shape)
            at += size
            if len(shape) == 2:
                part = part.transpose(1, 0, 2).reshape(shape[0], count * shape[1])
            else:
                part = part.reshape(count * shape[0])
            found.append(part)
        return found

    narrow = jnp.concatenate([qkv_weight[0], out_weight[0]], axis=1)
    pieces = (both(qkv_weight[0]), both(out_weight[0]), both(up_weight[0]), both(down_weight[0]))
    qkv_width = qkv_weight.shape[2]
    weights = []
    for layer in range(2):
        joined = []
        packed = (
            jnp.concatenate([pieces[0][layer], pieces[1][layer]], axis=1),
            pieces[2][layer],
            pieces[3][layer],
        )
        for piece in packed:
            mine = gather_rows(piece)
            joined.append((mine, swap_cores(mine)))
        cut = qkv_width // 2
        weight_qkv = halves_joined(is_first, joined[0][0][:, :cut], joined[0][1][:, :cut])
        weight_out = halves_joined(is_first, joined[0][0][:, cut:], joined[0][1][:, cut:])
        weight_up = halves_joined(is_first, *joined[1])
        weight_down = halves_joined(is_first, *joined[2])
        bias_qkv, bias_up, bias_out, gains, shifts = small_of(layer)
        weights.append(
            (
                weight_qkv,
                bias_qkv,
                weight_out,
                weight_up,
                bias_up,
                weight_down,
                bias_out,
                gains,
                shifts,
            )
        )

    middle, saved_lower = layer_forward(entry, segment, position, weights[0])
    middle = middle.astype(jnp.bfloat16)
    produced, saved_upper = layer_forward(middle, segment, position, weights[1])
    grad_middle, grads_upper = layer_backward(
        cotangent, middle, segment, position, saved_upper, weights[1]
    )
    grad_entry, grads_lower = layer_backward(
        grad_middle.astype(jnp.bfloat16), entry, segment, position, saved_lower, weights[0]
    )

    def reduce_half(*grads):
        sent = [half_of(g, 1 - section_index).astype(jnp.bfloat16) for g in grads]
        kept = [half_of(g, section_index).astype(jnp.float32) for g in grads]
        sent = jnp.concatenate(sent, axis=1) if len(sent) > 1 else sent[0]
        kept = jnp.concatenate(kept, axis=1) if len(kept) > 1 else kept[0]
        return scatter_rows(kept + swap_cores(sent).astype(jnp.float32))

    reduced = []
    for grads in (grads_upper, grads_lower):
        down = reduce_half(grads[5])
        up = reduce_half(grads[3])
        narrow = reduce_half(grads[0], grads[2])
        reduced.append((narrow, up, down))
    reduced = reduced[::-1]

    def finish(upper_lower):
        lower, upper = upper_lower
        mine = jnp.where(is_first, lower, upper)
        other = swap_cores(jnp.where(is_first, upper, lower))
        return halves_joined(is_first, mine, other)

    cut = qkv_width // 2
    total_qkv = finish((reduced[0][0][:, :cut], reduced[1][0][:, :cut]))
    total_out = finish((reduced[0][0][:, cut:], reduced[1][0][:, cut:]))
    total_up = finish((reduced[0][1], reduced[1][1]))
    total_down = finish((reduced[0][2], reduced[1][2]))

    def small_rows(grads):
        parts = []
        for index in (1, 4, 6, 7, 8):
            grad = grads[index].astype(jnp.float32)
            if grad.ndim == 2:
                part = grad.reshape(grad.shape[0], count, -1).transpose(1, 0, 2)
                parts.append(part.reshape(count, -1))
            else:
                parts.append(grad.reshape(count, -1))
        return jnp.concatenate(parts, axis=1)

    small_lower = small_rows(grads_lower)
    small_upper = small_rows(grads_upper)
    small_kept = jnp.where(is_first, small_lower, small_upper)
    small_sent = jnp.where(is_first, small_upper, small_lower)
    small_total = scatter_rows(small_kept + swap_cores(small_sent))[0]
    small_outs = []
    at = 0
    for shape in small_shapes:
        size = math.prod(shape)
        small_outs.append(small_total[at : at + size].reshape((1,) + shape))
        at += size

    crossing = swap_cores(jnp.where(is_first, produced, grad_entry))
    staying = jnp.where(is_first, grad_entry, produced)
    ends_out = jnp.where(
        is_first,
        jnp.concatenate([staying, crossing]),
        jnp.concatenate([crossing, staying]),
    )
    return (
        ends_out[None],
        total_qkv[None],
        small_outs[0],
        total_out[None],
        total_up[None],
        small_outs[1],
        total_down[None],
        small_outs[2],
        small_outs[3],
        small_outs[4],
    )


def solution(mesh):
    return jax.shard_map(
        on_device,
        mesh=mesh,
        in_specs=(
            P("section", "dp", None),
            P("dp", None),
            P("section", "dp", None),
            P("section", "dp"),
            P("section", "dp", None),
            P("section", "dp", None),
            P("section", "dp"),
            P("section", "dp", None),
            P("section", None, "dp"),
            P("section", None, "dp"),
            P("section", None, "dp"),
        ),
        out_specs=(
            P("section", "dp", None),
            P("section", "dp", None),
            P("section", "dp"),
            P("section", "dp", None),
            P("section", "dp", None),
            P("section", "dp"),
            P("section", "dp", None),
            P("section", None, "dp"),
            P("section", None, "dp"),
            P("section", None, "dp"),
        ),
        check_vma=False,
    )
```

```python
import math

import jax
import jax.numpy as jnp
from jax import lax
from jax.experimental import pallas as pl
from jax.experimental.pallas import tpu as pltpu
from jax.sharding import PartitionSpec as P

HD = 64
ROT = 16
LANES = 128
TILES = 3


eps = 1e-05
masked_score = -1e30
vmem_bytes = 48 * 1024 * 1024


def product(left, right):
    return jnp.dot(left, right, preferred_element_type=jnp.float32)


def product_transposed(left, right):
    return lax.dot_general(
        left, right, (((1,), (1,)), ((), ())), preferred_element_type=jnp.float32
    )


def layouts(lengths, slot_count):
    ends_at = jnp.cumsum(lengths)
    indices = jnp.arange(slot_count, dtype=jnp.int32)
    passed = indices[:, None] >= ends_at[None, :]
    segments = jnp.sum(passed.astype(jnp.int32), axis=1)
    starts = jnp.sum(jnp.where(passed, lengths[None, :], 0), axis=1)
    return (segments, indices - starts)


def rotary_tables(positions):
    lane = jnp.arange(LANES, dtype=jnp.int32) % HD
    half = ROT // 2
    freqs = 10000.0 ** (-2.0 * (lane % half).astype(jnp.float32) / ROT)
    angles = positions.astype(jnp.float32)[:, None] * freqs[None, :]
    cosine = jnp.where(lane < ROT, jnp.cos(angles), 1.0)
    sine = jnp.sin(angles)
    ahead = jnp.where(lane < half, -sine, 0.0)
    behind = jnp.where((lane >= half) & (lane < ROT), sine, 0.0)
    return jnp.stack([cosine, ahead, behind])


def allowed_transposed(segment):
    indices = jnp.arange(segment.shape[0], dtype=jnp.int32)
    allowed = (segment[:, None] == segment[None, :]) & (indices[:, None] <= indices[None, :])
    return allowed.astype(jnp.float32)


def turned(values, tables, back):
    half = ROT // 2
    parts = []
    for at in range(0, values.shape[1], LANES):
        part = values[:, at : at + LANES]
        moved = (
            pltpu.roll(part, LANES - half, 1) * tables[1] + pltpu.roll(part, half, 1) * tables[2]
        )
        kept = part * tables[0]
        parts.append(kept - moved if back else kept + moved)
    return jnp.concatenate(parts, axis=1)


def unit_rows(rows):
    centred = rows - jnp.mean(rows, axis=-1, keepdims=True)
    spread = jnp.mean(centred * centred, axis=-1, keepdims=True)
    scale = lax.rsqrt(spread + eps)
    return (centred * scale, scale)


def lane_half(which, width):
    return pl.ds(pl.multiple_of(which * width, LANES), width)


def head_lanes(values, which):
    lane = lax.broadcasted_iota(jnp.int32, values.shape, 1)
    return jnp.where((lane < HD) == (which == 0), values, jnp.zeros_like(values))


def scores_of(key_pair, query_pair, which, allowed):
    scores = product_transposed(head_lanes(key_pair, which), query_pair) * (1.0 / math.sqrt(HD))
    return jnp.where(allowed, scores, masked_score)


def attn_forward_kernel(
    side, rows, tables, mask, norms, bias_qkv, bias_out, mine, other, qkv, logs, attended, passed
):
    width = mine.shape[1] // 4
    entry = rows[...].astype(jnp.float32)
    unit, _ = unit_rows(entry)
    normed = (unit * norms[0:1] + norms[2:3]).astype(jnp.bfloat16)
    allowed = mask[...] > 0.5
    for at, weight in enumerate((mine, other)):
        half = side[0] if at == 0 else 1 - side[0]
        parts = []
        for part in range(3):
            cut = slice(part * width, (part + 1) * width)
            value = product(normed, weight[:, cut]) + bias_qkv[at : at + 1, cut]
            if part < 2:
                value = turned(value, tables, False)
            value = value.astype(jnp.bfloat16)
            qkv[at, :, cut] = value
            parts.append(value)
        queries, keys, values = parts
        values = values.T
        outs = []
        for pair in range(width // LANES):
            cut = slice(pair * LANES, (pair + 1) * LANES)
            for which in range(2):
                head = 2 * pair + which
                scores = scores_of(keys[:, cut], queries[:, cut], which, allowed)
                peak = jnp.max(scores, axis=0, keepdims=True)
                raised = jnp.exp(scores - peak)
                total = jnp.sum(raised, axis=0, keepdims=True)
                chances = (raised * (1.0 / total)).astype(jnp.bfloat16)
                outs.append(product(values[head * HD : (head + 1) * HD], chances))
                logs[at, head : head + 1, :] = peak + jnp.log(total)
        mixed = jnp.concatenate(outs, axis=0).T.astype(jnp.bfloat16)
        attended[:, lane_half(half, width)] = mixed
    mixed = attended[...]
    for at, weight in enumerate((mine, other)):
        half = side[0] if at == 0 else 1 - side[0]
        lanes = lane_half(half, width)
        passed[:, lanes] = (
            rows[:, lanes].astype(jnp.float32)
            + product(mixed, weight[:, 3 * width :])
            + bias_out[0:1, lanes]
        )


def whole_blocks(count):
    return [pl.BlockSpec(memory_space=pltpu.VMEM)] * count


def attn_forward(side, rows, tables, mask, small, mine, other):
    length, features = rows.shape
    width = features // 2
    heads = width // HD
    return pl.pallas_call(
        attn_forward_kernel,
        out_shape=(
            jax.ShapeDtypeStruct((2, length, 3 * width), jnp.bfloat16),
            jax.ShapeDtypeStruct((2, heads, length), jnp.float32),
            jax.ShapeDtypeStruct((length, features), jnp.bfloat16),
            jax.ShapeDtypeStruct((length, features), jnp.float32),
        ),
        in_specs=[pl.BlockSpec(memory_space=pltpu.SMEM)] + whole_blocks(8),
        out_specs=tuple(whole_blocks(4)),
        compiler_params=pltpu.CompilerParams(vmem_limit_bytes=vmem_bytes),
        cost_estimate=pl.CostEstimate(
            flops=2 * length * features * features * 5,
            bytes_accessed=8 * features * features,
            transcendentals=length * length * features // HD,
        ),
        name="attn_forward",
    )(side, rows, tables, mask, small["norms"], small["qkv"], small["out"], mine, other)


def tile_of(step, side):
    half = jnp.where(step < TILES, side[0], 1 - side[0])
    return half * TILES + step % TILES


def first_tile(step):
    return jnp.minimum(step, TILES - 1)


def second_tile(step):
    return jnp.maximum(step - TILES, 0)


def mlp_forward_kernel(
    side, rows, passed, norms, bias_up, bias_out, up_mine, up_other, down_mine, down_other,
    active, slope, produced, normed, sum_mine, sum_other
):
    step = pl.program_id(0)

    @pl.when(step == 0)
    def _():
        unit, _ = unit_rows(rows[...].astype(jnp.float32))
        normed[...] = (unit * norms[1:2] + norms[3:4]).astype(jnp.bfloat16)
        sum_mine[...] = jnp.zeros_like(sum_mine)
        sum_other[...] = jnp.zeros_like(sum_other)

    weight = jnp.where(step < TILES, up_mine[...], up_other[...])
    hidden = product(normed[...], weight) + bias_up[...]
    bell = 0.5 * (1.0 + lax.erf(hidden * (1.0 / math.sqrt(2.0))))
    density = jnp.exp(-0.5 * hidden * hidden) * (1.0 / math.sqrt(2.0 * math.pi))
    slope[...] = bell + hidden * density
    lit = (hidden * bell).astype(jnp.bfloat16)
    active[...] = lit
    sum_mine[...] += product(lit, down_mine[...])
    sum_other[...] += product(lit, down_other[...])

    @pl.when(step == 2 * TILES - 1)
    def _():
        width = sum_mine.shape[1]
        for half, total in ((side[0], sum_mine), (1 - side[0], sum_other)):
            lanes = lane_half(half, width)
            produced[:, lanes] = (
                passed[:, lanes] + total[...] + bias_out[1:2, lanes]
            ).astype(produced.dtype)


def mlp_forward(side, rows, passed, small, weights, kind):
    up_mine, up_other, down_mine, down_other = weights
    length, features = rows.shape
    hidden = down_mine.shape[0]
    tile = hidden // (2 * TILES)
    width = features // 2

    def fixed(*shape):
        return pl.BlockSpec(shape, lambda step, side: (0,) * len(shape))

    tiled = pl.BlockSpec((length, tile), lambda step, side: (0, tile_of(step, side)))
    down_spec = pl.BlockSpec((tile, width), lambda step, side: (tile_of(step, side), 0))
    return pl.pallas_call(
        mlp_forward_kernel,
        out_shape=(
            jax.ShapeDtypeStruct((length, hidden), jnp.bfloat16),
            jax.ShapeDtypeStruct((length, hidden), jnp.float32),
            jax.ShapeDtypeStruct((length, features), kind),
        ),
        grid_spec=pltpu.PrefetchScalarGridSpec(
            num_scalar_prefetch=1,
            grid=(2 * TILES,),
            in_specs=[
                fixed(length, features),
                fixed(length, features),
                fixed(4, features),
                pl.BlockSpec((1, tile), lambda step, side: (0, tile_of(step, side))),
                fixed(2, features),
                pl.BlockSpec((features, tile), lambda step, side: (0, first_tile(step))),
                pl.BlockSpec((features, tile), lambda step, side: (0, second_tile(step))),
                down_spec,
                down_spec,
            ],
            out_specs=(tiled, tiled, fixed(length, features)),
            scratch_shapes=[
                pltpu.VMEM((length, features), jnp.bfloat16),
                pltpu.VMEM((length, width), jnp.float32),
                pltpu.VMEM((length, width), jnp.float32),
            ],
        ),
        compiler_params=pltpu.CompilerParams(vmem_limit_bytes=vmem_bytes),
        cost_estimate=pl.CostEstimate(
            flops=4 * length * features * hidden,
            bytes_accessed=4 * features * hidden + 6 * length * hidden,
            transcendentals=2 * length * hidden,
        ),
        name="mlp_forward",
    )(
        side, rows, passed, small["norms"], small["up"], small["out"],
        up_mine, up_other, down_mine, down_other,
    )


def mlp_backward_kernel(
    side, rows, grad, norms, active, slope, up_mine, up_other, down_mine, down_other,
    up_kept, up_sent, down_kept, down_sent, bias_grad, grad_normed, normed
):
    step = pl.program_id(0)
    width = down_mine.shape[1]

    @pl.when(step == 0)
    def _():
        unit, _ = unit_rows(rows[...].astype(jnp.float32))
        normed[...] = (unit * norms[1:2] + norms[3:4]).T.astype(jnp.bfloat16)
        grad_normed[...] = jnp.zeros_like(grad_normed)

    grad_mine = grad[:, lane_half(side[0], width)]
    grad_other = grad[:, lane_half(1 - side[0], width)]
    weight = jnp.where(step < TILES, up_mine[...], up_other[...])
    lit = active[...].T
    down_kept[...] = product(lit, grad_mine).astype(jnp.bfloat16)
    down_sent[...] = product(lit, grad_other).astype(jnp.bfloat16)
    back = product_transposed(grad_mine, down_mine[...])
    back += product_transposed(grad_other, down_other[...])
    back = (back * slope[...]).astype(jnp.bfloat16)
    bias_grad[...] = jnp.sum(back.astype(jnp.float32), axis=0, keepdims=True)
    up_grad = product(normed[...], back).astype(jnp.bfloat16)

    @pl.when(step < TILES)
    def _():
        up_kept[...] = up_grad

    @pl.when(step >= TILES)
    def _():
        up_sent[...] = up_grad

    grad_normed[...] += product_transposed(back, weight)


def mlp_backward(side, rows, grad, small, saved, weights):
    active, slope = saved
    up_mine, up_other, down_mine, down_other = weights
    length, features = rows.shape
    hidden = down_mine.shape[0]
    tile = hidden // (2 * TILES)
    width = features // 2

    def fixed(*shape):
        return pl.BlockSpec(shape, lambda step, side: (0,) * len(shape))

    tiled = pl.BlockSpec((length, tile), lambda step, side: (0, tile_of(step, side)))
    down_spec = pl.BlockSpec((tile, width), lambda step, side: (tile_of(step, side), 0))
    up_first = pl.BlockSpec((features, tile), lambda step, side: (0, first_tile(step)))
    up_second = pl.BlockSpec((features, tile), lambda step, side: (0, second_tile(step)))
    return pl.pallas_call(
        mlp_backward_kernel,
        out_shape=(
            jax.ShapeDtypeStruct((features, hidden // 2), jnp.bfloat16),
            jax.ShapeDtypeStruct((features, hidden // 2), jnp.bfloat16),
            jax.ShapeDtypeStruct((hidden, width), jnp.bfloat16),
            jax.ShapeDtypeStruct((hidden, width), jnp.bfloat16),
            jax.ShapeDtypeStruct((1, hidden), jnp.float32),
            jax.ShapeDtypeStruct((length, features), jnp.float32),
        ),
        grid_spec=pltpu.PrefetchScalarGridSpec(
            num_scalar_prefetch=1,
            grid=(2 * TILES,),
            in_specs=[
                fixed(length, features),
                fixed(length, features),
                fixed(4, features),
                tiled,
                tiled,
                up_first,
                up_second,
                down_spec,
                down_spec,
            ],
            out_specs=(
                up_first,
                up_second,
                down_spec,
                down_spec,
                pl.BlockSpec((1, tile), lambda step, side: (0, tile_of(step, side))),
                fixed(length, features),
            ),
            scratch_shapes=[pltpu.VMEM((features, length), jnp.bfloat16)],
        ),
        compiler_params=pltpu.CompilerParams(vmem_limit_bytes=vmem_bytes),
        cost_estimate=pl.CostEstimate(
            flops=8 * length * features * hidden,
            bytes_accessed=8 * features * hidden + 6 * length * hidden,
            transcendentals=0,
        ),
        name="mlp_backward",
    )(
        side, rows, grad, small["norms"], active, slope,
        up_mine, up_other, down_mine, down_other,
    )


def attn_backward_kernel(
    side, rows, grad, tables, mask, norms, qkv, logs, attended, grad_mlp, mine, other,
    kept, sent, bias_grad, sums, passed, mixed_back
):
    width = mine.shape[1] // 4
    unit, scale = unit_rows(rows[...].astype(jnp.float32))
    normed = (unit * norms[0:1] + norms[2:3]).T.astype(jnp.bfloat16)
    allowed = mask[...] > 0.5
    mixed = attended[...].T
    back = None
    for at, (weight, result) in enumerate(((mine, kept), (other, sent))):
        half = side[0] if at == 0 else 1 - side[0]
        part = grad[:, lane_half(half, width)]
        result[:, 3 * width :] = product(mixed, part).astype(jnp.bfloat16)
        term = product_transposed(part, weight[:, 3 * width :])
        back = term if back is None else back + term
    mixed_back[...] = back.astype(jnp.bfloat16)
    grad_attn = None
    for at, (weight, result) in enumerate(((mine, kept), (other, sent))):
        half = side[0] if at == 0 else 1 - side[0]
        queries = qkv[at, :, 0:width]
        keys = qkv[at, :, width : 2 * width]
        values = qkv[at, :, 2 * width :]
        keys_turned = keys.T
        grad_out = mixed_back[:, lane_half(half, width)]
        query_grads, key_grads, value_grads = [], [], []
        for pair in range(width // LANES):
            cut = slice(pair * LANES, (pair + 1) * LANES)
            key_pair, value_pair = [], []
            for which in range(2):
                head = 2 * pair + which
                scores = scores_of(keys[:, cut], queries[:, cut], which, allowed)
                chances = jnp.exp(scores - logs[at, head : head + 1, :])
                value_pair.append(product(chances.astype(jnp.bfloat16), grad_out[:, cut]))
                slopes = product_transposed(head_lanes(values[:, cut], which), grad_out[:, cut])
                inner = jnp.sum(slopes * chances, axis=0, keepdims=True)
                slopes = (chances * (slopes - inner)).astype(jnp.bfloat16)
                key_pair.append(product(slopes, queries[:, cut]))
                query_grads.append(product(keys_turned[head * HD : (head + 1) * HD], slopes))
            lane = lax.broadcasted_iota(jnp.int32, key_pair[0].shape, 1)
            key_grads.append(jnp.where(lane < HD, key_pair[0], key_pair[1]))
            value_grads.append(jnp.where(lane < HD, value_pair[0], value_pair[1]))
        factor = 1.0 / math.sqrt(HD)
        query_grad = turned(jnp.concatenate(query_grads, axis=0).T * factor, tables, True)
        key_grad = turned(jnp.concatenate(key_grads, axis=1) * factor, tables, True)
        value_grad = jnp.concatenate(value_grads, axis=1)
        for index, part in enumerate((query_grad, key_grad, value_grad)):
            cut = slice(index * width, (index + 1) * width)
            part = part.astype(jnp.bfloat16)
            bias_grad[at : at + 1, cut] = jnp.sum(
                part.astype(jnp.float32), axis=0, keepdims=True
            )
            result[:, cut] = product(normed, part).astype(jnp.bfloat16)
            term = product_transposed(part, weight[:, cut])
            grad_attn = term if grad_attn is None else grad_attn + term
    grad_up = grad_mlp[...]
    grad_rows = grad[...].astype(jnp.float32)
    sums[0:1] = jnp.sum(unit * grad_attn, axis=0, keepdims=True)
    sums[1:2] = jnp.sum(unit * grad_up, axis=0, keepdims=True)
    sums[2:3] = jnp.sum(grad_attn, axis=0, keepdims=True)
    sums[3:4] = jnp.sum(grad_up, axis=0, keepdims=True)
    sums[4:5] = jnp.sum(grad_rows, axis=0, keepdims=True)
    inward = grad_attn * norms[0:1] + grad_up * norms[1:2]
    level = jnp.mean(inward, axis=-1, keepdims=True)
    along = jnp.mean(inward * unit, axis=-1, keepdims=True)
    passed[...] = (grad_rows + (inward - level - unit * along) * scale).astype(passed.dtype)


def attn_backward(side, rows, grad, tables, mask, small, saved, grad_mlp, mine, other, kind):
    qkv, logs, attended = saved
    length, features = rows.shape
    return pl.pallas_call(
        attn_backward_kernel,
        out_shape=(
            jax.ShapeDtypeStruct(mine.shape, jnp.bfloat16),
            jax.ShapeDtypeStruct(mine.shape, jnp.bfloat16),
            jax.ShapeDtypeStruct((2, 3 * features // 2), jnp.float32),
            jax.ShapeDtypeStruct((5, features), jnp.float32),
            jax.ShapeDtypeStruct((length, features), kind),
        ),
        in_specs=[pl.BlockSpec(memory_space=pltpu.SMEM)] + whole_blocks(11),
        out_specs=tuple(whole_blocks(5)),
        scratch_shapes=[pltpu.VMEM((length, features), jnp.bfloat16)],
        compiler_params=pltpu.CompilerParams(vmem_limit_bytes=vmem_bytes),
        cost_estimate=pl.CostEstimate(
            flops=2 * length * features * features * 12,
            bytes_accessed=16 * features * features,
            transcendentals=length * length * features // HD,
        ),
        name="attn_backward",
    )(
        side, rows, grad, tables, mask, small["norms"], qkv, logs, attended, grad_mlp, mine, other
    )


SQUARE = 4
RING = 4


def swap_cores(value):
    return lax.ppermute(value, "section", [(0, 1), (1, 0)])


def swap_square(value, bit):
    count = lax.axis_size("dp")
    return lax.ppermute(value, "dp", [(i, i ^ bit) for i in range(count)])


def ring_on(value):
    count = lax.axis_size("dp")
    return lax.ppermute(value, "dp", [(i, (i + SQUARE) % count) for i in range(count)])


def small_slice():
    return lax.axis_size("dp") == SQUARE * RING


def place_kernel(spot_ref, own, first, second, far_low, far_high, out, sems):
    spot = spot_ref[0]
    half = RING // 2
    copies = [
        pltpu.make_async_copy(own, out.at[:, spot], sems.at[0]),
        pltpu.make_async_copy(first, out.at[:, spot ^ 1], sems.at[1]),
        pltpu.make_async_copy(second, out.at[:, spot ^ 2], sems.at[2]),
        pltpu.make_async_copy(far_low, out.at[pl.ds(0, half), spot ^ 3], sems.at[3]),
        pltpu.make_async_copy(far_high, out.at[pl.ds(half, half), spot ^ 3], sems.at[4]),
    ]
    for copy in copies:
        copy.start()
    for copy in copies:
        copy.wait()


def place_blocks(spot, blocks):
    _, rows, columns = blocks[0].shape
    any_space = pl.BlockSpec(memory_space=pl.ANY)
    return pl.pallas_call(
        place_kernel,
        out_shape=jax.ShapeDtypeStruct((RING, SQUARE, rows, columns), blocks[0].dtype),
        in_specs=[pl.BlockSpec(memory_space=pltpu.SMEM)] + [any_space] * 5,
        out_specs=pl.BlockSpec(memory_space=pltpu.VMEM),
        scratch_shapes=[pltpu.SemaphoreType.DMA((5,))],
        compiler_params=pltpu.CompilerParams(vmem_limit_bytes=vmem_bytes),
        name="place_blocks",
    )(spot, *blocks)


def gather_rows(piece):
    rows, columns = piece.shape
    if not small_slice():
        return lax.all_gather(piece, "dp", axis=0, tiled=True)
    place = lax.axis_index("dp")
    level = place // SQUARE
    spot = (place % SQUARE).astype(jnp.int32).reshape(1)
    held = [piece]
    for _ in range(RING - 1):
        held.append(ring_on(held[-1]))
    doubled = jnp.stack([held[3], held[2], held[1], held[0], held[3], held[2], held[1]])
    column = lax.dynamic_slice_in_dim(doubled, RING - 1 - level, RING, 0)
    first = swap_square(column, 1)
    second = swap_square(column, 2)
    half = RING // 2
    far_low = swap_square(first[:half], 2)
    far_high = swap_square(second[half:], 1)
    whole = place_blocks(spot, (column, first, second, far_low, far_high))
    return whole.reshape(RING * SQUARE * rows, columns)


def scatter_rows(summed):
    rows = summed.shape[0] // lax.axis_size("dp")
    columns = summed.shape[1]
    if not small_slice():
        return lax.psum_scatter(summed, "dp", scatter_dimension=0, tiled=True)
    place = lax.axis_index("dp")
    level = place // SQUARE
    spot = place % SQUARE
    blocks = summed.reshape(RING, SQUARE, rows, columns)

    def block(index):
        return lax.dynamic_index_in_dim(blocks, index, 1, keepdims=False)

    half = RING // 2
    wire = jnp.bfloat16
    far = block(spot ^ 3).astype(wire)
    far_low = swap_square(far[:half], 1)
    far_high = swap_square(far[half:], 2)
    first = block(spot ^ 1)
    second = block(spot ^ 2)
    first = jnp.concatenate([first[:half], first[half:] + far_high.astype(jnp.float32)])
    second = jnp.concatenate([second[:half] + far_low.astype(jnp.float32), second[half:]])
    from_first = swap_square(first.astype(wire), 1)
    from_second = swap_square(second.astype(wire), 2)
    column = block(spot) + from_first.astype(jnp.float32) + from_second.astype(jnp.float32)

    def rung(back):
        return lax.dynamic_index_in_dim(column, (level - back) % RING, 0, keepdims=False)

    travelling = rung(1)
    for step in range(1, RING):
        travelling = ring_on(travelling.astype(wire)).astype(jnp.float32) + rung(step + 1)
    return travelling


def half_of(array, which):
    width = array.shape[1] // 2
    return lax.dynamic_slice_in_dim(array, which * width, width, 1)


def half_slots(array, which):
    length = array.shape[0] // 2
    return lax.dynamic_slice_in_dim(array, which * length, length, 0)


def ordered(is_first, mine, other):
    return (jnp.where(is_first, mine, other), jnp.where(is_first, other, mine))


def on_device(
    ends_in,
    lengths,
    qkv_weight,
    qkv_bias,
    out_weight,
    up_weight,
    up_bias,
    down_weight,
    out_biases,
    norm_gains,
    norm_biases,
):
    section_index = lax.axis_index("section")
    is_first = section_index == 0
    side = section_index.astype(jnp.int32).reshape(1)
    features = ends_in.shape[2]
    width = features // 2
    count = lax.axis_size("dp")
    own_rows = ends_in[0]
    slot_count = own_rows.shape[0] // 2
    kept_rows = half_slots(own_rows, section_index)
    other_rows = swap_cores(half_slots(own_rows, 1 - section_index))
    entry, cotangent = ordered(is_first, kept_rows, other_rows)
    segment, position = layouts(
        lax.dynamic_index_in_dim(lengths, section_index, 0, keepdims=False), slot_count
    )
    tables = rotary_tables(position)
    mask = allowed_transposed(segment)

    def both(take):
        kept = take(section_index)
        other = swap_cores(take(1 - section_index))
        return ordered(is_first, kept, other)

    def take_narrow(which):
        thirds = [
            qkv_weight[0, :, part * features : (part + 1) * features] for part in range(3)
        ]
        return jnp.concatenate([half_of(part, which) for part in thirds + [out_weight[0]]], axis=1)

    pieces = (
        both(take_narrow),
        both(lambda which: half_of(up_weight[0], which)),
        both(lambda which: half_of(down_weight[0], which)),
    )

    small_shapes = [
        (qkv_bias.shape[1],),
        (up_bias.shape[1],),
        out_biases.shape[1:],
        norm_gains.shape[1:],
        norm_biases.shape[1:],
    ]
    small_own = jnp.concatenate(
        [a[0].reshape(-1) for a in (qkv_bias, up_bias, out_biases, norm_gains, norm_biases)]
    )
    small_both = jnp.concatenate(ordered(is_first, small_own, swap_cores(small_own)))
    small_full = gather_rows(small_both[None])
    small_full = small_full.reshape(count, 2, small_own.shape[0]).astype(jnp.float32)

    def small_of(layer):
        rows = small_full[:, layer]
        found = []
        at = 0
        for shape in small_shapes:
            size = math.prod(shape)
            part = rows[:, at : at + size].reshape((count,) + shape)
            at += size
            if len(shape) == 2:
                part = part.transpose(1, 0, 2).reshape(shape[0], count * shape[1])
            else:
                part = part.reshape(1, count * shape[0])
            found.append(part)
        bias_qkv, bias_up, bias_out, gains, shifts = found
        bias_qkv = bias_qkv.reshape(3, 2, width).transpose(1, 0, 2).reshape(2, 3 * width)
        return dict(
            qkv=jnp.where(is_first, bias_qkv, bias_qkv[::-1]),
            up=bias_up,
            out=bias_out,
            norms=jnp.concatenate([gains, shifts]),
        )

    gathered = []
    for layer in range(2):
        found = []
        for piece in pieces:
            mine = gather_rows(piece[layer])
            found.append((mine, swap_cores(mine)))
        gathered.append(found)
    small = [small_of(layer) for layer in range(2)]

    def forward(rows, layer, kind):
        narrow, up, down = gathered[layer]
        qkv, logs, attended, passed = attn_forward(side, rows, tables, mask, small[layer], *narrow)
        active, slope, produced = mlp_forward(
            side, rows, passed, small[layer], up + down, kind
        )
        return (produced, (qkv, logs, attended), (active, slope))

    def backward(rows, grad, layer, attn_saved, mlp_saved, kind):
        narrow, up, down = gathered[layer]
        up_kept, up_sent, down_kept, down_sent, bias_up, grad_mlp = mlp_backward(
            side, rows, grad, small[layer], mlp_saved, up + down
        )
        kept, sent, bias_qkv, sums, passed = attn_backward(
            side, rows, grad, tables, mask, small[layer], attn_saved, grad_mlp, *narrow, kind
        )
        bias_qkv = jnp.where(is_first, bias_qkv, bias_qkv[::-1])
        bias_qkv = bias_qkv.reshape(2, 3, width).transpose(1, 0, 2).reshape(1, 6 * width)
        vectors = (
            bias_qkv,
            bias_up,
            jnp.concatenate([sums[4:5], sums[4:5]]),
            sums[0:2],
            sums[2:4],
        )
        return (passed, ((down_kept, down_sent), (up_kept, up_sent), (kept, sent)), vectors)

    middle, attn_lower, mlp_lower = forward(entry, 0, jnp.bfloat16)
    produced, attn_upper, mlp_upper = forward(middle, 1, jnp.float32)
    grad_middle, grads_upper, vectors_upper = backward(
        middle, cotangent, 1, attn_upper, mlp_upper, jnp.bfloat16
    )
    grad_entry, grads_lower, vectors_lower = backward(
        entry, grad_middle, 0, attn_lower, mlp_lower, jnp.float32
    )

    def reduce_half(kept, sent):
        return scatter_rows(kept.astype(jnp.float32) + swap_cores(sent).astype(jnp.float32))

    reduced_upper = [reduce_half(*pair) for pair in grads_upper]
    reduced_lower = [reduce_half(*pair) for pair in grads_lower]

    def finish(lower, upper):
        mine, leaving = ordered(is_first, lower, upper)
        return ordered(is_first, mine, swap_cores(leaving))

    down_halves, up_halves, narrow_halves = (
        finish(*pair) for pair in zip(reduced_lower, reduced_upper)
    )
    total_down = jnp.concatenate(down_halves, axis=1)
    total_up = jnp.concatenate(up_halves, axis=1)
    total_qkv = jnp.concatenate(
        [
            part[:, at * width : (at + 1) * width]
            for at in range(3)
            for part in narrow_halves
        ],
        axis=1,
    )
    total_out = jnp.concatenate([part[:, 3 * width :] for part in narrow_halves], axis=1)

    def small_rows(vectors):
        parts = []
        for grad in vectors:
            part = grad.reshape(grad.shape[0], count, -1).transpose(1, 0, 2)
            parts.append(part.reshape(count, -1))
        return jnp.concatenate(parts, axis=1)

    small_kept, small_sent = ordered(
        is_first, small_rows(vectors_lower), small_rows(vectors_upper)
    )
    small_total = scatter_rows(small_kept + swap_cores(small_sent))[0]
    small_outs = []
    at = 0
    for shape in small_shapes:
        size = math.prod(shape)
        small_outs.append(small_total[at : at + size].reshape((1,) + shape))
        at += size

    staying, leaving = ordered(is_first, grad_entry, produced)
    ends_out = jnp.concatenate(ordered(is_first, staying, swap_cores(leaving)))
    return (
        ends_out[None],
        total_qkv[None],
        small_outs[0],
        total_out[None],
        total_up[None],
        small_outs[1],
        total_down[None],
        small_outs[2],
        small_outs[3],
        small_outs[4],
    )


def solution(mesh):
    return jax.shard_map(
        on_device,
        mesh=mesh,
        in_specs=(
            P("section", "dp", None),
            P("dp", None),
            P("section", "dp", None),
            P("section", "dp"),
            P("section", "dp", None),
            P("section", "dp", None),
            P("section", "dp"),
            P("section", "dp", None),
            P("section", None, "dp"),
            P("section", None, "dp"),
            P("section", None, "dp"),
        ),
        out_specs=(
            P("section", "dp", None),
            P("section", "dp", None),
            P("section", "dp"),
            P("section", "dp", None),
            P("section", "dp", None),
            P("section", "dp"),
            P("section", "dp", None),
            P("section", None, "dp"),
            P("section", None, "dp"),
            P("section", None, "dp"),
        ),
        check_vma=False,
    )
```

```python
import math

import jax
import jax.numpy as jnp
from jax import lax
from jax.experimental import pallas as pl
from jax.experimental.pallas import tpu as pltpu
from jax.sharding import PartitionSpec as P

HD = 64
ROT = 16
LANES = 128
TILES = 3


eps = 1e-05
masked_score = -1e30
vmem_bytes = 48 * 1024 * 1024


def product(left, right):
    return jnp.dot(left, right, preferred_element_type=jnp.float32)


def product_transposed(left, right):
    return lax.dot_general(
        left, right, (((1,), (1,)), ((), ())), preferred_element_type=jnp.float32
    )


def layouts(lengths, slot_count):
    ends_at = jnp.cumsum(lengths)
    indices = jnp.arange(slot_count, dtype=jnp.int32)
    passed = indices[:, None] >= ends_at[None, :]
    segments = jnp.sum(passed.astype(jnp.int32), axis=1)
    starts = jnp.sum(jnp.where(passed, lengths[None, :], 0), axis=1)
    return (segments, indices - starts)


def rotary_tables(positions):
    lane = jnp.arange(LANES, dtype=jnp.int32) % HD
    half = ROT // 2
    freqs = 10000.0 ** (-2.0 * (lane % half).astype(jnp.float32) / ROT)
    angles = positions.astype(jnp.float32)[:, None] * freqs[None, :]
    cosine = jnp.where(lane < ROT, jnp.cos(angles), 1.0)
    sine = jnp.sin(angles)
    ahead = jnp.where(lane < half, -sine, 0.0)
    behind = jnp.where((lane >= half) & (lane < ROT), sine, 0.0)
    return jnp.stack([cosine, ahead, behind])


def allowed_transposed(segment):
    indices = jnp.arange(segment.shape[0], dtype=jnp.int32)
    allowed = (segment[:, None] == segment[None, :]) & (indices[:, None] <= indices[None, :])
    return allowed.astype(jnp.float32)


def turned(values, tables, back):
    half = ROT // 2
    parts = []
    for at in range(0, values.shape[1], LANES):
        part = values[:, at : at + LANES]
        moved = (
            pltpu.roll(part, LANES - half, 1) * tables[1] + pltpu.roll(part, half, 1) * tables[2]
        )
        kept = part * tables[0]
        parts.append(kept - moved if back else kept + moved)
    return jnp.concatenate(parts, axis=1)


def unit_rows(rows):
    centred = rows - jnp.mean(rows, axis=-1, keepdims=True)
    spread = jnp.mean(centred * centred, axis=-1, keepdims=True)
    scale = lax.rsqrt(spread + eps)
    return (centred * scale, scale)


def lane_half(which, width):
    return pl.ds(pl.multiple_of(which * width, LANES), width)


def head_lanes(values, which):
    lane = lax.broadcasted_iota(jnp.int32, values.shape, 1)
    return jnp.where((lane < HD) == (which == 0), values, jnp.zeros_like(values))


def scores_of(key_pair, query_pair, which, allowed):
    scores = product_transposed(head_lanes(key_pair, which), query_pair) * (1.0 / math.sqrt(HD))
    return jnp.where(allowed, scores, masked_score)


def attn_forward_kernel(
    side, rows, tables, mask, norms, bias_qkv, bias_out, mine, other, qkv, logs, attended, passed
):
    width = mine.shape[1] // 4
    entry = rows[...].astype(jnp.float32)
    unit, _ = unit_rows(entry)
    normed = (unit * norms[0:1] + norms[2:3]).astype(jnp.bfloat16)
    allowed = mask[...] > 0.5
    for at, weight in enumerate((mine, other)):
        half = side[0] if at == 0 else 1 - side[0]
        parts = []
        for part in range(3):
            cut = slice(part * width, (part + 1) * width)
            value = product(normed, weight[:, cut]) + bias_qkv[at : at + 1, cut]
            if part < 2:
                value = turned(value, tables, False)
            value = value.astype(jnp.bfloat16)
            qkv[at, :, cut] = value
            parts.append(value)
        queries, keys, values = parts
        values = values.T
        outs = []
        for pair in range(width // LANES):
            cut = slice(pair * LANES, (pair + 1) * LANES)
            for which in range(2):
                head = 2 * pair + which
                scores = scores_of(keys[:, cut], queries[:, cut], which, allowed)
                peak = jnp.max(scores, axis=0, keepdims=True)
                raised = jnp.exp(scores - peak)
                total = jnp.sum(raised, axis=0, keepdims=True)
                chances = (raised * (1.0 / total)).astype(jnp.bfloat16)
                outs.append(product(values[head * HD : (head + 1) * HD], chances))
                logs[at, head : head + 1, :] = peak + jnp.log(total)
        mixed = jnp.concatenate(outs, axis=0).T.astype(jnp.bfloat16)
        attended[:, lane_half(half, width)] = mixed
    mixed = attended[...]
    for at, weight in enumerate((mine, other)):
        half = side[0] if at == 0 else 1 - side[0]
        lanes = lane_half(half, width)
        passed[:, lanes] = (
            rows[:, lanes].astype(jnp.float32)
            + product(mixed, weight[:, 3 * width :])
            + bias_out[0:1, lanes]
        )


def whole_blocks(count):
    return [pl.BlockSpec(memory_space=pltpu.VMEM)] * count


def attn_forward(side, rows, tables, mask, small, mine, other):
    length, features = rows.shape
    width = features // 2
    heads = width // HD
    return pl.pallas_call(
        attn_forward_kernel,
        out_shape=(
            jax.ShapeDtypeStruct((2, length, 3 * width), jnp.bfloat16),
            jax.ShapeDtypeStruct((2, heads, length), jnp.float32),
            jax.ShapeDtypeStruct((length, features), jnp.bfloat16),
            jax.ShapeDtypeStruct((length, features), jnp.float32),
        ),
        in_specs=[pl.BlockSpec(memory_space=pltpu.SMEM)] + whole_blocks(8),
        out_specs=tuple(whole_blocks(4)),
        compiler_params=pltpu.CompilerParams(vmem_limit_bytes=vmem_bytes),
        cost_estimate=pl.CostEstimate(
            flops=2 * length * features * features * 5,
            bytes_accessed=8 * features * features,
            transcendentals=length * length * features // HD,
        ),
        name="attn_forward",
    )(side, rows, tables, mask, small["norms"], small["qkv"], small["out"], mine, other)


def tile_of(step, side):
    half = jnp.where(step < TILES, side[0], 1 - side[0])
    return half * TILES + step % TILES


def first_tile(step):
    return jnp.minimum(step, TILES - 1)


def second_tile(step):
    return jnp.maximum(step - TILES, 0)


def mlp_forward_kernel(
    side, rows, passed, norms, bias_up, bias_out, up_mine, up_other, down_mine, down_other,
    active, slope, produced, normed, sum_mine, sum_other
):
    step = pl.program_id(0)

    @pl.when(step == 0)
    def _():
        unit, _ = unit_rows(rows[...].astype(jnp.float32))
        normed[...] = (unit * norms[1:2] + norms[3:4]).astype(jnp.bfloat16)
        sum_mine[...] = jnp.zeros_like(sum_mine)
        sum_other[...] = jnp.zeros_like(sum_other)

    weight = jnp.where(step < TILES, up_mine[...], up_other[...])
    hidden = product(normed[...], weight) + bias_up[...]
    bell = 0.5 * (1.0 + lax.erf(hidden * (1.0 / math.sqrt(2.0))))
    density = jnp.exp(-0.5 * hidden * hidden) * (1.0 / math.sqrt(2.0 * math.pi))
    slope[...] = bell + hidden * density
    lit = (hidden * bell).astype(jnp.bfloat16)
    active[...] = lit
    sum_mine[...] += product(lit, down_mine[...])
    sum_other[...] += product(lit, down_other[...])

    @pl.when(step == 2 * TILES - 1)
    def _():
        width = sum_mine.shape[1]
        for half, total in ((side[0], sum_mine), (1 - side[0], sum_other)):
            lanes = lane_half(half, width)
            produced[:, lanes] = (
                passed[:, lanes] + total[...] + bias_out[1:2, lanes]
            ).astype(produced.dtype)


def mlp_forward(side, rows, passed, small, weights, kind):
    up_mine, up_other, down_mine, down_other = weights
    length, features = rows.shape
    hidden = down_mine.shape[0]
    tile = hidden // (2 * TILES)
    width = features // 2

    def fixed(*shape):
        return pl.BlockSpec(shape, lambda step, side: (0,) * len(shape))

    tiled = pl.BlockSpec((length, tile), lambda step, side: (0, tile_of(step, side)))
    down_spec = pl.BlockSpec((tile, width), lambda step, side: (tile_of(step, side), 0))
    return pl.pallas_call(
        mlp_forward_kernel,
        out_shape=(
            jax.ShapeDtypeStruct((length, hidden), jnp.bfloat16),
            jax.ShapeDtypeStruct((length, hidden), jnp.float32),
            jax.ShapeDtypeStruct((length, features), kind),
        ),
        grid_spec=pltpu.PrefetchScalarGridSpec(
            num_scalar_prefetch=1,
            grid=(2 * TILES,),
            in_specs=[
                fixed(length, features),
                fixed(length, features),
                fixed(4, features),
                pl.BlockSpec((1, tile), lambda step, side: (0, tile_of(step, side))),
                fixed(2, features),
                pl.BlockSpec((features, tile), lambda step, side: (0, first_tile(step))),
                pl.BlockSpec((features, tile), lambda step, side: (0, second_tile(step))),
                down_spec,
                down_spec,
            ],
            out_specs=(tiled, tiled, fixed(length, features)),
            scratch_shapes=[
                pltpu.VMEM((length, features), jnp.bfloat16),
                pltpu.VMEM((length, width), jnp.float32),
                pltpu.VMEM((length, width), jnp.float32),
            ],
        ),
        compiler_params=pltpu.CompilerParams(vmem_limit_bytes=vmem_bytes),
        cost_estimate=pl.CostEstimate(
            flops=4 * length * features * hidden,
            bytes_accessed=4 * features * hidden + 6 * length * hidden,
            transcendentals=2 * length * hidden,
        ),
        name="mlp_forward",
    )(
        side, rows, passed, small["norms"], small["up"], small["out"],
        up_mine, up_other, down_mine, down_other,
    )


def mlp_backward_kernel(
    side, rows, grad, norms, active, slope, up_mine, up_other, down_mine, down_other,
    up_kept, up_sent, down_kept, down_sent, bias_grad, grad_normed, normed
):
    step = pl.program_id(0)
    width = down_mine.shape[1]

    @pl.when(step == 0)
    def _():
        unit, _ = unit_rows(rows[...].astype(jnp.float32))
        normed[...] = (unit * norms[1:2] + norms[3:4]).T.astype(jnp.bfloat16)
        grad_normed[...] = jnp.zeros_like(grad_normed)

    grad_mine = grad[:, lane_half(side[0], width)]
    grad_other = grad[:, lane_half(1 - side[0], width)]
    weight = jnp.where(step < TILES, up_mine[...], up_other[...])
    lit = active[...].T
    down_kept[...] = product(lit, grad_mine).astype(jnp.bfloat16)
    down_sent[...] = product(lit, grad_other).astype(jnp.bfloat16)
    back = product_transposed(grad_mine, down_mine[...])
    back += product_transposed(grad_other, down_other[...])
    back = (back * slope[...]).astype(jnp.bfloat16)
    bias_grad[...] = jnp.sum(back.astype(jnp.float32), axis=0, keepdims=True)
    up_grad = product(normed[...], back).astype(jnp.bfloat16)

    @pl.when(step < TILES)
    def _():
        up_kept[...] = up_grad

    @pl.when(step >= TILES)
    def _():
        up_sent[...] = up_grad

    grad_normed[...] += product_transposed(back, weight)


def mlp_backward(side, rows, grad, small, saved, weights):
    active, slope = saved
    up_mine, up_other, down_mine, down_other = weights
    length, features = rows.shape
    hidden = down_mine.shape[0]
    tile = hidden // (2 * TILES)
    width = features // 2

    def fixed(*shape):
        return pl.BlockSpec(shape, lambda step, side: (0,) * len(shape))

    tiled = pl.BlockSpec((length, tile), lambda step, side: (0, tile_of(step, side)))
    down_spec = pl.BlockSpec((tile, width), lambda step, side: (tile_of(step, side), 0))
    up_first = pl.BlockSpec((features, tile), lambda step, side: (0, first_tile(step)))
    up_second = pl.BlockSpec((features, tile), lambda step, side: (0, second_tile(step)))
    return pl.pallas_call(
        mlp_backward_kernel,
        out_shape=(
            jax.ShapeDtypeStruct((features, hidden // 2), jnp.bfloat16),
            jax.ShapeDtypeStruct((features, hidden // 2), jnp.bfloat16),
            jax.ShapeDtypeStruct((hidden, width), jnp.bfloat16),
            jax.ShapeDtypeStruct((hidden, width), jnp.bfloat16),
            jax.ShapeDtypeStruct((1, hidden), jnp.float32),
            jax.ShapeDtypeStruct((length, features), jnp.float32),
        ),
        grid_spec=pltpu.PrefetchScalarGridSpec(
            num_scalar_prefetch=1,
            grid=(2 * TILES,),
            in_specs=[
                fixed(length, features),
                fixed(length, features),
                fixed(4, features),
                tiled,
                tiled,
                up_first,
                up_second,
                down_spec,
                down_spec,
            ],
            out_specs=(
                up_first,
                up_second,
                down_spec,
                down_spec,
                pl.BlockSpec((1, tile), lambda step, side: (0, tile_of(step, side))),
                fixed(length, features),
            ),
            scratch_shapes=[pltpu.VMEM((features, length), jnp.bfloat16)],
        ),
        compiler_params=pltpu.CompilerParams(vmem_limit_bytes=vmem_bytes),
        cost_estimate=pl.CostEstimate(
            flops=8 * length * features * hidden,
            bytes_accessed=8 * features * hidden + 6 * length * hidden,
            transcendentals=0,
        ),
        name="mlp_backward",
    )(
        side, rows, grad, small["norms"], active, slope,
        up_mine, up_other, down_mine, down_other,
    )


def attn_backward_kernel(
    side, rows, grad, tables, mask, norms, qkv, logs, attended, grad_mlp, mine, other,
    kept, sent, bias_grad, sums, passed, mixed_back
):
    width = mine.shape[1] // 4
    unit, scale = unit_rows(rows[...].astype(jnp.float32))
    normed = (unit * norms[0:1] + norms[2:3]).T.astype(jnp.bfloat16)
    allowed = mask[...] > 0.5
    mixed = attended[...].T
    back = None
    for at, (weight, result) in enumerate(((mine, kept), (other, sent))):
        half = side[0] if at == 0 else 1 - side[0]
        part = grad[:, lane_half(half, width)]
        result[:, 3 * width :] = product(mixed, part).astype(jnp.bfloat16)
        term = product_transposed(part, weight[:, 3 * width :])
        back = term if back is None else back + term
    mixed_back[...] = back.astype(jnp.bfloat16)
    grad_attn = None
    for at, (weight, result) in enumerate(((mine, kept), (other, sent))):
        half = side[0] if at == 0 else 1 - side[0]
        queries = qkv[at, :, 0:width]
        keys = qkv[at, :, width : 2 * width]
        values = qkv[at, :, 2 * width :]
        keys_turned = keys.T
        grad_out = mixed_back[:, lane_half(half, width)]
        query_grads, key_grads, value_grads = [], [], []
        for pair in range(width // LANES):
            cut = slice(pair * LANES, (pair + 1) * LANES)
            key_pair, value_pair = [], []
            for which in range(2):
                head = 2 * pair + which
                scores = scores_of(keys[:, cut], queries[:, cut], which, allowed)
                chances = jnp.exp(scores - logs[at, head : head + 1, :])
                value_pair.append(product(chances.astype(jnp.bfloat16), grad_out[:, cut]))
                slopes = product_transposed(head_lanes(values[:, cut], which), grad_out[:, cut])
                inner = jnp.sum(slopes * chances, axis=0, keepdims=True)
                slopes = (chances * (slopes - inner)).astype(jnp.bfloat16)
                key_pair.append(product(slopes, queries[:, cut]))
                query_grads.append(product(keys_turned[head * HD : (head + 1) * HD], slopes))
            lane = lax.broadcasted_iota(jnp.int32, key_pair[0].shape, 1)
            key_grads.append(jnp.where(lane < HD, key_pair[0], key_pair[1]))
            value_grads.append(jnp.where(lane < HD, value_pair[0], value_pair[1]))
        factor = 1.0 / math.sqrt(HD)
        query_grad = turned(jnp.concatenate(query_grads, axis=0).T * factor, tables, True)
        key_grad = turned(jnp.concatenate(key_grads, axis=1) * factor, tables, True)
        value_grad = jnp.concatenate(value_grads, axis=1)
        for index, part in enumerate((query_grad, key_grad, value_grad)):
            cut = slice(index * width, (index + 1) * width)
            part = part.astype(jnp.bfloat16)
            bias_grad[at : at + 1, cut] = jnp.sum(
                part.astype(jnp.float32), axis=0, keepdims=True
            )
            result[:, cut] = product(normed, part).astype(jnp.bfloat16)
            term = product_transposed(part, weight[:, cut])
            grad_attn = term if grad_attn is None else grad_attn + term
    grad_up = grad_mlp[...]
    grad_rows = grad[...].astype(jnp.float32)
    sums[0:1] = jnp.sum(unit * grad_attn, axis=0, keepdims=True)
    sums[1:2] = jnp.sum(unit * grad_up, axis=0, keepdims=True)
    sums[2:3] = jnp.sum(grad_attn, axis=0, keepdims=True)
    sums[3:4] = jnp.sum(grad_up, axis=0, keepdims=True)
    sums[4:5] = jnp.sum(grad_rows, axis=0, keepdims=True)
    inward = grad_attn * norms[0:1] + grad_up * norms[1:2]
    level = jnp.mean(inward, axis=-1, keepdims=True)
    along = jnp.mean(inward * unit, axis=-1, keepdims=True)
    passed[...] = (grad_rows + (inward - level - unit * along) * scale).astype(passed.dtype)


def attn_backward(side, rows, grad, tables, mask, small, saved, grad_mlp, mine, other, kind):
    qkv, logs, attended = saved
    length, features = rows.shape
    return pl.pallas_call(
        attn_backward_kernel,
        out_shape=(
            jax.ShapeDtypeStruct(mine.shape, jnp.bfloat16),
            jax.ShapeDtypeStruct(mine.shape, jnp.bfloat16),
            jax.ShapeDtypeStruct((2, 3 * features // 2), jnp.float32),
            jax.ShapeDtypeStruct((5, features), jnp.float32),
            jax.ShapeDtypeStruct((length, features), kind),
        ),
        in_specs=[pl.BlockSpec(memory_space=pltpu.SMEM)] + whole_blocks(11),
        out_specs=tuple(whole_blocks(5)),
        scratch_shapes=[pltpu.VMEM((length, features), jnp.bfloat16)],
        compiler_params=pltpu.CompilerParams(vmem_limit_bytes=vmem_bytes),
        cost_estimate=pl.CostEstimate(
            flops=2 * length * features * features * 12,
            bytes_accessed=16 * features * features,
            transcendentals=length * length * features // HD,
        ),
        name="attn_backward",
    )(
        side, rows, grad, tables, mask, small["norms"], qkv, logs, attended, grad_mlp, mine, other
    )


SQUARE = 4
RING = 4
LAG = 2


def swap_cores(value):
    return lax.ppermute(value, "section", [(0, 1), (1, 0)])


def swap_square(value, bit):
    count = lax.axis_size("dp")
    return lax.ppermute(value, "dp", [(i, i ^ bit) for i in range(count)])


def shift_ring(value, steps):
    count = lax.axis_size("dp")
    pairs = [(i, (i + SQUARE * steps) % count) for i in range(count)]
    return lax.ppermute(value, "dp", pairs)


def small_slice():
    return lax.axis_size("dp") == SQUARE * RING


def place_kernel(spot_ref, own, first, second, far_low, far_high, out, sems):
    spot = spot_ref[0]
    half = RING // 2
    copies = [
        pltpu.make_async_copy(own, out.at[:, spot], sems.at[0]),
        pltpu.make_async_copy(first, out.at[:, spot ^ 1], sems.at[1]),
        pltpu.make_async_copy(second, out.at[:, spot ^ 2], sems.at[2]),
        pltpu.make_async_copy(far_low, out.at[pl.ds(0, half), spot ^ 3], sems.at[3]),
        pltpu.make_async_copy(far_high, out.at[pl.ds(half, half), spot ^ 3], sems.at[4]),
    ]
    for copy in copies:
        copy.start()
    for copy in copies:
        copy.wait()


def place_blocks(spot, blocks):
    _, rows, columns = blocks[0].shape
    any_space = pl.BlockSpec(memory_space=pl.ANY)
    return pl.pallas_call(
        place_kernel,
        out_shape=jax.ShapeDtypeStruct((RING, SQUARE, rows, columns), blocks[0].dtype),
        in_specs=[pl.BlockSpec(memory_space=pltpu.SMEM)] + [any_space] * 5,
        out_specs=pl.BlockSpec(memory_space=pltpu.VMEM),
        scratch_shapes=[pltpu.SemaphoreType.DMA((5,))],
        compiler_params=pltpu.CompilerParams(vmem_limit_bytes=vmem_bytes),
        name="place_blocks",
    )(spot, *blocks)


def after(values, earlier):
    flat, shape = jax.tree.flatten(values)
    waited = jax.tree.leaves(earlier)
    if not waited:
        return values
    tied = lax.optimization_barrier(tuple(flat) + tuple(waited))
    return jax.tree.unflatten(shape, tied[: len(flat)])


def gather_whole(piece):
    return lax.all_gather(piece, "dp", axis=0, tiled=True)


def column_moved(piece):
    return [piece] + [shift_ring(piece, steps) for steps in range(1, RING)]


def column_kernel(level_ref, *refs):
    held, out, sems = refs[:RING], refs[RING], refs[RING + 1]
    level = level_ref[0]
    copies = [
        pltpu.make_async_copy(part, out.at[lax.rem(level + RING - steps, RING)], sems.at[steps])
        for steps, part in enumerate(held)
    ]
    for copy in copies:
        copy.start()
    for copy in copies:
        copy.wait()


def column_placed(held):
    level = (lax.axis_index("dp") // SQUARE).astype(jnp.int32).reshape(1)
    return pl.pallas_call(
        column_kernel,
        out_shape=jax.ShapeDtypeStruct((RING,) + held[0].shape, held[0].dtype),
        in_specs=[pl.BlockSpec(memory_space=pltpu.SMEM)]
        + [pl.BlockSpec(memory_space=pl.ANY)] * RING,
        out_specs=pl.BlockSpec(memory_space=pltpu.VMEM),
        scratch_shapes=[pltpu.SemaphoreType.DMA((RING,))],
        name="place_column",
    )(level, *held)


def gather_stages(piece, tied):
    held = column_moved(tied(piece))
    yield held[1:]
    column = tied(column_placed(held))
    first = swap_square(column, 1)
    second = swap_square(column, 2)
    yield (first, second)
    half = RING // 2
    low, high = tied((first[:half], second[half:]))
    far_low = swap_square(low, 2)
    far_high = swap_square(high, 1)
    yield (far_low, far_high)
    spot = (lax.axis_index("dp") % SQUARE).astype(jnp.int32).reshape(1)
    whole = place_blocks(spot, (column, first, second, far_low, far_high))
    whole = tied(whole.reshape(RING * SQUARE * piece.shape[0], piece.shape[1]))
    other = swap_cores(whole)
    yield other
    return (whole, other)


def gather_small(piece):
    if not small_slice():
        return gather_whole(piece)
    spot = lax.axis_index("dp") % SQUARE
    level = lax.axis_index("dp") // SQUARE
    order = (level - jnp.arange(RING)) % RING
    column = jnp.take(jnp.stack(column_moved(piece)), order, axis=0)
    blocks = [column] + [swap_square(column, bit) for bit in range(1, SQUARE)]
    stacked = jnp.stack(blocks, axis=1)
    order = jnp.arange(SQUARE) ^ spot
    return jnp.take(stacked, order, axis=1).reshape(RING * SQUARE * piece.shape[0], -1)


def scatter_stages(kept, sent, tied):
    wire = jnp.bfloat16
    rows = kept.shape[0] // (RING * SQUARE)
    columns = kept.shape[1]
    place = lax.axis_index("dp")
    level = place // SQUARE
    spot = place % SQUARE
    received = swap_cores(tied(sent))
    yield received
    kept = kept.reshape(RING, SQUARE, rows, columns)
    received = received.reshape(RING, SQUARE, rows, columns)

    def block(index):
        mine = lax.dynamic_index_in_dim(kept, index, 1, keepdims=False)
        theirs = lax.dynamic_index_in_dim(received, index, 1, keepdims=False)
        return mine.astype(jnp.float32) + theirs.astype(jnp.float32)

    half = RING // 2
    far = block(spot ^ 3).astype(wire)
    low, high = tied((far[:half], far[half:]))
    far_low = swap_square(low, 1)
    far_high = swap_square(high, 2)
    yield (far_low, far_high)
    first = block(spot ^ 1)
    second = block(spot ^ 2)
    first = jnp.concatenate([first[:half], first[half:] + far_high.astype(jnp.float32)])
    second = jnp.concatenate([second[:half] + far_low.astype(jnp.float32), second[half:]])
    first, second = tied((first.astype(wire), second.astype(wire)))
    from_first = swap_square(first, 1)
    from_second = swap_square(second, 2)
    yield (from_first, from_second)
    column = block(spot) + from_first.astype(jnp.float32) + from_second.astype(jnp.float32)
    column = [lax.dynamic_index_in_dim(column, (level + steps) % RING, 0, keepdims=False) for steps in range(RING)]
    moving = tied(tuple(part.astype(wire) for part in column[1:]))
    moved = [shift_ring(part, steps + 1) for steps, part in enumerate(moving)]
    yield tuple(moved)
    total = column[0]
    for part in moved:
        total = total + part.astype(jnp.float32)
    return total


def scatter_small(kept, sent):
    summed = kept + swap_cores(sent)
    if not small_slice():
        return lax.psum_scatter(summed, "dp", scatter_dimension=0, tiled=True)
    place = lax.axis_index("dp")
    level = place // SQUARE
    spot = place % SQUARE
    blocks = summed.reshape(RING, SQUARE, -1)

    def block(index):
        return lax.dynamic_index_in_dim(blocks, index, 1, keepdims=False)

    column = block(spot)
    for bit in range(1, SQUARE):
        column = column + swap_square(block(spot ^ bit), bit)
    total = lax.dynamic_index_in_dim(column, level, 0, keepdims=True)
    for steps in range(1, RING):
        part = lax.dynamic_index_in_dim(column, (level + steps) % RING, 0, keepdims=True)
        total = total + shift_ring(part, steps)
    return total


class Rounds:
    def __init__(self, lag):
        self.lag = lag
        self.made = []
        self.current = []

    def tied(self, values):
        at = len(self.made) - self.lag
        return after(values, self.made[at]) if at >= 0 else values

    def note(self, values):
        self.current.append(values)

    def close(self):
        self.made.append(self.current)
        self.current = []


def advance(stages, rounds, results, name):
    try:
        rounds.note(next(stages))
    except StopIteration as ended:
        results[name] = ended.value


def half_of(array, which):
    width = array.shape[1] // 2
    return lax.dynamic_slice_in_dim(array, which * width, width, 1)


def half_slots(array, which):
    length = array.shape[0] // 2
    return lax.dynamic_slice_in_dim(array, which * length, length, 0)


def ordered(is_first, mine, other):
    return (jnp.where(is_first, mine, other), jnp.where(is_first, other, mine))


def on_device(
    ends_in,
    lengths,
    qkv_weight,
    qkv_bias,
    out_weight,
    up_weight,
    up_bias,
    down_weight,
    out_biases,
    norm_gains,
    norm_biases,
):
    section_index = lax.axis_index("section")
    is_first = section_index == 0
    side = section_index.astype(jnp.int32).reshape(1)
    features = ends_in.shape[2]
    width = features // 2
    count = lax.axis_size("dp")
    own_rows = ends_in[0]
    slot_count = own_rows.shape[0] // 2
    kept_rows = half_slots(own_rows, section_index)
    other_rows = swap_cores(half_slots(own_rows, 1 - section_index))
    entry, cotangent = ordered(is_first, kept_rows, other_rows)
    segment, position = layouts(
        lax.dynamic_index_in_dim(lengths, section_index, 0, keepdims=False), slot_count
    )
    tables = rotary_tables(position)
    mask = allowed_transposed(segment)

    def both(take):
        kept = take(section_index)
        other = swap_cores(take(1 - section_index))
        return ordered(is_first, kept, other)

    def take_narrow(which):
        thirds = [
            qkv_weight[0, :, part * features : (part + 1) * features] for part in range(3)
        ]
        return jnp.concatenate([half_of(part, which) for part in thirds + [out_weight[0]]], axis=1)

    pieces = (
        both(take_narrow),
        both(lambda which: half_of(up_weight[0], which)),
        both(lambda which: half_of(down_weight[0], which)),
    )

    small_shapes = [
        (qkv_bias.shape[1],),
        (up_bias.shape[1],),
        out_biases.shape[1:],
        norm_gains.shape[1:],
        norm_biases.shape[1:],
    ]
    small_own = jnp.concatenate(
        [a[0].reshape(-1) for a in (qkv_bias, up_bias, out_biases, norm_gains, norm_biases)]
    )
    small_both = jnp.concatenate(ordered(is_first, small_own, swap_cores(small_own)))
    small_full = gather_small(small_both[None])
    small_full = small_full.reshape(count, 2, small_own.shape[0]).astype(jnp.float32)

    def small_of(layer):
        rows = small_full[:, layer]
        found = []
        at = 0
        for shape in small_shapes:
            size = math.prod(shape)
            part = rows[:, at : at + size].reshape((count,) + shape)
            at += size
            if len(shape) == 2:
                part = part.transpose(1, 0, 2).reshape(shape[0], count * shape[1])
            else:
                part = part.reshape(1, count * shape[0])
            found.append(part)
        bias_qkv, bias_up, bias_out, gains, shifts = found
        bias_qkv = bias_qkv.reshape(3, 2, width).transpose(1, 0, 2).reshape(2, 3 * width)
        return dict(
            qkv=jnp.where(is_first, bias_qkv, bias_qkv[::-1]),
            up=bias_up,
            out=bias_out,
            norms=jnp.concatenate([gains, shifts]),
        )

    small = [small_of(layer) for layer in range(2)]
    flat_pieces = [piece[layer] for layer in range(2) for piece in pieces]
    kept_forward = {}

    def attn_step(layer, rows, weights):
        kept_forward[layer, "rows"] = rows
        made = attn_forward(side, rows, tables, mask, small[layer], *weights)
        kept_forward[layer, "attn"] = made
        return made

    def mlp_step(layer, up, down, kind):
        passed = kept_forward[layer, "attn"][3]
        rows = kept_forward[layer, "rows"]
        made = mlp_forward(side, rows, passed, small[layer], up + down, kind)
        kept_forward[layer, "mlp"] = made
        return made

    def mlp_back(layer, grad):
        rows = kept_forward[layer, "rows"]
        return mlp_backward(
            side, rows, grad, small[layer], kept_forward[layer, "mlp"][:2],
            gathered[layer][1] + gathered[layer][2],
        )

    def attn_back(layer, grad, grad_mlp, kind):
        return attn_backward(
            side, kept_forward[layer, "rows"], grad, tables, mask, small[layer],
            kept_forward[layer, "attn"][:3], grad_mlp, *gathered[layer][0], kind,
        )

    def vectors_of(bias_qkv, bias_up, sums):
        bias_qkv = jnp.where(is_first, bias_qkv, bias_qkv[::-1])
        bias_qkv = bias_qkv.reshape(2, 3, width).transpose(1, 0, 2).reshape(1, 6 * width)
        double = jnp.concatenate([sums[4:5], sums[4:5]])
        return (bias_qkv, bias_up, double, sums[0:2], sums[2:4])

    whole = {}
    if small_slice():
        rounds = Rounds(LAG)
        tied = rounds.tied
        chunks = [gather_stages(piece, tied) for piece in flat_pieces]
        for turn in range(len(chunks) + 4):
            for index in range(len(chunks)):
                if index <= turn <= index + 4:
                    advance(chunks[index], rounds, whole, index)
            if turn == 4:
                rounds.note(attn_step(0, entry, whole[0]))
            if turn == 6:
                rounds.note(mlp_step(0, whole[1], whole[2], jnp.bfloat16))
            if turn == 7:
                middle = kept_forward[0, "mlp"][2]
                rounds.note(attn_step(1, middle, whole[3]))
            rounds.close()
        mlp_step(1, whole[4], whole[5], jnp.float32)
    else:
        for index, piece in enumerate(flat_pieces):
            mine = gather_whole(piece)
            whole[index] = (mine, swap_cores(mine))
        attn_step(0, entry, whole[0])
        mlp_step(0, whole[1], whole[2], jnp.bfloat16)
        attn_step(1, kept_forward[0, "mlp"][2], whole[3])
        mlp_step(1, whole[4], whole[5], jnp.float32)
    gathered = [[whole[0], whole[1], whole[2]], [whole[3], whole[4], whole[5]]]
    produced = kept_forward[1, "mlp"][2]

    reduced = {}
    if small_slice():
        rounds = Rounds(LAG)
        tied = rounds.tied
        stages = {}
        plan = {
            "down1": (0, 1, 2, 3, 4),
            "up1": (0, 1, 3, 4, 5),
            "narrow1": (1, 2, 4, 5, 6),
            "down0": (2, 3, 5, 6, 7),
            "up0": (2, 4, 6, 7, 8),
            "narrow0": (3, 5, 7, 8, 9),
        }
        upper = mlp_back(1, cotangent)
        stages["down1"] = scatter_stages(upper[2], upper[3], tied)
        stages["up1"] = scatter_stages(upper[0], upper[1], tied)
        for turn in range(10):
            for name, when in plan.items():
                if turn in when:
                    advance(stages[name], rounds, reduced, name)
            if turn == 0:
                upper_attn = attn_back(1, cotangent, upper[5], jnp.bfloat16)
                stages["narrow1"] = scatter_stages(upper_attn[0], upper_attn[1], tied)
                rounds.note(upper_attn)
            if turn == 1:
                lower = mlp_back(0, upper_attn[4])
                stages["down0"] = scatter_stages(lower[2], lower[3], tied)
                stages["up0"] = scatter_stages(lower[0], lower[1], tied)
                rounds.note(lower)
            if turn == 2:
                lower_attn = attn_back(0, upper_attn[4], lower[5], jnp.float32)
                stages["narrow0"] = scatter_stages(lower_attn[0], lower_attn[1], tied)
                rounds.note(lower_attn)
            rounds.close()
    else:
        upper = mlp_back(1, cotangent)
        upper_attn = attn_back(1, cotangent, upper[5], jnp.bfloat16)
        lower = mlp_back(0, upper_attn[4])
        lower_attn = attn_back(0, upper_attn[4], lower[5], jnp.float32)
        for layer, mlp, attn in ((1, upper, upper_attn), (0, lower, lower_attn)):
            for name, kept, sent in (
                ("down", mlp[2], mlp[3]),
                ("up", mlp[0], mlp[1]),
                ("narrow", attn[0], attn[1]),
            ):
                summed = kept.astype(jnp.float32) + swap_cores(sent).astype(jnp.float32)
                reduced[name + str(layer)] = lax.psum_scatter(
                    summed, "dp", scatter_dimension=0, tiled=True
                )
    grad_entry = lower_attn[4]
    vectors_upper = vectors_of(upper_attn[2], upper[4], upper_attn[3])
    vectors_lower = vectors_of(lower_attn[2], lower[4], lower_attn[3])

    def finish(lower, upper):
        mine, leaving = ordered(is_first, lower, upper)
        return ordered(is_first, mine, swap_cores(leaving))

    down_halves, up_halves, narrow_halves = (
        finish(reduced[name + "0"], reduced[name + "1"]) for name in ("down", "up", "narrow")
    )
    total_down = jnp.concatenate(down_halves, axis=1)
    total_up = jnp.concatenate(up_halves, axis=1)
    total_qkv = jnp.concatenate(
        [
            part[:, at * width : (at + 1) * width]
            for at in range(3)
            for part in narrow_halves
        ],
        axis=1,
    )
    total_out = jnp.concatenate([part[:, 3 * width :] for part in narrow_halves], axis=1)

    def small_rows(vectors):
        parts = []
        for grad in vectors:
            part = grad.reshape(grad.shape[0], count, -1).transpose(1, 0, 2)
            parts.append(part.reshape(count, -1))
        return jnp.concatenate(parts, axis=1)

    small_kept, small_sent = ordered(
        is_first, small_rows(vectors_lower), small_rows(vectors_upper)
    )
    small_total = scatter_small(small_kept, small_sent)[0]
    small_outs = []
    at = 0
    for shape in small_shapes:
        size = math.prod(shape)
        small_outs.append(small_total[at : at + size].reshape((1,) + shape))
        at += size

    staying, leaving = ordered(is_first, grad_entry, produced)
    ends_out = jnp.concatenate(ordered(is_first, staying, swap_cores(leaving)))
    return (
        ends_out[None],
        total_qkv[None],
        small_outs[0],
        total_out[None],
        total_up[None],
        small_outs[1],
        total_down[None],
        small_outs[2],
        small_outs[3],
        small_outs[4],
    )


def solution(mesh):
    return jax.shard_map(
        on_device,
        mesh=mesh,
        in_specs=(
            P("section", "dp", None),
            P("dp", None),
            P("section", "dp", None),
            P("section", "dp"),
            P("section", "dp", None),
            P("section", "dp", None),
            P("section", "dp"),
            P("section", "dp", None),
            P("section", None, "dp"),
            P("section", None, "dp"),
            P("section", None, "dp"),
        ),
        out_specs=(
            P("section", "dp", None),
            P("section", "dp", None),
            P("section", "dp"),
            P("section", "dp", None),
            P("section", "dp", None),
            P("section", "dp"),
            P("section", "dp", None),
            P("section", None, "dp"),
            P("section", None, "dp"),
            P("section", None, "dp"),
        ),
        check_vma=False,
    )
```

```python
import math

import jax
import jax.numpy as jnp
from jax import lax
from jax.experimental import pallas as pl
from jax.experimental.pallas import tpu as pltpu
from jax.sharding import PartitionSpec as P

HD = 64
ROT = 16
LANES = 128
TILES = 3


eps = 1e-05
masked_score = -1e30
vmem_bytes = 48 * 1024 * 1024


def product(left, right):
    return jnp.dot(left, right, preferred_element_type=jnp.float32)


def product_transposed(left, right):
    return lax.dot_general(
        left, right, (((1,), (1,)), ((), ())), preferred_element_type=jnp.float32
    )


def layouts(lengths, slot_count):
    ends_at = jnp.cumsum(lengths)
    indices = jnp.arange(slot_count, dtype=jnp.int32)
    passed = indices[:, None] >= ends_at[None, :]
    segments = jnp.sum(passed.astype(jnp.int32), axis=1)
    starts = jnp.sum(jnp.where(passed, lengths[None, :], 0), axis=1)
    return (segments, indices - starts)


def rotary_tables(positions):
    lane = jnp.arange(LANES, dtype=jnp.int32) % HD
    half = ROT // 2
    freqs = 10000.0 ** (-2.0 * (lane % half).astype(jnp.float32) / ROT)
    angles = positions.astype(jnp.float32)[:, None] * freqs[None, :]
    cosine = jnp.where(lane < ROT, jnp.cos(angles), 1.0)
    sine = jnp.sin(angles)
    ahead = jnp.where(lane < half, -sine, 0.0)
    behind = jnp.where((lane >= half) & (lane < ROT), sine, 0.0)
    return jnp.stack([cosine, ahead, behind])


def allowed_transposed(segment):
    indices = jnp.arange(segment.shape[0], dtype=jnp.int32)
    allowed = (segment[:, None] == segment[None, :]) & (indices[:, None] <= indices[None, :])
    return allowed.astype(jnp.float32)


def turned(values, tables, back):
    half = ROT // 2
    parts = []
    for at in range(0, values.shape[1], LANES):
        part = values[:, at : at + LANES]
        moved = (
            pltpu.roll(part, LANES - half, 1) * tables[1] + pltpu.roll(part, half, 1) * tables[2]
        )
        kept = part * tables[0]
        parts.append(kept - moved if back else kept + moved)
    return jnp.concatenate(parts, axis=1)


def unit_rows(rows):
    centred = rows - jnp.mean(rows, axis=-1, keepdims=True)
    spread = jnp.mean(centred * centred, axis=-1, keepdims=True)
    scale = lax.rsqrt(spread + eps)
    return (centred * scale, scale)


def lane_half(which, width):
    return pl.ds(pl.multiple_of(which * width, LANES), width)


def head_lanes(values, which):
    lane = lax.broadcasted_iota(jnp.int32, values.shape, 1)
    return jnp.where((lane < HD) == (which == 0), values, jnp.zeros_like(values))


def scores_of(key_pair, query_pair, which, allowed):
    scores = product_transposed(head_lanes(key_pair, which), query_pair) * (1.0 / math.sqrt(HD))
    return jnp.where(allowed, scores, masked_score)


def attn_forward_kernel(
    side, rows, tables, mask, norms, bias_qkv, bias_out, mine, other, qkv, logs, attended, passed
):
    width = mine.shape[1] // 4
    entry = rows[...].astype(jnp.float32)
    unit, _ = unit_rows(entry)
    normed = (unit * norms[0:1] + norms[2:3]).astype(jnp.bfloat16)
    allowed = mask[...] > 0.5
    for at, weight in enumerate((mine, other)):
        half = side[0] if at == 0 else 1 - side[0]
        parts = []
        for part in range(3):
            cut = slice(part * width, (part + 1) * width)
            value = product(normed, weight[:, cut]) + bias_qkv[at : at + 1, cut]
            if part < 2:
                value = turned(value, tables, False)
            value = value.astype(jnp.bfloat16)
            qkv[at, :, cut] = value
            parts.append(value)
        queries, keys, values = parts
        values = values.T
        outs = []
        for pair in range(width // LANES):
            cut = slice(pair * LANES, (pair + 1) * LANES)
            for which in range(2):
                head = 2 * pair + which
                scores = scores_of(keys[:, cut], queries[:, cut], which, allowed)
                peak = jnp.max(scores, axis=0, keepdims=True)
                raised = jnp.exp(scores - peak)
                total = jnp.sum(raised, axis=0, keepdims=True)
                chances = (raised * (1.0 / total)).astype(jnp.bfloat16)
                outs.append(product(values[head * HD : (head + 1) * HD], chances))
                logs[at, head : head + 1, :] = peak + jnp.log(total)
        mixed = jnp.concatenate(outs, axis=0).T.astype(jnp.bfloat16)
        attended[:, lane_half(half, width)] = mixed
    mixed = attended[...]
    for at, weight in enumerate((mine, other)):
        half = side[0] if at == 0 else 1 - side[0]
        lanes = lane_half(half, width)
        passed[:, lanes] = (
            rows[:, lanes].astype(jnp.float32)
            + product(mixed, weight[:, 3 * width :])
            + bias_out[0:1, lanes]
        )


def whole_blocks(count):
    return [pl.BlockSpec(memory_space=pltpu.VMEM)] * count


def attn_forward(side, rows, tables, mask, small, mine, other):
    length, features = rows.shape
    width = features // 2
    heads = width // HD
    return pl.pallas_call(
        attn_forward_kernel,
        out_shape=(
            jax.ShapeDtypeStruct((2, length, 3 * width), jnp.bfloat16),
            jax.ShapeDtypeStruct((2, heads, length), jnp.float32),
            jax.ShapeDtypeStruct((length, features), jnp.bfloat16),
            jax.ShapeDtypeStruct((length, features), jnp.float32),
        ),
        in_specs=[pl.BlockSpec(memory_space=pltpu.SMEM)] + whole_blocks(8),
        out_specs=tuple(whole_blocks(4)),
        compiler_params=pltpu.CompilerParams(vmem_limit_bytes=vmem_bytes),
        cost_estimate=pl.CostEstimate(
            flops=2 * length * features * features * 5,
            bytes_accessed=8 * features * features,
            transcendentals=length * length * features // HD,
        ),
        name="attn_forward",
    )(side, rows, tables, mask, small["norms"], small["qkv"], small["out"], mine, other)


def tile_of(step, side):
    half = jnp.where(step < TILES, side[0], 1 - side[0])
    return half * TILES + step % TILES


def first_tile(step):
    return jnp.minimum(step, TILES - 1)


def second_tile(step):
    return jnp.maximum(step - TILES, 0)


def mlp_forward_kernel(
    side, rows, passed, norms, bias_up, bias_out, up_mine, up_other, down_mine, down_other,
    active, slope, produced, normed, sum_mine, sum_other
):
    step = pl.program_id(0)

    @pl.when(step == 0)
    def _():
        unit, _ = unit_rows(rows[...].astype(jnp.float32))
        normed[...] = (unit * norms[1:2] + norms[3:4]).astype(jnp.bfloat16)
        sum_mine[...] = jnp.zeros_like(sum_mine)
        sum_other[...] = jnp.zeros_like(sum_other)

    weight = jnp.where(step < TILES, up_mine[...], up_other[...])
    hidden = product(normed[...], weight) + bias_up[...]
    bell = 0.5 * (1.0 + lax.erf(hidden * (1.0 / math.sqrt(2.0))))
    density = jnp.exp(-0.5 * hidden * hidden) * (1.0 / math.sqrt(2.0 * math.pi))
    slope[...] = bell + hidden * density
    lit = (hidden * bell).astype(jnp.bfloat16)
    active[...] = lit
    sum_mine[...] += product(lit, down_mine[...])
    sum_other[...] += product(lit, down_other[...])

    @pl.when(step == 2 * TILES - 1)
    def _():
        width = sum_mine.shape[1]
        for half, total in ((side[0], sum_mine), (1 - side[0], sum_other)):
            lanes = lane_half(half, width)
            produced[:, lanes] = (
                passed[:, lanes] + total[...] + bias_out[1:2, lanes]
            ).astype(produced.dtype)


def mlp_forward(side, rows, passed, small, weights, kind):
    up_mine, up_other, down_mine, down_other = weights
    length, features = rows.shape
    hidden = down_mine.shape[0]
    tile = hidden // (2 * TILES)
    width = features // 2

    def fixed(*shape):
        return pl.BlockSpec(shape, lambda step, side: (0,) * len(shape))

    tiled = pl.BlockSpec((length, tile), lambda step, side: (0, tile_of(step, side)))
    down_spec = pl.BlockSpec((tile, width), lambda step, side: (tile_of(step, side), 0))
    return pl.pallas_call(
        mlp_forward_kernel,
        out_shape=(
            jax.ShapeDtypeStruct((length, hidden), jnp.bfloat16),
            jax.ShapeDtypeStruct((length, hidden), jnp.float32),
            jax.ShapeDtypeStruct((length, features), kind),
        ),
        grid_spec=pltpu.PrefetchScalarGridSpec(
            num_scalar_prefetch=1,
            grid=(2 * TILES,),
            in_specs=[
                fixed(length, features),
                fixed(length, features),
                fixed(4, features),
                pl.BlockSpec((1, tile), lambda step, side: (0, tile_of(step, side))),
                fixed(2, features),
                pl.BlockSpec((features, tile), lambda step, side: (0, first_tile(step))),
                pl.BlockSpec((features, tile), lambda step, side: (0, second_tile(step))),
                down_spec,
                down_spec,
            ],
            out_specs=(tiled, tiled, fixed(length, features)),
            scratch_shapes=[
                pltpu.VMEM((length, features), jnp.bfloat16),
                pltpu.VMEM((length, width), jnp.float32),
                pltpu.VMEM((length, width), jnp.float32),
            ],
        ),
        compiler_params=pltpu.CompilerParams(vmem_limit_bytes=vmem_bytes),
        cost_estimate=pl.CostEstimate(
            flops=4 * length * features * hidden,
            bytes_accessed=4 * features * hidden + 6 * length * hidden,
            transcendentals=2 * length * hidden,
        ),
        name="mlp_forward",
    )(
        side, rows, passed, small["norms"], small["up"], small["out"],
        up_mine, up_other, down_mine, down_other,
    )


def mlp_backward_kernel(
    side, rows, grad, norms, active, slope, up_mine, up_other, down_mine, down_other,
    up_kept, up_sent, down_kept, down_sent, bias_grad, grad_normed, normed
):
    step = pl.program_id(0)
    width = down_mine.shape[1]

    @pl.when(step == 0)
    def _():
        unit, _ = unit_rows(rows[...].astype(jnp.float32))
        normed[...] = (unit * norms[1:2] + norms[3:4]).T.astype(jnp.bfloat16)
        grad_normed[...] = jnp.zeros_like(grad_normed)

    grad_mine = grad[:, lane_half(side[0], width)]
    grad_other = grad[:, lane_half(1 - side[0], width)]
    weight = jnp.where(step < TILES, up_mine[...], up_other[...])
    lit = active[...].T
    down_kept[...] = product(lit, grad_mine).astype(jnp.bfloat16)
    down_sent[...] = product(lit, grad_other).astype(jnp.bfloat16)
    back = product_transposed(grad_mine, down_mine[...])
    back += product_transposed(grad_other, down_other[...])
    back = (back * slope[...]).astype(jnp.bfloat16)
    bias_grad[...] = jnp.sum(back.astype(jnp.float32), axis=0, keepdims=True)
    up_grad = product(normed[...], back).astype(jnp.bfloat16)

    @pl.when(step < TILES)
    def _():
        up_kept[...] = up_grad

    @pl.when(step >= TILES)
    def _():
        up_sent[...] = up_grad

    grad_normed[...] += product_transposed(back, weight)


def mlp_backward(side, rows, grad, small, saved, weights):
    active, slope = saved
    up_mine, up_other, down_mine, down_other = weights
    length, features = rows.shape
    hidden = down_mine.shape[0]
    tile = hidden // (2 * TILES)
    width = features // 2

    def fixed(*shape):
        return pl.BlockSpec(shape, lambda step, side: (0,) * len(shape))

    tiled = pl.BlockSpec((length, tile), lambda step, side: (0, tile_of(step, side)))
    down_spec = pl.BlockSpec((tile, width), lambda step, side: (tile_of(step, side), 0))
    up_first = pl.BlockSpec((features, tile), lambda step, side: (0, first_tile(step)))
    up_second = pl.BlockSpec((features, tile), lambda step, side: (0, second_tile(step)))
    return pl.pallas_call(
        mlp_backward_kernel,
        out_shape=(
            jax.ShapeDtypeStruct((features, hidden // 2), jnp.bfloat16),
            jax.ShapeDtypeStruct((features, hidden // 2), jnp.bfloat16),
            jax.ShapeDtypeStruct((hidden, width), jnp.bfloat16),
            jax.ShapeDtypeStruct((hidden, width), jnp.bfloat16),
            jax.ShapeDtypeStruct((1, hidden), jnp.float32),
            jax.ShapeDtypeStruct((length, features), jnp.float32),
        ),
        grid_spec=pltpu.PrefetchScalarGridSpec(
            num_scalar_prefetch=1,
            grid=(2 * TILES,),
            in_specs=[
                fixed(length, features),
                fixed(length, features),
                fixed(4, features),
                tiled,
                tiled,
                up_first,
                up_second,
                down_spec,
                down_spec,
            ],
            out_specs=(
                up_first,
                up_second,
                down_spec,
                down_spec,
                pl.BlockSpec((1, tile), lambda step, side: (0, tile_of(step, side))),
                fixed(length, features),
            ),
            scratch_shapes=[pltpu.VMEM((features, length), jnp.bfloat16)],
        ),
        compiler_params=pltpu.CompilerParams(vmem_limit_bytes=vmem_bytes),
        cost_estimate=pl.CostEstimate(
            flops=8 * length * features * hidden,
            bytes_accessed=8 * features * hidden + 6 * length * hidden,
            transcendentals=0,
        ),
        name="mlp_backward",
    )(
        side, rows, grad, small["norms"], active, slope,
        up_mine, up_other, down_mine, down_other,
    )


def attn_backward_kernel(
    side, rows, grad, tables, mask, norms, qkv, logs, attended, grad_mlp, mine, other,
    kept, sent, bias_grad, sums, passed, mixed_back
):
    width = mine.shape[1] // 4
    unit, scale = unit_rows(rows[...].astype(jnp.float32))
    normed = (unit * norms[0:1] + norms[2:3]).T.astype(jnp.bfloat16)
    allowed = mask[...] > 0.5
    mixed = attended[...].T
    back = None
    for at, (weight, result) in enumerate(((mine, kept), (other, sent))):
        half = side[0] if at == 0 else 1 - side[0]
        part = grad[:, lane_half(half, width)]
        result[:, 3 * width :] = product(mixed, part).astype(jnp.bfloat16)
        term = product_transposed(part, weight[:, 3 * width :])
        back = term if back is None else back + term
    mixed_back[...] = back.astype(jnp.bfloat16)
    grad_attn = None
    for at, (weight, result) in enumerate(((mine, kept), (other, sent))):
        half = side[0] if at == 0 else 1 - side[0]
        queries = qkv[at, :, 0:width]
        keys = qkv[at, :, width : 2 * width]
        values = qkv[at, :, 2 * width :]
        keys_turned = keys.T
        grad_out = mixed_back[:, lane_half(half, width)]
        query_grads, key_grads, value_grads = [], [], []
        for pair in range(width // LANES):
            cut = slice(pair * LANES, (pair + 1) * LANES)
            key_pair, value_pair = [], []
            for which in range(2):
                head = 2 * pair + which
                scores = scores_of(keys[:, cut], queries[:, cut], which, allowed)
                chances = jnp.exp(scores - logs[at, head : head + 1, :])
                value_pair.append(product(chances.astype(jnp.bfloat16), grad_out[:, cut]))
                slopes = product_transposed(head_lanes(values[:, cut], which), grad_out[:, cut])
                inner = jnp.sum(slopes * chances, axis=0, keepdims=True)
                slopes = (chances * (slopes - inner)).astype(jnp.bfloat16)
                key_pair.append(product(slopes, queries[:, cut]))
                query_grads.append(product(keys_turned[head * HD : (head + 1) * HD], slopes))
            lane = lax.broadcasted_iota(jnp.int32, key_pair[0].shape, 1)
            key_grads.append(jnp.where(lane < HD, key_pair[0], key_pair[1]))
            value_grads.append(jnp.where(lane < HD, value_pair[0], value_pair[1]))
        factor = 1.0 / math.sqrt(HD)
        query_grad = turned(jnp.concatenate(query_grads, axis=0).T * factor, tables, True)
        key_grad = turned(jnp.concatenate(key_grads, axis=1) * factor, tables, True)
        value_grad = jnp.concatenate(value_grads, axis=1)
        for index, part in enumerate((query_grad, key_grad, value_grad)):
            cut = slice(index * width, (index + 1) * width)
            part = part.astype(jnp.bfloat16)
            bias_grad[at : at + 1, cut] = jnp.sum(
                part.astype(jnp.float32), axis=0, keepdims=True
            )
            result[:, cut] = product(normed, part).astype(jnp.bfloat16)
            term = product_transposed(part, weight[:, cut])
            grad_attn = term if grad_attn is None else grad_attn + term
    grad_up = grad_mlp[...]
    grad_rows = grad[...].astype(jnp.float32)
    sums[0:1] = jnp.sum(unit * grad_attn, axis=0, keepdims=True)
    sums[1:2] = jnp.sum(unit * grad_up, axis=0, keepdims=True)
    sums[2:3] = jnp.sum(grad_attn, axis=0, keepdims=True)
    sums[3:4] = jnp.sum(grad_up, axis=0, keepdims=True)
    sums[4:5] = jnp.sum(grad_rows, axis=0, keepdims=True)
    inward = grad_attn * norms[0:1] + grad_up * norms[1:2]
    level = jnp.mean(inward, axis=-1, keepdims=True)
    along = jnp.mean(inward * unit, axis=-1, keepdims=True)
    passed[...] = (grad_rows + (inward - level - unit * along) * scale).astype(passed.dtype)


def attn_backward(side, rows, grad, tables, mask, small, saved, grad_mlp, mine, other, kind):
    qkv, logs, attended = saved
    length, features = rows.shape
    return pl.pallas_call(
        attn_backward_kernel,
        out_shape=(
            jax.ShapeDtypeStruct(mine.shape, jnp.bfloat16),
            jax.ShapeDtypeStruct(mine.shape, jnp.bfloat16),
            jax.ShapeDtypeStruct((2, 3 * features // 2), jnp.float32),
            jax.ShapeDtypeStruct((5, features), jnp.float32),
            jax.ShapeDtypeStruct((length, features), kind),
        ),
        in_specs=[pl.BlockSpec(memory_space=pltpu.SMEM)] + whole_blocks(11),
        out_specs=tuple(whole_blocks(5)),
        scratch_shapes=[pltpu.VMEM((length, features), jnp.bfloat16)],
        compiler_params=pltpu.CompilerParams(vmem_limit_bytes=vmem_bytes),
        cost_estimate=pl.CostEstimate(
            flops=2 * length * features * features * 12,
            bytes_accessed=16 * features * features,
            transcendentals=length * length * features // HD,
        ),
        name="attn_backward",
    )(
        side, rows, grad, tables, mask, small["norms"], qkv, logs, attended, grad_mlp, mine, other
    )


SQUARE = 4
RING = 4
LAG = 2


def swap_cores(value):
    return lax.ppermute(value, "section", [(0, 1), (1, 0)])


def swap_square(value, bit):
    count = lax.axis_size("dp")
    return lax.ppermute(value, "dp", [(i, i ^ bit) for i in range(count)])


def shift_ring(value, steps):
    count = lax.axis_size("dp")
    pairs = [(i, (i + SQUARE * steps) % count) for i in range(count)]
    return lax.ppermute(value, "dp", pairs)


def small_slice():
    return lax.axis_size("dp") == SQUARE * RING


def place_kernel(spot_ref, own, first, second, far_low, far_high, out, sems):
    spot = spot_ref[0]
    half = RING // 2
    copies = [
        pltpu.make_async_copy(own, out.at[:, spot], sems.at[0]),
        pltpu.make_async_copy(first, out.at[:, spot ^ 1], sems.at[1]),
        pltpu.make_async_copy(second, out.at[:, spot ^ 2], sems.at[2]),
        pltpu.make_async_copy(far_low, out.at[pl.ds(0, half), spot ^ 3], sems.at[3]),
        pltpu.make_async_copy(far_high, out.at[pl.ds(half, half), spot ^ 3], sems.at[4]),
    ]
    for copy in copies:
        copy.start()
    for copy in copies:
        copy.wait()


def place_blocks(spot, blocks):
    _, rows, columns = blocks[0].shape
    any_space = pl.BlockSpec(memory_space=pl.ANY)
    return pl.pallas_call(
        place_kernel,
        out_shape=jax.ShapeDtypeStruct((RING, SQUARE, rows, columns), blocks[0].dtype),
        in_specs=[pl.BlockSpec(memory_space=pltpu.SMEM)] + [any_space] * 5,
        out_specs=pl.BlockSpec(memory_space=pltpu.VMEM),
        scratch_shapes=[pltpu.SemaphoreType.DMA((5,))],
        compiler_params=pltpu.CompilerParams(vmem_limit_bytes=vmem_bytes),
        name="place_blocks",
    )(spot, *blocks)


def after(values, earlier):
    flat, shape = jax.tree.flatten(values)
    waited = jax.tree.leaves(earlier)
    if not waited:
        return values
    tied = lax.optimization_barrier(tuple(flat) + tuple(waited))
    return jax.tree.unflatten(shape, tied[: len(flat)])


def gather_whole(piece):
    return lax.all_gather(piece, "dp", axis=0, tiled=True)


def column_moved(piece):
    return [piece] + [shift_ring(piece, steps) for steps in range(1, RING)]


def column_kernel(level_ref, *refs):
    held, out, sems = refs[:RING], refs[RING], refs[RING + 1]
    level = level_ref[0]
    copies = [
        pltpu.make_async_copy(part, out.at[lax.rem(level + RING - steps, RING)], sems.at[steps])
        for steps, part in enumerate(held)
    ]
    for copy in copies:
        copy.start()
    for copy in copies:
        copy.wait()


def column_placed(held):
    level = (lax.axis_index("dp") // SQUARE).astype(jnp.int32).reshape(1)
    return pl.pallas_call(
        column_kernel,
        out_shape=jax.ShapeDtypeStruct((RING,) + held[0].shape, held[0].dtype),
        in_specs=[pl.BlockSpec(memory_space=pltpu.SMEM)]
        + [pl.BlockSpec(memory_space=pl.ANY)] * RING,
        out_specs=pl.BlockSpec(memory_space=pltpu.VMEM),
        scratch_shapes=[pltpu.SemaphoreType.DMA((RING,))],
        name="place_column",
    )(level, *held)


def gather_stages(piece, tied):
    held = column_moved(tied(piece))
    yield held[1:]
    column = tied(column_placed(held))
    first = swap_square(column, 1)
    second = swap_square(column, 2)
    yield (first, second)
    half = RING // 2
    low, high = tied((first[:half], second[half:]))
    far_low = swap_square(low, 2)
    far_high = swap_square(high, 1)
    yield (far_low, far_high)
    spot = (lax.axis_index("dp") % SQUARE).astype(jnp.int32).reshape(1)
    whole = place_blocks(spot, (column, first, second, far_low, far_high))
    whole = tied(whole.reshape(RING * SQUARE * piece.shape[0], piece.shape[1]))
    other = swap_cores(whole)
    yield other
    return (whole, other)


def gather_small(piece):
    if not small_slice():
        return gather_whole(piece)
    spot = lax.axis_index("dp") % SQUARE
    level = lax.axis_index("dp") // SQUARE
    order = (level - jnp.arange(RING)) % RING
    column = jnp.take(jnp.stack(column_moved(piece)), order, axis=0)
    blocks = [column] + [swap_square(column, bit) for bit in range(1, SQUARE)]
    stacked = jnp.stack(blocks, axis=1)
    order = jnp.arange(SQUARE) ^ spot
    return jnp.take(stacked, order, axis=1).reshape(RING * SQUARE * piece.shape[0], -1)


def scatter_stages(kept, sent, tied):
    wire = jnp.bfloat16
    rows = kept.shape[0] // (RING * SQUARE)
    columns = kept.shape[1]
    place = lax.axis_index("dp")
    level = place // SQUARE
    spot = place % SQUARE
    received = swap_cores(tied(sent))
    yield received
    kept = kept.reshape(RING, SQUARE, rows, columns)
    received = received.reshape(RING, SQUARE, rows, columns)

    def block(index):
        mine = lax.dynamic_index_in_dim(kept, index, 1, keepdims=False)
        theirs = lax.dynamic_index_in_dim(received, index, 1, keepdims=False)
        return mine.astype(jnp.float32) + theirs.astype(jnp.float32)

    half = RING // 2
    far = block(spot ^ 3).astype(wire)
    low, high = tied((far[:half], far[half:]))
    far_low = swap_square(low, 1)
    far_high = swap_square(high, 2)
    yield (far_low, far_high)
    first = block(spot ^ 1)
    second = block(spot ^ 2)
    first = jnp.concatenate([first[:half], first[half:] + far_high.astype(jnp.float32)])
    second = jnp.concatenate([second[:half] + far_low.astype(jnp.float32), second[half:]])
    first, second = tied((first.astype(wire), second.astype(wire)))
    from_first = swap_square(first, 1)
    from_second = swap_square(second, 2)
    yield (from_first, from_second)
    column = block(spot) + from_first.astype(jnp.float32) + from_second.astype(jnp.float32)
    column = [lax.dynamic_index_in_dim(column, (level + steps) % RING, 0, keepdims=False) for steps in range(RING)]
    moving = tied(tuple(part.astype(wire) for part in column[1:]))
    moved = [shift_ring(part, steps + 1) for steps, part in enumerate(moving)]
    yield tuple(moved)
    total = column[0]
    for part in moved:
        total = total + part.astype(jnp.float32)
    return total


def scatter_small(kept, sent):
    summed = kept + swap_cores(sent)
    if not small_slice():
        return lax.psum_scatter(summed, "dp", scatter_dimension=0, tiled=True)
    place = lax.axis_index("dp")
    level = place // SQUARE
    spot = place % SQUARE
    blocks = summed.reshape(RING, SQUARE, -1)

    def block(index):
        return lax.dynamic_index_in_dim(blocks, index, 1, keepdims=False)

    column = block(spot)
    for bit in range(1, SQUARE):
        column = column + swap_square(block(spot ^ bit), bit)
    total = lax.dynamic_index_in_dim(column, level, 0, keepdims=True)
    for steps in range(1, RING):
        part = lax.dynamic_index_in_dim(column, (level + steps) % RING, 0, keepdims=True)
        total = total + shift_ring(part, steps)
    return total


class Rounds:
    def __init__(self, lag):
        self.lag = lag
        self.made = []
        self.current = []

    def tied(self, values):
        at = len(self.made) - self.lag
        return after(values, self.made[at]) if at >= 0 else values

    def note(self, values):
        self.current.append(values)

    def close(self):
        self.made.append(self.current)
        self.current = []


def advance(stages, rounds, results, name):
    try:
        rounds.note(next(stages))
    except StopIteration as ended:
        results[name] = ended.value


def half_of(array, which):
    width = array.shape[1] // 2
    return lax.dynamic_slice_in_dim(array, which * width, width, 1)


def half_slots(array, which):
    length = array.shape[0] // 2
    return lax.dynamic_slice_in_dim(array, which * length, length, 0)


def ordered(is_first, mine, other):
    return (jnp.where(is_first, mine, other), jnp.where(is_first, other, mine))


def on_device(
    ends_in,
    lengths,
    qkv_weight,
    qkv_bias,
    out_weight,
    up_weight,
    up_bias,
    down_weight,
    out_biases,
    norm_gains,
    norm_biases,
):
    section_index = lax.axis_index("section")
    is_first = section_index == 0
    side = section_index.astype(jnp.int32).reshape(1)
    features = ends_in.shape[2]
    width = features // 2
    count = lax.axis_size("dp")
    own_rows = ends_in[0]
    slot_count = own_rows.shape[0] // 2
    kept_rows = half_slots(own_rows, section_index)
    other_rows = swap_cores(half_slots(own_rows, 1 - section_index))
    entry, cotangent = ordered(is_first, kept_rows, other_rows)
    segment, position = layouts(
        lax.dynamic_index_in_dim(lengths, section_index, 0, keepdims=False), slot_count
    )
    tables = rotary_tables(position)
    mask = allowed_transposed(segment)

    def both(take):
        kept = take(section_index)
        other = swap_cores(take(1 - section_index))
        return ordered(is_first, kept, other)

    def take_narrow(which):
        thirds = [
            qkv_weight[0, :, part * features : (part + 1) * features] for part in range(3)
        ]
        return jnp.concatenate([half_of(part, which) for part in thirds + [out_weight[0]]], axis=1)

    pieces = (
        both(take_narrow),
        both(lambda which: half_of(up_weight[0], which)),
        both(lambda which: half_of(down_weight[0], which)),
    )

    small_shapes = [
        (qkv_bias.shape[1],),
        (up_bias.shape[1],),
        out_biases.shape[1:],
        norm_gains.shape[1:],
        norm_biases.shape[1:],
    ]
    small_own = jnp.concatenate(
        [a[0].reshape(-1) for a in (qkv_bias, up_bias, out_biases, norm_gains, norm_biases)]
    )
    small_both = jnp.concatenate(ordered(is_first, small_own, swap_cores(small_own)))
    small_full = gather_small(small_both[None])
    small_full = small_full.reshape(count, 2, small_own.shape[0]).astype(jnp.float32)

    def small_of(layer):
        rows = small_full[:, layer]
        found = []
        at = 0
        for shape in small_shapes:
            size = math.prod(shape)
            part = rows[:, at : at + size].reshape((count,) + shape)
            at += size
            if len(shape) == 2:
                part = part.transpose(1, 0, 2).reshape(shape[0], count * shape[1])
            else:
                part = part.reshape(1, count * shape[0])
            found.append(part)
        bias_qkv, bias_up, bias_out, gains, shifts = found
        bias_qkv = bias_qkv.reshape(3, 2, width).transpose(1, 0, 2).reshape(2, 3 * width)
        return dict(
            qkv=jnp.where(is_first, bias_qkv, bias_qkv[::-1]),
            up=bias_up,
            out=bias_out,
            norms=jnp.concatenate([gains, shifts]),
        )

    small = [small_of(layer) for layer in range(2)]
    flat_pieces = [piece[layer] for layer in range(2) for piece in pieces]
    kept_forward = {}

    def attn_step(layer, rows, weights):
        kept_forward[layer, "rows"] = rows
        made = attn_forward(side, rows, tables, mask, small[layer], *weights)
        kept_forward[layer, "attn"] = made
        return made

    def mlp_step(layer, up, down, kind):
        passed = kept_forward[layer, "attn"][3]
        rows = kept_forward[layer, "rows"]
        made = mlp_forward(side, rows, passed, small[layer], up + down, kind)
        kept_forward[layer, "mlp"] = made
        return made

    def mlp_back(layer, grad):
        rows = kept_forward[layer, "rows"]
        return mlp_backward(
            side, rows, grad, small[layer], kept_forward[layer, "mlp"][:2],
            gathered[layer][1] + gathered[layer][2],
        )

    def attn_back(layer, grad, grad_mlp, kind):
        return attn_backward(
            side, kept_forward[layer, "rows"], grad, tables, mask, small[layer],
            kept_forward[layer, "attn"][:3], grad_mlp, *gathered[layer][0], kind,
        )

    def vectors_of(bias_qkv, bias_up, sums):
        bias_qkv = jnp.where(is_first, bias_qkv, bias_qkv[::-1])
        bias_qkv = bias_qkv.reshape(2, 3, width).transpose(1, 0, 2).reshape(1, 6 * width)
        double = jnp.concatenate([sums[4:5], sums[4:5]])
        return (bias_qkv, bias_up, double, sums[0:2], sums[2:4])

    whole = {}
    if small_slice():
        rounds = Rounds(LAG)
        tied = rounds.tied
        rows, columns = flat_pieces[3].shape
        deep = flat_pieces[5].reshape(-1, rows, width).transpose(1, 0, 2).reshape(rows, -1)
        packed = gather_whole(jnp.concatenate([flat_pieces[3], flat_pieces[4], deep], axis=1))
        chunks = [gather_stages(piece, tied) for piece in flat_pieces[:3]]
        for turn in range(len(chunks) + 4):
            for index in range(len(chunks)):
                if index <= turn <= index + 4:
                    advance(chunks[index], rounds, whole, index)
            if turn == 4:
                rounds.note(attn_step(0, entry, whole[0]))
            rounds.close()
        mlp_step(0, whole[1], whole[2], jnp.bfloat16)
        packed = after(packed, kept_forward[0, "attn"][3])
        deep = packed[:, 2 * columns :].reshape(count, rows, -1, width).transpose(0, 2, 1, 3)
        parts = (packed[:, :columns], packed[:, columns : 2 * columns], deep.reshape(-1, width))
        for index, part in enumerate(parts):
            whole[3 + index] = (part, swap_cores(part))
        attn_step(1, kept_forward[0, "mlp"][2], whole[3])
        mlp_step(1, whole[4], whole[5], jnp.float32)
    else:
        for index, piece in enumerate(flat_pieces):
            mine = gather_whole(piece)
            whole[index] = (mine, swap_cores(mine))
        attn_step(0, entry, whole[0])
        mlp_step(0, whole[1], whole[2], jnp.bfloat16)
        attn_step(1, kept_forward[0, "mlp"][2], whole[3])
        mlp_step(1, whole[4], whole[5], jnp.float32)
    gathered = [[whole[0], whole[1], whole[2]], [whole[3], whole[4], whole[5]]]
    produced = kept_forward[1, "mlp"][2]

    reduced = {}
    if small_slice():
        rounds = Rounds(LAG)
        tied = rounds.tied
        stages = {}
        plan = {
            "down1": (0, 1, 2, 3, 4),
            "up1": (0, 1, 3, 4, 5),
            "narrow1": (1, 2, 4, 5, 6),
            "down0": (2, 3, 5, 6, 7),
            "up0": (2, 4, 6, 7, 8),
            "narrow0": (3, 5, 7, 8, 9),
        }
        upper = mlp_back(1, cotangent)
        stages["down1"] = scatter_stages(upper[2], upper[3], tied)
        stages["up1"] = scatter_stages(upper[0], upper[1], tied)
        for turn in range(10):
            for name, when in plan.items():
                if turn in when:
                    advance(stages[name], rounds, reduced, name)
            if turn == 0:
                upper_attn = attn_back(1, cotangent, upper[5], jnp.bfloat16)
                stages["narrow1"] = scatter_stages(upper_attn[0], upper_attn[1], tied)
                rounds.note(upper_attn)
            if turn == 1:
                lower = mlp_back(0, after(upper_attn[4], rounds.made[-1]))
                stages["down0"] = scatter_stages(lower[2], lower[3], tied)
                stages["up0"] = scatter_stages(lower[0], lower[1], tied)
                rounds.note(lower)
            if turn == 2:
                lower_attn = attn_back(
                    0, upper_attn[4], after(lower[5], rounds.made[-1]), jnp.float32
                )
                stages["narrow0"] = scatter_stages(lower_attn[0], lower_attn[1], tied)
                rounds.note(lower_attn)
            rounds.close()
    else:
        upper = mlp_back(1, cotangent)
        upper_attn = attn_back(1, cotangent, upper[5], jnp.bfloat16)
        lower = mlp_back(0, upper_attn[4])
        lower_attn = attn_back(0, upper_attn[4], lower[5], jnp.float32)
        for layer, mlp, attn in ((1, upper, upper_attn), (0, lower, lower_attn)):
            for name, kept, sent in (
                ("down", mlp[2], mlp[3]),
                ("up", mlp[0], mlp[1]),
                ("narrow", attn[0], attn[1]),
            ):
                summed = kept.astype(jnp.float32) + swap_cores(sent).astype(jnp.float32)
                reduced[name + str(layer)] = lax.psum_scatter(
                    summed, "dp", scatter_dimension=0, tiled=True
                )
    grad_entry = lower_attn[4]
    vectors_upper = vectors_of(upper_attn[2], upper[4], upper_attn[3])
    vectors_lower = vectors_of(lower_attn[2], lower[4], lower_attn[3])

    def finish(lower, upper):
        mine, leaving = ordered(is_first, lower, upper)
        return ordered(is_first, mine, swap_cores(leaving))

    down_halves, up_halves, narrow_halves = (
        finish(reduced[name + "0"], reduced[name + "1"]) for name in ("down", "up", "narrow")
    )
    total_down = jnp.concatenate(down_halves, axis=1)
    total_up = jnp.concatenate(up_halves, axis=1)
    total_qkv = jnp.concatenate(
        [
            part[:, at * width : (at + 1) * width]
            for at in range(3)
            for part in narrow_halves
        ],
        axis=1,
    )
    total_out = jnp.concatenate([part[:, 3 * width :] for part in narrow_halves], axis=1)

    def small_rows(vectors):
        parts = []
        for grad in vectors:
            part = grad.reshape(grad.shape[0], count, -1).transpose(1, 0, 2)
            parts.append(part.reshape(count, -1))
        return jnp.concatenate(parts, axis=1)

    small_kept, small_sent = ordered(
        is_first, small_rows(vectors_lower), small_rows(vectors_upper)
    )
    small_total = scatter_small(small_kept, small_sent)[0]
    small_outs = []
    at = 0
    for shape in small_shapes:
        size = math.prod(shape)
        small_outs.append(small_total[at : at + size].reshape((1,) + shape))
        at += size

    staying, leaving = ordered(is_first, grad_entry, produced)
    ends_out = jnp.concatenate(ordered(is_first, staying, swap_cores(leaving)))
    return (
        ends_out[None],
        total_qkv[None],
        small_outs[0],
        total_out[None],
        total_up[None],
        small_outs[1],
        total_down[None],
        small_outs[2],
        small_outs[3],
        small_outs[4],
    )


def solution(mesh):
    return jax.shard_map(
        on_device,
        mesh=mesh,
        in_specs=(
            P("section", "dp", None),
            P("dp", None),
            P("section", "dp", None),
            P("section", "dp"),
            P("section", "dp", None),
            P("section", "dp", None),
            P("section", "dp"),
            P("section", "dp", None),
            P("section", None, "dp"),
            P("section", None, "dp"),
            P("section", None, "dp"),
        ),
        out_specs=(
            P("section", "dp", None),
            P("section", "dp", None),
            P("section", "dp"),
            P("section", "dp", None),
            P("section", "dp", None),
            P("section", "dp"),
            P("section", "dp", None),
            P("section", None, "dp"),
            P("section", None, "dp"),
            P("section", None, "dp"),
        ),
        check_vma=False,
    )
```

```python
import math

import jax
import jax.numpy as jnp
from jax import lax
from jax.experimental import pallas as pl
from jax.experimental.pallas import tpu as pltpu
from jax.sharding import PartitionSpec as P

HD = 64
ROT = 16
LANES = 128
TILES = 4
PARTS = 16


eps = 1e-05
masked_score = -1e30
vmem_bytes = 48 * 1024 * 1024


def product(left, right):
    return jnp.dot(left, right, preferred_element_type=jnp.float32)


def product_transposed(left, right):
    return lax.dot_general(
        left, right, (((1,), (1,)), ((), ())), preferred_element_type=jnp.float32
    )


def layouts(lengths, slot_count):
    ends_at = jnp.cumsum(lengths)
    indices = jnp.arange(slot_count, dtype=jnp.int32)
    passed = indices[:, None] >= ends_at[None, :]
    segments = jnp.sum(passed.astype(jnp.int32), axis=1)
    starts = jnp.sum(jnp.where(passed, lengths[None, :], 0), axis=1)
    return (segments, indices - starts)


def rotary_tables(positions):
    lane = jnp.arange(LANES, dtype=jnp.int32) % HD
    half = ROT // 2
    freqs = 10000.0 ** (-2.0 * (lane % half).astype(jnp.float32) / ROT)
    angles = positions.astype(jnp.float32)[:, None] * freqs[None, :]
    cosine = jnp.where(lane < ROT, jnp.cos(angles), 1.0)
    sine = jnp.sin(angles)
    ahead = jnp.where(lane < half, -sine, 0.0)
    behind = jnp.where((lane >= half) & (lane < ROT), sine, 0.0)
    return jnp.stack([cosine, ahead, behind])


def allowed_transposed(segment):
    indices = jnp.arange(segment.shape[0], dtype=jnp.int32)
    allowed = (segment[:, None] == segment[None, :]) & (indices[:, None] <= indices[None, :])
    return allowed.astype(jnp.float32)


def turned(values, tables, back):
    half = ROT // 2
    parts = []
    for at in range(0, values.shape[1], LANES):
        part = values[:, at : at + LANES]
        moved = (
            pltpu.roll(part, LANES - half, 1) * tables[1] + pltpu.roll(part, half, 1) * tables[2]
        )
        kept = part * tables[0]
        parts.append(kept - moved if back else kept + moved)
    return jnp.concatenate(parts, axis=1)


def unit_rows(rows):
    centred = rows - jnp.mean(rows, axis=-1, keepdims=True)
    spread = jnp.mean(centred * centred, axis=-1, keepdims=True)
    scale = lax.rsqrt(spread + eps)
    return (centred * scale, scale)


def lane_half(which, width):
    return pl.ds(pl.multiple_of(which * width, LANES), width)


def head_lanes(values, which):
    lane = lax.broadcasted_iota(jnp.int32, values.shape, 1)
    return jnp.where((lane < HD) == (which == 0), values, jnp.zeros_like(values))


def scores_of(key_pair, query_pair, which, allowed):
    scores = product_transposed(head_lanes(key_pair, which), query_pair) * (1.0 / math.sqrt(HD))
    return jnp.where(allowed, scores, masked_score)


def attn_forward_kernel(
    side, rows, tables, mask, norms, bias_qkv, bias_out, mine, other, qkv, logs, attended, passed
):
    width = mine.shape[1] // 4
    entry = rows[...].astype(jnp.float32)
    unit, _ = unit_rows(entry)
    normed = (unit * norms[0:1] + norms[2:3]).astype(jnp.bfloat16)
    allowed = mask[...] > 0.5
    for at, weight in enumerate((mine, other)):
        half = side[0] if at == 0 else 1 - side[0]
        parts = []
        for part in range(3):
            cut = slice(part * width, (part + 1) * width)
            value = product(normed, weight[:, cut]) + bias_qkv[at : at + 1, cut]
            if part < 2:
                value = turned(value, tables, False)
            value = value.astype(jnp.bfloat16)
            qkv[at, :, cut] = value
            parts.append(value)
        queries, keys, values = parts
        values = values.T
        outs = []
        for pair in range(width // LANES):
            cut = slice(pair * LANES, (pair + 1) * LANES)
            for which in range(2):
                head = 2 * pair + which
                scores = scores_of(keys[:, cut], queries[:, cut], which, allowed)
                peak = jnp.max(scores, axis=0, keepdims=True)
                raised = jnp.exp(scores - peak)
                total = jnp.sum(raised, axis=0, keepdims=True)
                chances = (raised * (1.0 / total)).astype(jnp.bfloat16)
                outs.append(product(values[head * HD : (head + 1) * HD], chances))
                logs[at, head : head + 1, :] = peak + jnp.log(total)
        mixed = jnp.concatenate(outs, axis=0).T.astype(jnp.bfloat16)
        attended[:, lane_half(half, width)] = mixed
    mixed = attended[...]
    for at, weight in enumerate((mine, other)):
        half = side[0] if at == 0 else 1 - side[0]
        lanes = lane_half(half, width)
        passed[:, lanes] = (
            rows[:, lanes].astype(jnp.float32)
            + product(mixed, weight[:, 3 * width :])
            + bias_out[0:1, lanes]
        )


def fixed(*shape):
    return pl.BlockSpec(shape, lambda *at: (0,) * len(shape))


def fixed_like(*arrays):
    return [fixed(*array.shape) for array in arrays]


def attn_forward(side, rows, tables, mask, small, mine, other):
    length, features = rows.shape
    width = features // 2
    heads = width // HD
    return pl.pallas_call(
        attn_forward_kernel,
        out_shape=(
            jax.ShapeDtypeStruct((2, length, 3 * width), jnp.bfloat16),
            jax.ShapeDtypeStruct((2, heads, length), jnp.float32),
            jax.ShapeDtypeStruct((length, features), jnp.bfloat16),
            jax.ShapeDtypeStruct((length, features), jnp.float32),
        ),
        grid=(1,),
        in_specs=[pl.BlockSpec(memory_space=pltpu.SMEM)]
        + fixed_like(rows, tables, mask, small["norms"], small["qkv"], small["out"])
        + [fixed(features, 4 * width)] * 2,
        out_specs=(
            fixed(2, length, 3 * width),
            fixed(2, heads, length),
            fixed(length, features),
            fixed(length, features),
        ),
        compiler_params=pltpu.CompilerParams(vmem_limit_bytes=vmem_bytes),
        cost_estimate=pl.CostEstimate(
            flops=2 * length * features * features * 5,
            bytes_accessed=8 * features * features,
            transcendentals=length * length * features // HD,
        ),
        name="attn_forward",
    )(side, rows, tables, mask, small["norms"], small["qkv"], small["out"], mine, other)


def tile_of(step, side):
    half = jnp.where(step < TILES, side[0], 1 - side[0])
    return half * TILES + step % TILES


def first_tile(step):
    return jnp.minimum(step, TILES - 1)


def second_tile(step):
    return jnp.maximum(step - TILES, 0)


def folded_cuts(shape, width):
    rows = shape[0] // 2
    for part in range(2):
        for column in range(shape[1] // width):
            yield (
                slice(part * rows, (part + 1) * rows),
                slice(column * width, (column + 1) * width),
            )


def unfolded(block, width):
    return jnp.concatenate([block[cut] for cut in folded_cuts(block.shape, width)], axis=0)


def mlp_forward_kernel(
    side, rows, passed, norms, bias_up, bias_out, up_mine, up_other, down_mine, down_other,
    active, slope, produced, normed, sum_mine, sum_other
):
    step = pl.program_id(0)

    @pl.when(step == 0)
    def _():
        unit, _ = unit_rows(rows[...].astype(jnp.float32))
        normed[...] = (unit * norms[1:2] + norms[3:4]).astype(jnp.bfloat16)
        sum_mine[...] = jnp.zeros_like(sum_mine)
        sum_other[...] = jnp.zeros_like(sum_other)

    weight = jnp.where(step < TILES, up_mine[...], up_other[...])
    hidden = product(normed[...], weight) + bias_up[...]
    bell = 0.5 * (1.0 + lax.erf(hidden * (1.0 / math.sqrt(2.0))))
    density = jnp.exp(-0.5 * hidden * hidden) * (1.0 / math.sqrt(2.0 * math.pi))
    slope[...] = bell + hidden * density
    lit = (hidden * bell).astype(jnp.bfloat16)
    active[...] = lit
    width = sum_mine.shape[1]
    sum_mine[...] += product(lit, unfolded(down_mine, width))
    sum_other[...] += product(lit, unfolded(down_other, width))

    @pl.when(step == 2 * TILES - 1)
    def _():
        for half, total in ((side[0], sum_mine), (1 - side[0], sum_other)):
            lanes = lane_half(half, width)
            produced[:, lanes] = (
                passed[:, lanes] + total[...] + bias_out[1:2, lanes]
            ).astype(produced.dtype)


def mlp_forward(side, rows, passed, small, weights, places, kind):
    up_mine, up_other, down_mine, down_other = weights
    up_at, down_at = places
    length, features = rows.shape
    width = features // 2
    tile = width
    hidden = 2 * TILES * tile
    folded = features // (2 * TILES)
    tiled = pl.BlockSpec((length, tile), lambda step, side: (0, tile_of(step, side)))
    down_spec = pl.BlockSpec(
        (folded, TILES * width), lambda step, side: (tile_of(step, side), down_at)
    )
    return pl.pallas_call(
        mlp_forward_kernel,
        out_shape=(
            jax.ShapeDtypeStruct((length, hidden), jnp.bfloat16),
            jax.ShapeDtypeStruct((length, hidden), jnp.float32),
            jax.ShapeDtypeStruct((length, features), kind),
        ),
        grid_spec=pltpu.PrefetchScalarGridSpec(
            num_scalar_prefetch=1,
            grid=(2 * TILES,),
            in_specs=[
                fixed(length, features),
                fixed(length, features),
                fixed(4, features),
                pl.BlockSpec((1, tile), lambda step, side: (0, tile_of(step, side))),
                fixed(2, features),
                pl.BlockSpec((features, tile), lambda step, side: (0, up_at + first_tile(step))),
                pl.BlockSpec((features, tile), lambda step, side: (0, up_at + second_tile(step))),
                down_spec,
                down_spec,
            ],
            out_specs=(tiled, tiled, fixed(length, features)),
            scratch_shapes=[
                pltpu.VMEM((length, features), jnp.bfloat16),
                pltpu.VMEM((length, width), jnp.float32),
                pltpu.VMEM((length, width), jnp.float32),
            ],
        ),
        compiler_params=pltpu.CompilerParams(vmem_limit_bytes=vmem_bytes),
        cost_estimate=pl.CostEstimate(
            flops=4 * length * features * hidden,
            bytes_accessed=4 * features * hidden + 6 * length * hidden,
            transcendentals=2 * length * hidden,
        ),
        name="mlp_forward",
    )(
        side, rows, passed, small["norms"], small["up"], small["out"],
        up_mine, up_other, down_mine, down_other,
    )


def mlp_backward_kernel(
    side, rows, grad, norms, active, slope, up_mine, up_other, down_mine, down_other,
    up_kept, up_sent, down_kept, down_sent, bias_grad, grad_normed, normed
):
    step = pl.program_id(0)
    width = grad.shape[1] // 2
    cuts = list(folded_cuts(down_mine.shape, width))

    @pl.when(step == 0)
    def _():
        unit, _ = unit_rows(rows[...].astype(jnp.float32))
        normed[...] = (unit * norms[1:2] + norms[3:4]).T.astype(jnp.bfloat16)
        grad_normed[...] = jnp.zeros_like(grad_normed)

    grad_mine = grad[:, lane_half(side[0], width)]
    grad_other = grad[:, lane_half(1 - side[0], width)]
    weight = jnp.where(step < TILES, up_mine[...], up_other[...])
    lit = active[...].T
    for grad_half, result in ((grad_mine, down_kept), (grad_other, down_sent)):
        made = product(lit, grad_half).astype(jnp.bfloat16)
        rows_each = made.shape[0] // len(cuts)
        for index, cut in enumerate(cuts):
            result[cut] = made[index * rows_each : (index + 1) * rows_each]
    back = product_transposed(grad_mine, unfolded(down_mine, width))
    back += product_transposed(grad_other, unfolded(down_other, width))
    back = (back * slope[...]).astype(jnp.bfloat16)
    bias_grad[...] = jnp.sum(back.astype(jnp.float32), axis=0, keepdims=True)
    up_grad = product(normed[...], back).astype(jnp.bfloat16)

    @pl.when(step < TILES)
    def _():
        up_kept[...] = up_grad

    @pl.when(step >= TILES)
    def _():
        up_sent[...] = up_grad

    grad_normed[...] += product_transposed(back, weight)


def mlp_backward(side, rows, grad, small, saved, weights, places):
    active, slope = saved
    up_mine, up_other, down_mine, down_other = weights
    up_at, down_at = places
    length, features = rows.shape
    width = features // 2
    tile = width
    hidden = 2 * TILES * tile
    folded = features // (2 * TILES)
    tiled = pl.BlockSpec((length, tile), lambda step, side: (0, tile_of(step, side)))
    down_spec = pl.BlockSpec(
        (folded, TILES * width), lambda step, side: (tile_of(step, side), down_at)
    )
    up_first = pl.BlockSpec((features, tile), lambda step, side: (0, first_tile(step)))
    up_second = pl.BlockSpec((features, tile), lambda step, side: (0, second_tile(step)))
    down_out = pl.BlockSpec(
        (folded, TILES * width), lambda step, side: (tile_of(step, side), 0)
    )
    return pl.pallas_call(
        mlp_backward_kernel,
        out_shape=(
            jax.ShapeDtypeStruct((features, hidden // 2), jnp.bfloat16),
            jax.ShapeDtypeStruct((features, hidden // 2), jnp.bfloat16),
            jax.ShapeDtypeStruct((features, TILES * width), jnp.bfloat16),
            jax.ShapeDtypeStruct((features, TILES * width), jnp.bfloat16),
            jax.ShapeDtypeStruct((1, hidden), jnp.float32),
            jax.ShapeDtypeStruct((length, features), jnp.float32),
        ),
        grid_spec=pltpu.PrefetchScalarGridSpec(
            num_scalar_prefetch=1,
            grid=(2 * TILES,),
            in_specs=[
                fixed(length, features),
                fixed(length, features),
                fixed(4, features),
                tiled,
                tiled,
                pl.BlockSpec((features, tile), lambda step, side: (0, up_at + first_tile(step))),
                pl.BlockSpec((features, tile), lambda step, side: (0, up_at + second_tile(step))),
                down_spec,
                down_spec,
            ],
            out_specs=(
                up_first,
                up_second,
                down_out,
                down_out,
                pl.BlockSpec((1, tile), lambda step, side: (0, tile_of(step, side))),
                fixed(length, features),
            ),
            scratch_shapes=[pltpu.VMEM((features, length), jnp.bfloat16)],
        ),
        compiler_params=pltpu.CompilerParams(vmem_limit_bytes=vmem_bytes),
        cost_estimate=pl.CostEstimate(
            flops=8 * length * features * hidden,
            bytes_accessed=8 * features * hidden + 6 * length * hidden,
            transcendentals=0,
        ),
        name="mlp_backward",
    )(
        side, rows, grad, small["norms"], active, slope,
        up_mine, up_other, down_mine, down_other,
    )


def attn_backward_kernel(
    side, rows, grad, tables, mask, norms, qkv, logs, attended, grad_mlp, mine, other,
    kept, sent, bias_grad, sums, passed, mixed_back
):
    width = mine.shape[1] // 4
    unit, scale = unit_rows(rows[...].astype(jnp.float32))
    normed = (unit * norms[0:1] + norms[2:3]).T.astype(jnp.bfloat16)
    allowed = mask[...] > 0.5
    mixed = attended[...].T
    back = None
    for at, (weight, result) in enumerate(((mine, kept), (other, sent))):
        half = side[0] if at == 0 else 1 - side[0]
        part = grad[:, lane_half(half, width)]
        result[:, 3 * width :] = product(mixed, part).astype(jnp.bfloat16)
        term = product_transposed(part, weight[:, 3 * width :])
        back = term if back is None else back + term
    mixed_back[...] = back.astype(jnp.bfloat16)
    grad_attn = None
    for at, (weight, result) in enumerate(((mine, kept), (other, sent))):
        half = side[0] if at == 0 else 1 - side[0]
        queries = qkv[at, :, 0:width]
        keys = qkv[at, :, width : 2 * width]
        values = qkv[at, :, 2 * width :]
        keys_turned = keys.T
        grad_out = mixed_back[:, lane_half(half, width)]
        query_grads, key_grads, value_grads = [], [], []
        for pair in range(width // LANES):
            cut = slice(pair * LANES, (pair + 1) * LANES)
            key_pair, value_pair = [], []
            for which in range(2):
                head = 2 * pair + which
                scores = scores_of(keys[:, cut], queries[:, cut], which, allowed)
                chances = jnp.exp(scores - logs[at, head : head + 1, :])
                value_pair.append(product(chances.astype(jnp.bfloat16), grad_out[:, cut]))
                slopes = product_transposed(head_lanes(values[:, cut], which), grad_out[:, cut])
                inner = jnp.sum(slopes * chances, axis=0, keepdims=True)
                slopes = (chances * (slopes - inner)).astype(jnp.bfloat16)
                key_pair.append(product(slopes, queries[:, cut]))
                query_grads.append(product(keys_turned[head * HD : (head + 1) * HD], slopes))
            lane = lax.broadcasted_iota(jnp.int32, key_pair[0].shape, 1)
            key_grads.append(jnp.where(lane < HD, key_pair[0], key_pair[1]))
            value_grads.append(jnp.where(lane < HD, value_pair[0], value_pair[1]))
        factor = 1.0 / math.sqrt(HD)
        query_grad = turned(jnp.concatenate(query_grads, axis=0).T * factor, tables, True)
        key_grad = turned(jnp.concatenate(key_grads, axis=1) * factor, tables, True)
        value_grad = jnp.concatenate(value_grads, axis=1)
        for index, part in enumerate((query_grad, key_grad, value_grad)):
            cut = slice(index * width, (index + 1) * width)
            part = part.astype(jnp.bfloat16)
            bias_grad[at : at + 1, cut] = jnp.sum(
                part.astype(jnp.float32), axis=0, keepdims=True
            )
            result[:, cut] = product(normed, part).astype(jnp.bfloat16)
            term = product_transposed(part, weight[:, cut])
            grad_attn = term if grad_attn is None else grad_attn + term
    grad_up = grad_mlp[...]
    grad_rows = grad[...].astype(jnp.float32)
    sums[0:1] = jnp.sum(unit * grad_attn, axis=0, keepdims=True)
    sums[1:2] = jnp.sum(unit * grad_up, axis=0, keepdims=True)
    sums[2:3] = jnp.sum(grad_attn, axis=0, keepdims=True)
    sums[3:4] = jnp.sum(grad_up, axis=0, keepdims=True)
    sums[4:5] = jnp.sum(grad_rows, axis=0, keepdims=True)
    inward = grad_attn * norms[0:1] + grad_up * norms[1:2]
    level = jnp.mean(inward, axis=-1, keepdims=True)
    along = jnp.mean(inward * unit, axis=-1, keepdims=True)
    passed[...] = (grad_rows + (inward - level - unit * along) * scale).astype(passed.dtype)


def attn_backward(side, rows, grad, tables, mask, small, saved, grad_mlp, mine, other, kind):
    qkv, logs, attended = saved
    length, features = rows.shape
    return pl.pallas_call(
        attn_backward_kernel,
        out_shape=(
            jax.ShapeDtypeStruct((features, 2 * features), jnp.bfloat16),
            jax.ShapeDtypeStruct((features, 2 * features), jnp.bfloat16),
            jax.ShapeDtypeStruct((2, 3 * features // 2), jnp.float32),
            jax.ShapeDtypeStruct((5, features), jnp.float32),
            jax.ShapeDtypeStruct((length, features), kind),
        ),
        grid=(1,),
        in_specs=[pl.BlockSpec(memory_space=pltpu.SMEM)]
        + fixed_like(rows, grad, tables, mask, small["norms"], qkv, logs, attended, grad_mlp)
        + [fixed(features, 2 * features)] * 2,
        out_specs=(
            fixed(features, 2 * features),
            fixed(features, 2 * features),
            fixed(2, 3 * features // 2),
            fixed(5, features),
            fixed(length, features),
        ),
        scratch_shapes=[pltpu.VMEM((length, features), jnp.bfloat16)],
        compiler_params=pltpu.CompilerParams(vmem_limit_bytes=vmem_bytes),
        cost_estimate=pl.CostEstimate(
            flops=2 * length * features * features * 12,
            bytes_accessed=16 * features * features,
            transcendentals=length * length * features // HD,
        ),
        name="attn_backward",
    )(
        side, rows, grad, tables, mask, small["norms"], qkv, logs, attended, grad_mlp, mine, other
    )


SQUARE = 4
RING = 4


def swap_cores(value):
    return lax.ppermute(value, "section", [(0, 1), (1, 0)])


def swap_square(value, bit):
    count = lax.axis_size("dp")
    return lax.ppermute(value, "dp", [(i, i ^ bit) for i in range(count)])


def shift_ring(value, steps):
    count = lax.axis_size("dp")
    pairs = [(i, (i + SQUARE * steps) % count) for i in range(count)]
    return lax.ppermute(value, "dp", pairs)


def small_slice():
    return lax.axis_size("dp") == SQUARE * RING


def after(values, earlier):
    flat, shape = jax.tree.flatten(values)
    waited = jax.tree.leaves(earlier)
    tied = lax.optimization_barrier(tuple(flat) + tuple(waited))
    return jax.tree.unflatten(shape, tied[: len(flat)])


def own_place():
    place = lax.axis_index("dp").astype(jnp.int32)
    return (place // SQUARE, place % SQUARE)


def any_space(count):
    return [pl.BlockSpec(memory_space=pl.ANY)] * count


def place_kernel(spot_ref, own, first, second, far_low, far_high, out, sems):
    spot = spot_ref[0]
    half = RING // 2
    copies = [
        pltpu.make_async_copy(own, out.at[:, spot], sems.at[0]),
        pltpu.make_async_copy(first, out.at[:, spot ^ 1], sems.at[1]),
        pltpu.make_async_copy(second, out.at[:, spot ^ 2], sems.at[2]),
        pltpu.make_async_copy(far_low, out.at[pl.ds(0, half), spot ^ 3], sems.at[3]),
        pltpu.make_async_copy(far_high, out.at[pl.ds(half, half), spot ^ 3], sems.at[4]),
    ]
    for copy in copies:
        copy.start()
    for copy in copies:
        copy.wait()


def place_blocks(blocks):
    spot = own_place()[1].reshape(1)
    _, rows, columns = blocks[0].shape
    placed = pl.pallas_call(
        place_kernel,
        out_shape=jax.ShapeDtypeStruct((RING, SQUARE, rows, columns), blocks[0].dtype),
        in_specs=[pl.BlockSpec(memory_space=pltpu.SMEM)] + any_space(5),
        out_specs=pl.BlockSpec(memory_space=pltpu.VMEM),
        scratch_shapes=[pltpu.SemaphoreType.DMA((5,))],
        compiler_params=pltpu.CompilerParams(vmem_limit_bytes=vmem_bytes),
        name="place_blocks",
    )(spot, *blocks)
    return placed.reshape(RING * SQUARE * rows, columns)


def line_kernel(order_ref, *refs):
    held, out, sems = refs[:-2], refs[-2], refs[-1]
    copies = [
        pltpu.make_async_copy(part, out.at[order_ref[at]], sems.at[at])
        for at, part in enumerate(held)
    ]
    for copy in copies:
        copy.start()
    for copy in copies:
        copy.wait()


def line_placed(order, held):
    return pl.pallas_call(
        line_kernel,
        out_shape=jax.ShapeDtypeStruct((len(held),) + held[0].shape, held[0].dtype),
        in_specs=[pl.BlockSpec(memory_space=pltpu.SMEM)] + any_space(len(held)),
        out_specs=pl.BlockSpec(memory_space=pltpu.VMEM),
        scratch_shapes=[pltpu.SemaphoreType.DMA((len(held),))],
        compiler_params=pltpu.CompilerParams(vmem_limit_bytes=vmem_bytes),
        name="place_line",
    )(order, *held)


def ring_order():
    return (own_place()[0] + RING - jnp.arange(RING, dtype=jnp.int32)) % RING


def square_order():
    return own_place()[1] ^ jnp.arange(SQUARE, dtype=jnp.int32)


def gather_whole(piece):
    return lax.all_gather(piece, "dp", axis=0, tiled=True)


def ring_moved(piece):
    return [shift_ring(piece, steps) for steps in range(1, RING)]


def square_moved(piece):
    return [swap_square(piece, bit) for bit in range(1, SQUARE)]


def column_of(piece, moved):
    return line_placed(ring_order(), [piece] + moved)


def near_moved(column):
    return (swap_square(column, 1), swap_square(column, 2))


def far_moved(near):
    half = RING // 2
    return (swap_square(near[0][:half], 2), swap_square(near[1][half:], 1))


def ring_around(blocks):
    held = [blocks]
    for _ in range(RING - 1):
        held.append(shift_ring(held[-1], 1))
    return held


def gather_small(piece):
    if not small_slice():
        return gather_whole(piece)
    column = jnp.take(jnp.stack([piece] + ring_moved(piece)), ring_order(), axis=0)
    stacked = jnp.stack([column] + square_moved(column), axis=1)
    stacked = jnp.take(stacked, square_order(), axis=1)
    return stacked.reshape(RING * SQUARE * piece.shape[0], -1)


def far_kernel(place_ref, *refs):
    pairs, (low, high) = refs[:-2], refs[-2:]
    half = RING // 2
    columns = pairs[0].shape[-1]
    for at in range(0, len(pairs), 2):
        cut = slice(at // 2 * columns, (at // 2 + 1) * columns)
        total = pairs[at][...].astype(jnp.float32) + pairs[at + 1][...].astype(jnp.float32)
        total = total[:, 0].astype(low.dtype)
        low[:, :, cut] = total[:half]
        high[:, :, cut] = total[half:]


def near_kernel(place_ref, *refs):
    pairs, (far_low, far_high), (first, second) = refs[:-4], refs[-4:-2], refs[-2:]
    half = RING // 2
    columns = pairs[0].shape[-1]
    for at in range(0, len(pairs), 4):
        cut = slice(at // 4 * columns, (at // 4 + 1) * columns)
        one, two, three, four = (pair[...].astype(jnp.float32)[:, 0] for pair in pairs[at : at + 4])
        total = one + two
        first[:half, :, cut] = total[:half].astype(first.dtype)
        high = far_high[:, :, cut].astype(jnp.float32)
        first[half:, :, cut] = (total[half:] + high).astype(first.dtype)
        total = three + four
        low = far_low[:, :, cut].astype(jnp.float32)
        second[:half, :, cut] = (total[:half] + low).astype(first.dtype)
        second[half:, :, cut] = total[half:].astype(first.dtype)


def column_kernel(place_ref, *refs):
    pairs, (first, second), outs = refs[: -2 - RING], refs[-2 - RING : -RING], refs[-RING:]
    columns = pairs[0].shape[-1]
    for steps, out in enumerate(outs):
        level = lax.rem(place_ref[0] + steps, RING)
        for at in range(0, len(pairs), 2):
            cut = slice(at // 2 * columns, (at // 2 + 1) * columns)
            total = pairs[at][level, 0].astype(jnp.float32)
            total += pairs[at + 1][level, 0].astype(jnp.float32)
            total += first[level, :, cut].astype(jnp.float32)
            total += second[level, :, cut].astype(jnp.float32)
            out[:, cut] = total.astype(out.dtype)


def block_spec(rows, columns, bit):
    return pl.BlockSpec(
        (RING, 1, rows, columns), lambda step, place: (0, place[1] ^ bit, 0, 0)
    )


def scatter_call(body, name, pairs, bits, extra, outs):
    rows, columns = pairs[0].shape[0] // PARTS, pairs[0].shape[1]
    blocks, specs = [], []
    for at in range(0, len(pairs), 2):
        for bit in bits:
            for array in pairs[at : at + 2]:
                blocks.append(array.reshape(RING, SQUARE, rows, columns))
                specs.append(block_spec(rows, columns, bit))
    return pl.pallas_call(
        body,
        out_shape=tuple(outs),
        grid_spec=pltpu.PrefetchScalarGridSpec(
            num_scalar_prefetch=1,
            grid=(1,),
            in_specs=specs + fixed_like(*extra),
            out_specs=tuple(fixed_like(*outs)),
        ),
        compiler_params=pltpu.CompilerParams(vmem_limit_bytes=vmem_bytes),
        name=name,
    )(jnp.stack(own_place()), *blocks, *extra)


def wide_shape(pairs, count, kind=jnp.bfloat16):
    rows, columns = pairs[0].shape[0] // PARTS, pairs[0].shape[1] * len(pairs) // 2
    lead = (count,) if count else ()
    return jax.ShapeDtypeStruct(lead + (rows, columns), kind)


def far_blocks(pairs):
    half = wide_shape(pairs, RING // 2)
    return scatter_call(far_kernel, "far_blocks", pairs, (3,), (), [half, half])


def near_blocks(pairs, far):
    full = wide_shape(pairs, RING)
    return scatter_call(near_kernel, "near_blocks", pairs, (1, 2), far, [full, full])


def sent_both(blocks):
    return (swap_square(blocks[0], 1), swap_square(blocks[1], 2))


def column_sent(pairs, near):
    outs = [wide_shape(pairs, 0, jnp.float32)] + [wide_shape(pairs, 0)] * (RING - 1)
    own, *leaving = scatter_call(column_kernel, "column_blocks", pairs, (0,), near, outs)
    return [own] + [shift_ring(part, steps + 1) for steps, part in enumerate(leaving)]


def total_of(parts):
    total = parts[0].astype(jnp.float32)
    for part in parts[1:]:
        total = total + part.astype(jnp.float32)
    return total


def ring_steps(kept, received):
    rows, columns = kept.shape[0] // PARTS, kept.shape[1]
    kept = kept.reshape(RING, SQUARE, rows, columns)
    received = received.reshape(RING, SQUARE, rows, columns)
    level, _ = own_place()

    def rung(back):
        index = (level + RING - back) % RING
        parts = [lax.dynamic_index_in_dim(array, index, 0, False) for array in (kept, received)]
        return total_of(parts)

    moving = rung(1).astype(jnp.bfloat16)
    for step in range(1, RING):
        moved = shift_ring(moving, 1)
        yield moved
        total = moved.astype(jnp.float32) + rung(step + 1)
        moving = total.astype(jnp.bfloat16)
    yield total


def square_sent(blocks):
    _, spot = own_place()

    def block(index):
        return lax.dynamic_index_in_dim(blocks, index, 0, keepdims=False)

    moved = [
        swap_square(block(spot ^ bit).astype(jnp.bfloat16), bit) for bit in range(1, SQUARE)
    ]
    return [block(spot)] + moved


def scatter_small(kept, sent):
    summed = kept + swap_cores(sent)
    if not small_slice():
        return lax.psum_scatter(summed, "dp", scatter_dimension=0, tiled=True)
    level, spot = own_place()
    blocks = summed.reshape(RING, SQUARE, -1)

    def block(index):
        return lax.dynamic_index_in_dim(blocks, index, 1, keepdims=False)

    column = block(spot)
    for bit in range(1, SQUARE):
        column = column + swap_square(block(spot ^ bit), bit)
    total = lax.dynamic_index_in_dim(column, level, 0, keepdims=True)
    for steps in range(1, RING):
        part = lax.dynamic_index_in_dim(column, (level + steps) % RING, 0, keepdims=True)
        total = total + shift_ring(part, steps)
    return total


def folded(rows, parts):
    width = rows.shape[1]
    split = rows.reshape(parts, TILES, -1, width).transpose(0, 2, 1, 3)
    return split.reshape(-1, TILES * width)


def unfolded_rows(rows, parts):
    width = rows.shape[1] // TILES
    split = rows.reshape(parts, -1, TILES, width).transpose(0, 2, 1, 3)
    return split.reshape(-1, width)


def half_of(array, which):
    width = array.shape[1] // 2
    return lax.dynamic_slice_in_dim(array, which * width, width, 1)


def half_slots(array, which):
    length = array.shape[0] // 2
    return lax.dynamic_slice_in_dim(array, which * length, length, 0)


def ordered(is_first, mine, other):
    return (jnp.where(is_first, mine, other), jnp.where(is_first, other, mine))


def on_device(
    ends_in,
    lengths,
    qkv_weight,
    qkv_bias,
    out_weight,
    up_weight,
    up_bias,
    down_weight,
    out_biases,
    norm_gains,
    norm_biases,
):
    section_index = lax.axis_index("section")
    is_first = section_index == 0
    side = section_index.astype(jnp.int32).reshape(1)
    features = ends_in.shape[2]
    width = features // 2
    count = lax.axis_size("dp")
    own_rows = ends_in[0]
    slot_count = own_rows.shape[0] // 2
    kept_rows = half_slots(own_rows, section_index)
    other_rows = swap_cores(half_slots(own_rows, 1 - section_index))
    entry, cotangent = ordered(is_first, kept_rows, other_rows)
    segment, position = layouts(
        lax.dynamic_index_in_dim(lengths, section_index, 0, keepdims=False), slot_count
    )
    tables = rotary_tables(position)
    mask = allowed_transposed(segment)

    def both(take):
        kept = take(section_index)
        other = swap_cores(take(1 - section_index))
        return ordered(is_first, kept, other)

    def take_narrow(which):
        thirds = [
            qkv_weight[0, :, part * features : (part + 1) * features] for part in range(3)
        ]
        return jnp.concatenate([half_of(part, which) for part in thirds + [out_weight[0]]], axis=1)

    pieces = (
        both(take_narrow),
        both(lambda which: half_of(up_weight[0], which)),
        both(lambda which: half_of(down_weight[0], which)),
    )

    small_shapes = [
        (qkv_bias.shape[1],),
        (up_bias.shape[1],),
        out_biases.shape[1:],
        norm_gains.shape[1:],
        norm_biases.shape[1:],
    ]
    small_own = jnp.concatenate(
        [a[0].reshape(-1) for a in (qkv_bias, up_bias, out_biases, norm_gains, norm_biases)]
    )
    small_both = jnp.concatenate(ordered(is_first, small_own, swap_cores(small_own)))
    small_full = gather_small(small_both[None])
    small_full = small_full.reshape(count, 2, small_own.shape[0]).astype(jnp.float32)

    def small_of(layer):
        rows = small_full[:, layer]
        found = []
        at = 0
        for shape in small_shapes:
            size = math.prod(shape)
            part = rows[:, at : at + size].reshape((count,) + shape)
            at += size
            if len(shape) == 2:
                part = part.transpose(1, 0, 2).reshape(shape[0], count * shape[1])
            else:
                part = part.reshape(1, count * shape[0])
            found.append(part)
        bias_qkv, bias_up, bias_out, gains, shifts = found
        bias_qkv = bias_qkv.reshape(3, 2, width).transpose(1, 0, 2).reshape(2, 3 * width)
        return dict(
            qkv=jnp.where(is_first, bias_qkv, bias_qkv[::-1]),
            up=bias_up,
            out=bias_out,
            norms=jnp.concatenate([gains, shifts]),
        )

    small = [small_of(layer) for layer in range(2)]
    kept_forward = {}
    slabs = {}

    def attn_step(layer, rows):
        kept_forward[layer, "rows"] = rows
        made = attn_forward(side, rows, tables, mask, small[layer], *slabs[layer, "narrow"])
        kept_forward[layer, "attn"] = made
        return made

    def mlp_step(layer, kind):
        passed = kept_forward[layer, "attn"][3]
        rows = kept_forward[layer, "rows"]
        made = mlp_forward(
            side, rows, passed, small[layer], slabs[layer, "mlp"], places[layer], kind
        )
        kept_forward[layer, "mlp"] = made
        return made

    def mlp_back(layer, grad):
        rows = kept_forward[layer, "rows"]
        return mlp_backward(
            side, rows, grad, small[layer], kept_forward[layer, "mlp"][:2],
            slabs[layer, "mlp"], places[layer],
        )

    def attn_back(layer, grad, grad_mlp, kind):
        return attn_backward(
            side, kept_forward[layer, "rows"], grad, tables, mask, small[layer],
            kept_forward[layer, "attn"][:3], grad_mlp, *slabs[layer, "narrow"], kind,
        )

    def vectors_of(bias_qkv, bias_up, sums):
        bias_qkv = jnp.where(is_first, bias_qkv, bias_qkv[::-1])
        bias_qkv = bias_qkv.reshape(2, 3, width).transpose(1, 0, 2).reshape(1, 6 * width)
        double = jnp.concatenate([sums[4:5], sums[4:5]])
        return (bias_qkv, bias_up, double, sums[0:2], sums[2:4])

    places = ((0, 1), (TILES, 0))
    if small_slice():
        narrow, up, down = pieces
        lower_mlp = jnp.concatenate([up[0], folded(down[0], 1)], axis=1)
        upper_wide = jnp.concatenate([narrow[1], up[1]], axis=1)
        upper_down = folded(down[1], 1)

        ring_a = ring_moved(narrow[0])
        square_d = square_moved(upper_down)
        column_a = column_of(narrow[0], ring_a)
        near_a = near_moved(column_a)
        ring_b = ring_moved(after(lower_mlp, ring_a))
        column_b = column_of(lower_mlp, ring_b)
        far_a = far_moved(near_a)
        near_b = near_moved(column_b)
        ring_c = ring_moved(after(upper_wide, ring_b))
        whole_a = place_blocks((column_a,) + near_a + far_a)
        slabs[0, "narrow"] = (whole_a, swap_cores(whole_a))
        far_b = far_moved(near_b)
        column_c = column_of(upper_wide, ring_c)
        near_c = near_moved(after(column_c, near_b))
        blocks_d = line_placed(square_order(), [upper_down] + square_d)
        held_d = ring_around(after(blocks_d, ring_c))
        attn_rows, _ = after((entry, entry), (column_c, slabs[0, "narrow"], near_b))
        attn_step(0, attn_rows)
        whole_b = place_blocks((column_b,) + near_b + far_b)
        whole_b = after(whole_b, kept_forward[0, "attn"][3])
        swapped_b = swap_cores(whole_b)
        slabs[0, "mlp"] = (whole_b, swapped_b, whole_b, swapped_b)
        mlp_step(0, jnp.bfloat16)
        far_c = far_moved(near_c)
        whole_c = place_blocks((column_c,) + near_c + far_c)
        swapped_c = swap_cores(whole_c)
        slabs[1, "narrow"] = (whole_c, swapped_c)
        whole_d = line_placed(ring_order(), held_d).reshape(whole_a.shape)
        swapped_d = swap_cores(whole_d)
        slabs[1, "mlp"] = (whole_c, swapped_c, whole_d, swapped_d)
        attn_step(1, kept_forward[0, "mlp"][2])
        mlp_step(1, jnp.float32)
    else:
        for layer in range(2):
            narrow, up, down = (gather_whole(piece[layer]) for piece in pieces)
            down = folded(down, PARTS)
            joined = (narrow, up, down)
            if layer == 0:
                joined = (narrow, jnp.concatenate([up, down], axis=1))
            else:
                joined = (jnp.concatenate([narrow, up], axis=1), down)
            first, second = ((part, swap_cores(part)) for part in joined)
            slabs[layer, "narrow"] = first
            slabs[layer, "mlp"] = (second if layer == 0 else first) + second
        attn_step(0, entry)
        mlp_step(0, jnp.bfloat16)
        attn_step(1, kept_forward[0, "mlp"][2])
        mlp_step(1, jnp.float32)
    produced = kept_forward[1, "mlp"][2]

    def mlp_pairs(made):
        return (made[0], swap_cores(made[1]), made[2], swap_cores(made[3]))

    if small_slice():
        upper = mlp_back(1, cotangent)
        pairs_a = mlp_pairs(upper)
        upper_attn = attn_back(1, cotangent, upper[5], jnp.bfloat16)
        leaving_a = far_blocks(after(pairs_a, upper_attn[2]))
        far_a = sent_both(leaving_a)
        grad_middle, received_b = after(
            (upper_attn[4], swap_cores(upper_attn[1])), leaving_a
        )
        lower = mlp_back(0, grad_middle)
        near_a = near_blocks(pairs_a, after(far_a, lower[4]))
        steps_b = ring_steps(upper_attn[0], after(received_b, lower[4]))
        moved_b = next(steps_b)
        pairs_c = mlp_pairs(lower)
        grad_mlp = after(lower[5], near_a)
        near_a = sent_both(near_a)
        lower_attn = attn_back(0, grad_middle, grad_mlp, jnp.float32)
        pairs_c = after(pairs_c, (lower_attn[2], near_a, moved_b))
        far_c = sent_both(far_blocks(pairs_c))
        pairs_d = (lower_attn[0], swap_cores(lower_attn[1]))
        moved_b = next(steps_b)
        far_d = sent_both(far_blocks(after(pairs_d, moved_b)))
        parts_a = column_sent(pairs_a, near_a)
        near_c = sent_both(near_blocks(pairs_c, far_c))
        moved_b = next(steps_b)
        blocks_b = next(steps_b)
        parts_b = square_sent(blocks_b)
        near_d = sent_both(near_blocks(pairs_d, far_d))
        parts_c = column_sent(pairs_c, near_c)
        parts_d = column_sent(pairs_d, near_d)
        reduced = (
            (total_of(parts_d), total_of(parts_b)),
            (total_of(parts_c), total_of(parts_a)),
        )
    else:
        upper = mlp_back(1, cotangent)
        upper_attn = attn_back(1, cotangent, upper[5], jnp.bfloat16)
        lower = mlp_back(0, upper_attn[4])
        lower_attn = attn_back(0, upper_attn[4], lower[5], jnp.float32)

        def spread(kept, received):
            summed = kept.astype(jnp.float32) + received.astype(jnp.float32)
            return lax.psum_scatter(summed, "dp", scatter_dimension=0, tiled=True)

        def spread_mlp(made):
            up_kept, up_got, down_kept, down_got = mlp_pairs(made)
            down = spread(unfolded_rows(down_kept, PARTS), unfolded_rows(down_got, PARTS))
            return jnp.concatenate([spread(up_kept, up_got), folded(down, 1)], axis=1)

        reduced = (
            tuple(spread(made[0], swap_cores(made[1])) for made in (lower_attn, upper_attn)),
            tuple(spread_mlp(made) for made in (lower, upper)),
        )
    grad_entry = lower_attn[4]
    vectors_upper = vectors_of(upper_attn[2], upper[4], upper_attn[3])
    vectors_lower = vectors_of(lower_attn[2], lower[4], lower_attn[3])

    def finish(lower, upper):
        mine, leaving = ordered(is_first, lower, upper)
        return ordered(is_first, mine, swap_cores(leaving))

    narrow_halves, mlp_halves = (finish(*pair) for pair in reduced)
    up_width = up_weight.shape[2] // 2
    total_up = jnp.concatenate([part[:, :up_width] for part in mlp_halves], axis=1)
    total_down = jnp.concatenate(
        [unfolded_rows(part[:, up_width:], 1) for part in mlp_halves], axis=1
    )
    total_qkv = jnp.concatenate(
        [
            part[:, at * width : (at + 1) * width]
            for at in range(3)
            for part in narrow_halves
        ],
        axis=1,
    )
    total_out = jnp.concatenate([part[:, 3 * width :] for part in narrow_halves], axis=1)

    def small_rows(vectors):
        parts = []
        for grad in vectors:
            part = grad.reshape(grad.shape[0], count, -1).transpose(1, 0, 2)
            parts.append(part.reshape(count, -1))
        return jnp.concatenate(parts, axis=1)

    small_kept, small_sent = ordered(
        is_first, small_rows(vectors_lower), small_rows(vectors_upper)
    )
    small_total = scatter_small(small_kept, small_sent)[0]
    small_outs = []
    at = 0
    for shape in small_shapes:
        size = math.prod(shape)
        small_outs.append(small_total[at : at + size].reshape((1,) + shape))
        at += size

    staying, leaving = ordered(is_first, grad_entry, produced)
    ends_out = jnp.concatenate(ordered(is_first, staying, swap_cores(leaving)))
    return (
        ends_out[None],
        total_qkv[None],
        small_outs[0],
        total_out[None],
        total_up[None],
        small_outs[1],
        total_down[None],
        small_outs[2],
        small_outs[3],
        small_outs[4],
    )


def solution(mesh):
    return jax.shard_map(
        on_device,
        mesh=mesh,
        in_specs=(
            P("section", "dp", None),
            P("dp", None),
            P("section", "dp", None),
            P("section", "dp"),
            P("section", "dp", None),
            P("section", "dp", None),
            P("section", "dp"),
            P("section", "dp", None),
            P("section", None, "dp"),
            P("section", None, "dp"),
            P("section", None, "dp"),
        ),
        out_specs=(
            P("section", "dp", None),
            P("section", "dp", None),
            P("section", "dp"),
            P("section", "dp", None),
            P("section", "dp", None),
            P("section", "dp"),
            P("section", "dp", None),
            P("section", None, "dp"),
            P("section", None, "dp"),
            P("section", None, "dp"),
        ),
        check_vma=False,
    )
```

```python
import math

import jax
import jax.numpy as jnp
import numpy as np
from jax import lax
from jax.experimental import pallas as pl
from jax.experimental.pallas import tpu as pltpu
from jax.sharding import PartitionSpec as P

HD = 64
ROT = 16
LANES = 128
TILES = 4
PARTS = 16


eps = 1e-05
masked_score = -1e30
vmem_bytes = 48 * 1024 * 1024


def product(left, right):
    return jnp.dot(left, right, preferred_element_type=jnp.float32)


def product_transposed(left, right):
    return lax.dot_general(
        left, right, (((1,), (1,)), ((), ())), preferred_element_type=jnp.float32
    )


def layouts(lengths, slot_count):
    ends_at = jnp.cumsum(lengths)
    indices = jnp.arange(slot_count, dtype=jnp.int32)
    passed = indices[:, None] >= ends_at[None, :]
    segments = jnp.sum(passed.astype(jnp.int32), axis=1)
    starts = jnp.sum(jnp.where(passed, lengths[None, :], 0), axis=1)
    return (segments, indices - starts)


def rotary_tables(positions):
    lane = jnp.arange(LANES, dtype=jnp.int32) % HD
    half = ROT // 2
    freqs = 10000.0 ** (-2.0 * (lane % half).astype(jnp.float32) / ROT)
    angles = positions.astype(jnp.float32)[:, None] * freqs[None, :]
    cosine = jnp.where(lane < ROT, jnp.cos(angles), 1.0)
    sine = jnp.sin(angles)
    ahead = jnp.where(lane < half, -sine, 0.0)
    behind = jnp.where((lane >= half) & (lane < ROT), sine, 0.0)
    return jnp.stack([cosine, ahead, behind])


def allowed_transposed(segment):
    indices = jnp.arange(segment.shape[0], dtype=jnp.int32)
    allowed = (segment[:, None] == segment[None, :]) & (indices[:, None] <= indices[None, :])
    return allowed.astype(jnp.float32)


def turned(values, tables, back):
    half = ROT // 2
    parts = []
    for at in range(0, values.shape[1], LANES):
        part = values[:, at : at + LANES]
        moved = (
            pltpu.roll(part, LANES - half, 1) * tables[1] + pltpu.roll(part, half, 1) * tables[2]
        )
        kept = part * tables[0]
        parts.append(kept - moved if back else kept + moved)
    return jnp.concatenate(parts, axis=1)


def unit_rows(rows):
    centred = rows - jnp.mean(rows, axis=-1, keepdims=True)
    spread = jnp.mean(centred * centred, axis=-1, keepdims=True)
    scale = lax.rsqrt(spread + eps)
    return (centred * scale, scale)


def lane_half(which, width):
    return pl.ds(pl.multiple_of(which * width, LANES), width)


def head_lanes(values, which):
    lane = lax.broadcasted_iota(jnp.int32, values.shape, 1)
    return jnp.where((lane < HD) == (which == 0), values, jnp.zeros_like(values))


def scores_of(key_pair, query_pair, which, allowed):
    scores = product_transposed(head_lanes(key_pair, which), query_pair) * (1.0 / math.sqrt(HD))
    return jnp.where(allowed, scores, masked_score)


def attn_forward_kernel(
    side, rows, tables, mask, norms, bias_qkv, bias_out, mine, other, qkv, logs, attended, passed
):
    width = mine.shape[1] // 4
    entry = rows[...].astype(jnp.float32)
    unit, _ = unit_rows(entry)
    normed = (unit * norms[0:1] + norms[2:3]).astype(jnp.bfloat16)
    allowed = mask[...] > 0.5
    for at, weight in enumerate((mine, other)):
        half = side[0] if at == 0 else 1 - side[0]
        parts = []
        for part in range(3):
            cut = slice(part * width, (part + 1) * width)
            value = product(normed, weight[:, cut]) + bias_qkv[at : at + 1, cut]
            if part < 2:
                value = turned(value, tables, False)
            value = value.astype(jnp.bfloat16)
            qkv[at, :, cut] = value
            parts.append(value)
        queries, keys, values = parts
        values = values.T
        outs = []
        for pair in range(width // LANES):
            cut = slice(pair * LANES, (pair + 1) * LANES)
            for which in range(2):
                head = 2 * pair + which
                scores = scores_of(keys[:, cut], queries[:, cut], which, allowed)
                peak = jnp.max(scores, axis=0, keepdims=True)
                raised = jnp.exp(scores - peak)
                total = jnp.sum(raised, axis=0, keepdims=True)
                chances = (raised * (1.0 / total)).astype(jnp.bfloat16)
                outs.append(product(values[head * HD : (head + 1) * HD], chances))
                logs[at, head : head + 1, :] = peak + jnp.log(total)
        mixed = jnp.concatenate(outs, axis=0).T.astype(jnp.bfloat16)
        attended[:, lane_half(half, width)] = mixed
    mixed = attended[...]
    for at, weight in enumerate((mine, other)):
        half = side[0] if at == 0 else 1 - side[0]
        lanes = lane_half(half, width)
        passed[:, lanes] = (
            rows[:, lanes].astype(jnp.float32)
            + product(mixed, weight[:, 3 * width :])
            + bias_out[0:1, lanes]
        )


def fixed(*shape):
    return pl.BlockSpec(shape, lambda *at: (0,) * len(shape))


def fixed_like(*arrays):
    return [fixed(*array.shape) for array in arrays]


def attn_forward(side, rows, tables, mask, small, mine, other):
    length, features = rows.shape
    width = features // 2
    heads = width // HD
    return pl.pallas_call(
        attn_forward_kernel,
        out_shape=(
            jax.ShapeDtypeStruct((2, length, 3 * width), jnp.bfloat16),
            jax.ShapeDtypeStruct((2, heads, length), jnp.float32),
            jax.ShapeDtypeStruct((length, features), jnp.bfloat16),
            jax.ShapeDtypeStruct((length, features), jnp.float32),
        ),
        grid=(1,),
        in_specs=[pl.BlockSpec(memory_space=pltpu.SMEM)]
        + fixed_like(rows, tables, mask, small["norms"], small["qkv"], small["out"])
        + [fixed(features, 4 * width)] * 2,
        out_specs=(
            fixed(2, length, 3 * width),
            fixed(2, heads, length),
            fixed(length, features),
            fixed(length, features),
        ),
        compiler_params=pltpu.CompilerParams(vmem_limit_bytes=vmem_bytes),
        cost_estimate=pl.CostEstimate(
            flops=2 * length * features * features * 30,
            bytes_accessed=8 * features * features,
            transcendentals=length * length * features // HD,
        ),
        name="attn_forward",
    )(side, rows, tables, mask, small["norms"], small["qkv"], small["out"], mine, other)


def tile_of(step, side):
    half = jnp.where(step < TILES, side[0], 1 - side[0])
    return half * TILES + step % TILES


def first_tile(step):
    return jnp.minimum(step, TILES - 1)


def second_tile(step):
    return jnp.maximum(step - TILES, 0)


def folded_cuts(shape, width):
    rows = shape[0] // 2
    for part in range(2):
        for column in range(shape[1] // width):
            yield (
                slice(part * rows, (part + 1) * rows),
                slice(column * width, (column + 1) * width),
            )


def unfolded(block, width):
    return jnp.concatenate([block[cut] for cut in folded_cuts(block.shape, width)], axis=0)


def mlp_forward_kernel(
    side, rows, passed, norms, bias_up, bias_out, up_mine, up_other, down_mine, down_other,
    active, slope, produced, normed, sum_mine, sum_other
):
    step = pl.program_id(0)

    @pl.when(step == 0)
    def _():
        unit, _ = unit_rows(rows[...].astype(jnp.float32))
        normed[...] = (unit * norms[1:2] + norms[3:4]).astype(jnp.bfloat16)
        sum_mine[...] = jnp.zeros_like(sum_mine)
        sum_other[...] = jnp.zeros_like(sum_other)

    weight = jnp.where(step < TILES, up_mine[...], up_other[...])
    hidden = product(normed[...], weight) + bias_up[...]
    bell = 0.5 * (1.0 + lax.erf(hidden * (1.0 / math.sqrt(2.0))))
    density = jnp.exp(-0.5 * hidden * hidden) * (1.0 / math.sqrt(2.0 * math.pi))
    slope[...] = bell + hidden * density
    lit = (hidden * bell).astype(jnp.bfloat16)
    active[...] = lit
    width = sum_mine.shape[1]
    sum_mine[...] += product(lit, unfolded(down_mine, width))
    sum_other[...] += product(lit, unfolded(down_other, width))

    @pl.when(step == 2 * TILES - 1)
    def _():
        for half, total in ((side[0], sum_mine), (1 - side[0], sum_other)):
            lanes = lane_half(half, width)
            produced[:, lanes] = (
                passed[:, lanes] + total[...] + bias_out[1:2, lanes]
            ).astype(produced.dtype)


def mlp_forward(side, rows, passed, small, weights, places, kind):
    up_mine, up_other, down_mine, down_other = weights
    up_at, down_at = places
    length, features = rows.shape
    width = features // 2
    tile = width
    hidden = 2 * TILES * tile
    folded = features // (2 * TILES)
    tiled = pl.BlockSpec((length, tile), lambda step, side: (0, tile_of(step, side)))
    down_spec = pl.BlockSpec(
        (folded, TILES * width), lambda step, side: (tile_of(step, side), down_at)
    )
    return pl.pallas_call(
        mlp_forward_kernel,
        out_shape=(
            jax.ShapeDtypeStruct((length, hidden), jnp.bfloat16),
            jax.ShapeDtypeStruct((length, hidden), jnp.float32),
            jax.ShapeDtypeStruct((length, features), kind),
        ),
        grid_spec=pltpu.PrefetchScalarGridSpec(
            num_scalar_prefetch=1,
            grid=(2 * TILES,),
            in_specs=[
                fixed(length, features),
                fixed(length, features),
                fixed(4, features),
                pl.BlockSpec((1, tile), lambda step, side: (0, tile_of(step, side))),
                fixed(2, features),
                pl.BlockSpec((features, tile), lambda step, side: (0, up_at + first_tile(step))),
                pl.BlockSpec((features, tile), lambda step, side: (0, up_at + second_tile(step))),
                down_spec,
                down_spec,
            ],
            out_specs=(tiled, tiled, fixed(length, features)),
            scratch_shapes=[
                pltpu.VMEM((length, features), jnp.bfloat16),
                pltpu.VMEM((length, width), jnp.float32),
                pltpu.VMEM((length, width), jnp.float32),
            ],
        ),
        compiler_params=pltpu.CompilerParams(vmem_limit_bytes=vmem_bytes),
        cost_estimate=pl.CostEstimate(
            flops=20 * length * features * hidden,
            bytes_accessed=4 * features * hidden + 6 * length * hidden,
            transcendentals=2 * length * hidden,
        ),
        name="mlp_forward",
    )(
        side, rows, passed, small["norms"], small["up"], small["out"],
        up_mine, up_other, down_mine, down_other,
    )


def mlp_backward_kernel(
    side, rows, grad, norms, active, slope, up_mine, up_other, down_mine, down_other,
    up_kept, up_sent, down_kept, down_sent, bias_grad, grad_normed, normed
):
    step = pl.program_id(0)
    width = grad.shape[1] // 2
    cuts = list(folded_cuts(down_mine.shape, width))

    @pl.when(step == 0)
    def _():
        unit, _ = unit_rows(rows[...].astype(jnp.float32))
        normed[...] = (unit * norms[1:2] + norms[3:4]).T.astype(jnp.bfloat16)
        grad_normed[...] = jnp.zeros_like(grad_normed)

    grad_mine = grad[:, lane_half(side[0], width)]
    grad_other = grad[:, lane_half(1 - side[0], width)]
    weight = jnp.where(step < TILES, up_mine[...], up_other[...])
    lit = active[...].T
    for grad_half, result in ((grad_mine, down_kept), (grad_other, down_sent)):
        made = product(lit, grad_half).astype(jnp.bfloat16)
        rows_each = made.shape[0] // len(cuts)
        for index, cut in enumerate(cuts):
            result[cut] = made[index * rows_each : (index + 1) * rows_each]
    back = product_transposed(grad_mine, unfolded(down_mine, width))
    back += product_transposed(grad_other, unfolded(down_other, width))
    back = (back * slope[...]).astype(jnp.bfloat16)
    bias_grad[...] = jnp.sum(back.astype(jnp.float32), axis=0, keepdims=True)
    up_grad = product(normed[...], back).astype(jnp.bfloat16)

    @pl.when(step < TILES)
    def _():
        up_kept[...] = up_grad

    @pl.when(step >= TILES)
    def _():
        up_sent[...] = up_grad

    grad_normed[...] += product_transposed(back, weight)


def mlp_backward(side, rows, grad, small, saved, weights, places):
    active, slope = saved
    up_mine, up_other, down_mine, down_other = weights
    up_at, down_at = places
    length, features = rows.shape
    width = features // 2
    tile = width
    hidden = 2 * TILES * tile
    folded = features // (2 * TILES)
    tiled = pl.BlockSpec((length, tile), lambda step, side: (0, tile_of(step, side)))
    down_spec = pl.BlockSpec(
        (folded, TILES * width), lambda step, side: (tile_of(step, side), down_at)
    )
    up_first = pl.BlockSpec((features, tile), lambda step, side: (0, first_tile(step)))
    up_second = pl.BlockSpec((features, tile), lambda step, side: (0, second_tile(step)))
    down_out = pl.BlockSpec(
        (folded, TILES * width), lambda step, side: (tile_of(step, side), 0)
    )
    return pl.pallas_call(
        mlp_backward_kernel,
        out_shape=(
            jax.ShapeDtypeStruct((features, hidden // 2), jnp.bfloat16),
            jax.ShapeDtypeStruct((features, hidden // 2), jnp.bfloat16),
            jax.ShapeDtypeStruct((features, TILES * width), jnp.bfloat16),
            jax.ShapeDtypeStruct((features, TILES * width), jnp.bfloat16),
            jax.ShapeDtypeStruct((1, hidden), jnp.float32),
            jax.ShapeDtypeStruct((length, features), jnp.float32),
        ),
        grid_spec=pltpu.PrefetchScalarGridSpec(
            num_scalar_prefetch=1,
            grid=(2 * TILES,),
            in_specs=[
                fixed(length, features),
                fixed(length, features),
                fixed(4, features),
                tiled,
                tiled,
                pl.BlockSpec((features, tile), lambda step, side: (0, up_at + first_tile(step))),
                pl.BlockSpec((features, tile), lambda step, side: (0, up_at + second_tile(step))),
                down_spec,
                down_spec,
            ],
            out_specs=(
                up_first,
                up_second,
                down_out,
                down_out,
                pl.BlockSpec((1, tile), lambda step, side: (0, tile_of(step, side))),
                fixed(length, features),
            ),
            scratch_shapes=[pltpu.VMEM((features, length), jnp.bfloat16)],
        ),
        compiler_params=pltpu.CompilerParams(vmem_limit_bytes=vmem_bytes),
        cost_estimate=pl.CostEstimate(
            flops=32 * length * features * hidden,
            bytes_accessed=8 * features * hidden + 6 * length * hidden,
            transcendentals=0,
        ),
        name="mlp_backward",
    )(
        side, rows, grad, small["norms"], active, slope,
        up_mine, up_other, down_mine, down_other,
    )


def attn_backward_kernel(
    side, rows, grad, tables, mask, norms, qkv, logs, attended, grad_mlp, mine, other,
    kept, sent, bias_grad, sums, passed, mixed_back
):
    width = mine.shape[1] // 4
    unit, scale = unit_rows(rows[...].astype(jnp.float32))
    normed = (unit * norms[0:1] + norms[2:3]).T.astype(jnp.bfloat16)
    allowed = mask[...] > 0.5
    mixed = attended[...].T
    back = None
    for at, (weight, result) in enumerate(((mine, kept), (other, sent))):
        half = side[0] if at == 0 else 1 - side[0]
        part = grad[:, lane_half(half, width)]
        result[:, 3 * width :] = product(mixed, part).astype(jnp.bfloat16)
        term = product_transposed(part, weight[:, 3 * width :])
        back = term if back is None else back + term
    mixed_back[...] = back.astype(jnp.bfloat16)
    grad_attn = None
    for at, (weight, result) in enumerate(((mine, kept), (other, sent))):
        half = side[0] if at == 0 else 1 - side[0]
        queries = qkv[at, :, 0:width]
        keys = qkv[at, :, width : 2 * width]
        values = qkv[at, :, 2 * width :]
        keys_turned = keys.T
        grad_out = mixed_back[:, lane_half(half, width)]
        query_grads, key_grads, value_grads = [], [], []
        for pair in range(width // LANES):
            cut = slice(pair * LANES, (pair + 1) * LANES)
            key_pair, value_pair = [], []
            for which in range(2):
                head = 2 * pair + which
                scores = scores_of(keys[:, cut], queries[:, cut], which, allowed)
                chances = jnp.exp(scores - logs[at, head : head + 1, :])
                value_pair.append(product(chances.astype(jnp.bfloat16), grad_out[:, cut]))
                slopes = product_transposed(head_lanes(values[:, cut], which), grad_out[:, cut])
                inner = jnp.sum(slopes * chances, axis=0, keepdims=True)
                slopes = (chances * (slopes - inner)).astype(jnp.bfloat16)
                key_pair.append(product(slopes, queries[:, cut]))
                query_grads.append(product(keys_turned[head * HD : (head + 1) * HD], slopes))
            lane = lax.broadcasted_iota(jnp.int32, key_pair[0].shape, 1)
            key_grads.append(jnp.where(lane < HD, key_pair[0], key_pair[1]))
            value_grads.append(jnp.where(lane < HD, value_pair[0], value_pair[1]))
        factor = 1.0 / math.sqrt(HD)
        query_grad = turned(jnp.concatenate(query_grads, axis=0).T * factor, tables, True)
        key_grad = turned(jnp.concatenate(key_grads, axis=1) * factor, tables, True)
        value_grad = jnp.concatenate(value_grads, axis=1)
        for index, part in enumerate((query_grad, key_grad, value_grad)):
            cut = slice(index * width, (index + 1) * width)
            part = part.astype(jnp.bfloat16)
            bias_grad[pl.ds(half, 1), cut] = jnp.sum(
                part.astype(jnp.float32), axis=0, keepdims=True
            )
            result[:, cut] = product(normed, part).astype(jnp.bfloat16)
            term = product_transposed(part, weight[:, cut])
            grad_attn = term if grad_attn is None else grad_attn + term
    grad_up = grad_mlp[...]
    grad_rows = grad[...].astype(jnp.float32)
    sums[0:1] = jnp.sum(unit * grad_attn, axis=0, keepdims=True)
    sums[1:2] = jnp.sum(unit * grad_up, axis=0, keepdims=True)
    sums[2:3] = jnp.sum(grad_attn, axis=0, keepdims=True)
    sums[3:4] = jnp.sum(grad_up, axis=0, keepdims=True)
    sums[4:5] = jnp.sum(grad_rows, axis=0, keepdims=True)
    inward = grad_attn * norms[0:1] + grad_up * norms[1:2]
    level = jnp.mean(inward, axis=-1, keepdims=True)
    along = jnp.mean(inward * unit, axis=-1, keepdims=True)
    passed[...] = (grad_rows + (inward - level - unit * along) * scale).astype(passed.dtype)


def attn_backward(side, rows, grad, tables, mask, small, saved, grad_mlp, mine, other, kind):
    qkv, logs, attended = saved
    length, features = rows.shape
    return pl.pallas_call(
        attn_backward_kernel,
        out_shape=(
            jax.ShapeDtypeStruct((features, 2 * features), jnp.bfloat16),
            jax.ShapeDtypeStruct((features, 2 * features), jnp.bfloat16),
            jax.ShapeDtypeStruct((2, 3 * features // 2), jnp.float32),
            jax.ShapeDtypeStruct((5, features), jnp.float32),
            jax.ShapeDtypeStruct((length, features), kind),
        ),
        grid=(1,),
        in_specs=[pl.BlockSpec(memory_space=pltpu.SMEM)]
        + fixed_like(rows, grad, tables, mask, small["norms"], qkv, logs, attended, grad_mlp)
        + [fixed(features, 2 * features)] * 2,
        out_specs=(
            fixed(features, 2 * features),
            fixed(features, 2 * features),
            fixed(2, 3 * features // 2),
            fixed(5, features),
            fixed(length, features),
        ),
        scratch_shapes=[pltpu.VMEM((length, features), jnp.bfloat16)],
        compiler_params=pltpu.CompilerParams(vmem_limit_bytes=vmem_bytes),
        cost_estimate=pl.CostEstimate(
            flops=2 * length * features * features * 48,
            bytes_accessed=16 * features * features,
            transcendentals=length * length * features // HD,
        ),
        name="attn_backward",
    )(
        side, rows, grad, tables, mask, small["norms"], qkv, logs, attended, grad_mlp, mine, other
    )


SQUARE = 4
RING = 4


def swap_cores(value):
    return lax.ppermute(value, "section", [(0, 1), (1, 0)])


def swap_square(value, bit):
    count = lax.axis_size("dp")
    return lax.ppermute(value, "dp", [(i, i ^ bit) for i in range(count)])


def shift_ring(value, steps):
    count = lax.axis_size("dp")
    pairs = [(i, (i + SQUARE * steps) % count) for i in range(count)]
    return lax.ppermute(value, "dp", pairs)


def small_slice():
    return lax.axis_size("dp") == SQUARE * RING


def after(values, earlier):
    flat, shape = jax.tree.flatten(values)
    waited = jax.tree.leaves(earlier)
    tied = lax.optimization_barrier(tuple(flat) + tuple(waited))
    return jax.tree.unflatten(shape, tied[: len(flat)])


def own_place():
    place = lax.axis_index("dp").astype(jnp.int32)
    return (place // SQUARE, place % SQUARE)


def any_space(count):
    return [pl.BlockSpec(memory_space=pl.ANY)] * count


def place_kernel(spot_ref, own, first, second, far_low, far_high, out, sems):
    spot = spot_ref[0]
    half = RING // 2
    copies = [
        pltpu.make_async_copy(own, out.at[:, spot], sems.at[0]),
        pltpu.make_async_copy(first, out.at[:, spot ^ 1], sems.at[1]),
        pltpu.make_async_copy(second, out.at[:, spot ^ 2], sems.at[2]),
        pltpu.make_async_copy(far_low, out.at[pl.ds(0, half), spot ^ 3], sems.at[3]),
        pltpu.make_async_copy(far_high, out.at[pl.ds(half, half), spot ^ 3], sems.at[4]),
    ]
    for copy in copies:
        copy.start()
    for copy in copies:
        copy.wait()


def place_blocks(blocks):
    spot = own_place()[1].reshape(1)
    _, rows, columns = blocks[0].shape
    placed = pl.pallas_call(
        place_kernel,
        out_shape=jax.ShapeDtypeStruct((RING, SQUARE, rows, columns), blocks[0].dtype),
        in_specs=[pl.BlockSpec(memory_space=pltpu.SMEM)] + any_space(5),
        out_specs=pl.BlockSpec(memory_space=pltpu.VMEM),
        scratch_shapes=[pltpu.SemaphoreType.DMA((5,))],
        compiler_params=pltpu.CompilerParams(vmem_limit_bytes=vmem_bytes),
        name="place_blocks",
    )(spot, *blocks)
    return placed.reshape(RING * SQUARE * rows, columns)


def line_kernel(order_ref, *refs):
    held, out, sems = refs[:-2], refs[-2], refs[-1]
    copies = [
        pltpu.make_async_copy(part, out.at[order_ref[at]], sems.at[at])
        for at, part in enumerate(held)
    ]
    for copy in copies:
        copy.start()
    for copy in copies:
        copy.wait()


def line_placed(order, held):
    return pl.pallas_call(
        line_kernel,
        out_shape=jax.ShapeDtypeStruct((len(held),) + held[0].shape, held[0].dtype),
        in_specs=[pl.BlockSpec(memory_space=pltpu.SMEM)] + any_space(len(held)),
        out_specs=pl.BlockSpec(memory_space=pltpu.VMEM),
        scratch_shapes=[pltpu.SemaphoreType.DMA((len(held),))],
        compiler_params=pltpu.CompilerParams(vmem_limit_bytes=vmem_bytes),
        name="place_line",
    )(order, *held)


def ring_order():
    return (own_place()[0] + RING - jnp.arange(RING, dtype=jnp.int32)) % RING


def square_order():
    return own_place()[1] ^ jnp.arange(SQUARE, dtype=jnp.int32)


def gather_whole(piece):
    return lax.all_gather(piece, "dp", axis=0, tiled=True)


def ring_moved(piece):
    return [shift_ring(piece, steps) for steps in range(1, RING)]


def square_moved(piece):
    return [swap_square(piece, bit) for bit in range(1, SQUARE)]


def column_of(piece, moved):
    return line_placed(ring_order(), [piece] + moved)


def near_moved(column):
    return (swap_square(column, 1), swap_square(column, 2))


def cut_near(near):
    half = RING // 2
    return (near[0][:half], near[1][half:])


def far_moved(lows):
    return (swap_square(lows[0], 2), swap_square(lows[1], 1))


def ring_around(blocks):
    held = [blocks]
    for _ in range(RING - 1):
        held.append(shift_ring(held[-1], 1))
    return held


def spread_kernel(side, rows, *refs):
    picks, outs = refs[:6], refs[6:]
    count = rows.shape[0]
    width = outs[0].shape[2] // 3
    size = rows.shape[1] // 2

    def row(at, which):
        pick, keep = picks[2 * which], picks[2 * which + 1]
        found = product(rows[:, at : at + pick.shape[0]], pick[...])
        return jnp.sum(found * keep[...], axis=0, keepdims=True)

    for layer in range(2):
        at = layer * size
        found = row(at, 0)
        for half in range(2):
            parts = [
                found[:, (2 * part + half) * width : (2 * part + half + 1) * width]
                for part in range(3)
            ]
            outs[0][layer, pl.ds(half ^ side[0], 1), :] = jnp.concatenate(parts, axis=1)
        at += picks[0].shape[0]
        outs[1][layer] = row(at, 1)
        at += picks[2].shape[0]
        step = picks[4].shape[0]
        for index in range(2):
            outs[2][layer, index : index + 1, :] = row(at + index * step, 2)
        for index in range(4):
            outs[3][layer, index : index + 1, :] = row(at + (2 + index) * step, 2)


def spread_small(side, rows, shards, features):
    count = rows.shape[0]
    picks = []
    for shard in shards:
        lane = np.arange(count * shard)
        picks.append(jnp.asarray(np.arange(shard)[:, None] == lane % shard, jnp.bfloat16))
        picks.append(jnp.asarray(np.arange(count)[:, None] == lane // shard, jnp.float32))
    shapes = (
        (2, 2, 3 * features // 2),
        (2, 1, count * shards[1]),
        (2, 2, features),
        (2, 4, features),
    )
    outs = [jax.ShapeDtypeStruct(shape, jnp.float32) for shape in shapes]
    return pl.pallas_call(
        spread_kernel,
        out_shape=tuple(outs),
        grid=(1,),
        in_specs=[pl.BlockSpec(memory_space=pltpu.SMEM)] + fixed_like(rows, *picks),
        out_specs=tuple(fixed_like(*outs)),
        compiler_params=pltpu.CompilerParams(vmem_limit_bytes=vmem_bytes),
        name="spread_small",
    )(side, rows, *picks)


def far_kernel(place_ref, *refs):
    pairs, (low, high) = refs[:-2], refs[-2:]
    half = RING // 2
    columns = pairs[0].shape[-1]
    for at in range(0, len(pairs), 2):
        cut = slice(at // 2 * columns, (at // 2 + 1) * columns)
        total = pairs[at][...].astype(jnp.float32) + pairs[at + 1][...].astype(jnp.float32)
        total = total[:, 0].astype(low.dtype)
        low[:, :, cut] = total[:half]
        high[:, :, cut] = total[half:]


def near_kernel(place_ref, *refs):
    pairs, (far_low, far_high), (first, second) = refs[:-4], refs[-4:-2], refs[-2:]
    half = RING // 2
    columns = pairs[0].shape[-1]
    for at in range(0, len(pairs), 4):
        cut = slice(at // 4 * columns, (at // 4 + 1) * columns)
        one, two, three, four = (pair[...].astype(jnp.float32)[:, 0] for pair in pairs[at : at + 4])
        total = one + two
        first[:half, :, cut] = total[:half].astype(first.dtype)
        high = far_high[:, :, cut].astype(jnp.float32)
        first[half:, :, cut] = (total[half:] + high).astype(first.dtype)
        total = three + four
        low = far_low[:, :, cut].astype(jnp.float32)
        second[:half, :, cut] = (total[:half] + low).astype(first.dtype)
        second[half:, :, cut] = total[half:].astype(first.dtype)


def column_kernel(place_ref, *refs):
    pairs, (first, second), outs = refs[: -2 - RING], refs[-2 - RING : -RING], refs[-RING:]
    columns = pairs[0].shape[-1]
    for steps, out in enumerate(outs):
        level = lax.rem(place_ref[0] + steps, RING)
        for at in range(0, len(pairs), 2):
            cut = slice(at // 2 * columns, (at // 2 + 1) * columns)
            total = pairs[at][level, 0].astype(jnp.float32)
            total += pairs[at + 1][level, 0].astype(jnp.float32)
            total += first[level, :, cut].astype(jnp.float32)
            total += second[level, :, cut].astype(jnp.float32)
            out[:, cut] = total.astype(out.dtype)


def block_spec(rows, columns, bit):
    return pl.BlockSpec(
        (RING, 1, rows, columns), lambda step, place: (0, place[1] ^ bit, 0, 0)
    )


def scatter_call(body, name, pairs, bits, extra, outs):
    rows, columns = pairs[0].shape[0] // PARTS, pairs[0].shape[1]
    blocks, specs = [], []
    for at in range(0, len(pairs), 2):
        for bit in bits:
            for array in pairs[at : at + 2]:
                blocks.append(array.reshape(RING, SQUARE, rows, columns))
                specs.append(block_spec(rows, columns, bit))
    return pl.pallas_call(
        body,
        out_shape=tuple(outs),
        grid_spec=pltpu.PrefetchScalarGridSpec(
            num_scalar_prefetch=1,
            grid=(1,),
            in_specs=specs + fixed_like(*extra),
            out_specs=tuple(fixed_like(*outs)),
        ),
        compiler_params=pltpu.CompilerParams(vmem_limit_bytes=vmem_bytes),
        name=name,
    )(jnp.stack(own_place()), *blocks, *extra)


def wide_shape(pairs, count, kind=jnp.bfloat16):
    rows, columns = pairs[0].shape[0] // PARTS, pairs[0].shape[1] * len(pairs) // 2
    lead = (count,) if count else ()
    return jax.ShapeDtypeStruct(lead + (rows, columns), kind)


def far_blocks(pairs):
    half = wide_shape(pairs, RING // 2)
    return scatter_call(far_kernel, "far_blocks", pairs, (3,), (), [half, half])


def near_blocks(pairs, far):
    full = wide_shape(pairs, RING)
    return scatter_call(near_kernel, "near_blocks", pairs, (1, 2), far, [full, full])


def sent_both(blocks):
    return (swap_square(blocks[0], 1), swap_square(blocks[1], 2))


def column_sent(pairs, near):
    outs = [wide_shape(pairs, 0, jnp.float32)] + [wide_shape(pairs, 0)] * (RING - 1)
    own, *leaving = scatter_call(column_kernel, "column_blocks", pairs, (0,), near, outs)
    return [own] + [shift_ring(part, steps + 1) for steps, part in enumerate(leaving)]


def total_of(parts):
    total = parts[0].astype(jnp.float32)
    for part in parts[1:]:
        total = total + part.astype(jnp.float32)
    return total


def ring_steps(kept, received):
    rows, columns = kept.shape[0] // PARTS, kept.shape[1]
    kept = kept.reshape(RING, SQUARE, rows, columns)
    received = received.reshape(RING, SQUARE, rows, columns)
    level, _ = own_place()

    def rung(back):
        index = (level + RING - back) % RING
        parts = [lax.dynamic_index_in_dim(array, index, 0, False) for array in (kept, received)]
        return total_of(parts)

    moving = rung(1).astype(jnp.bfloat16)
    for step in range(1, RING):
        moved = shift_ring(moving, 1)
        yield moved
        total = moved.astype(jnp.float32) + rung(step + 1)
        moving = total.astype(jnp.bfloat16)
    yield total


def square_sent(blocks):
    _, spot = own_place()

    def block(index):
        return lax.dynamic_index_in_dim(blocks, index, 0, keepdims=False)

    moved = [
        swap_square(block(spot ^ bit).astype(jnp.bfloat16), bit) for bit in range(1, SQUARE)
    ]
    return [block(spot)] + moved


def folded(rows, parts):
    width = rows.shape[1]
    split = rows.reshape(parts, TILES, -1, width).transpose(0, 2, 1, 3)
    return split.reshape(-1, TILES * width)


def unfolded_rows(rows, parts):
    width = rows.shape[1] // TILES
    split = rows.reshape(parts, -1, TILES, width).transpose(0, 2, 1, 3)
    return split.reshape(-1, width)


def half_of(array, which):
    width = array.shape[1] // 2
    return lax.dynamic_slice_in_dim(array, which * width, width, 1)


def half_slots(array, which):
    length = array.shape[0] // 2
    return lax.dynamic_slice_in_dim(array, which * length, length, 0)


def ordered(is_first, mine, other):
    return (jnp.where(is_first, mine, other), jnp.where(is_first, other, mine))


def on_device(
    ends_in,
    lengths,
    qkv_weight,
    qkv_bias,
    out_weight,
    up_weight,
    up_bias,
    down_weight,
    out_biases,
    norm_gains,
    norm_biases,
):
    section_index = lax.axis_index("section")
    is_first = section_index == 0
    side = section_index.astype(jnp.int32).reshape(1)
    features = ends_in.shape[2]
    width = features // 2
    count = lax.axis_size("dp")
    own_rows = ends_in[0]
    slot_count = own_rows.shape[0] // 2
    kept_rows = half_slots(own_rows, section_index)
    other_rows = swap_cores(half_slots(own_rows, 1 - section_index))
    entry, cotangent = ordered(is_first, kept_rows, other_rows)
    segment, position = layouts(
        lax.dynamic_index_in_dim(lengths, section_index, 0, keepdims=False), slot_count
    )
    tables = rotary_tables(position)
    mask = allowed_transposed(segment)

    def both(take):
        kept = take(section_index)
        other = swap_cores(take(1 - section_index))
        return ordered(is_first, kept, other)

    def take_narrow(which):
        thirds = [
            qkv_weight[0, :, part * features : (part + 1) * features] for part in range(3)
        ]
        return jnp.concatenate([half_of(part, which) for part in thirds + [out_weight[0]]], axis=1)

    pieces = (
        both(take_narrow),
        both(lambda which: half_of(up_weight[0], which)),
        both(lambda which: half_of(down_weight[0], which)),
    )

    small_shapes = [
        (qkv_bias.shape[1],),
        (up_bias.shape[1],),
        out_biases.shape[1:],
        norm_gains.shape[1:],
        norm_biases.shape[1:],
    ]
    small_own = jnp.concatenate(
        [a[0].reshape(-1) for a in (qkv_bias, up_bias, out_biases, norm_gains, norm_biases)]
    )
    small_both = jnp.concatenate(ordered(is_first, small_own, swap_cores(small_own)))
    shards = (qkv_bias.shape[1], up_bias.shape[1], norm_gains.shape[2])
    kept_forward = {}
    slabs = {}

    def attn_step(layer, rows):
        kept_forward[layer, "rows"] = rows
        made = attn_forward(side, rows, tables, mask, small[layer], *slabs[layer, "narrow"])
        kept_forward[layer, "attn"] = made
        return made

    def mlp_step(layer, kind):
        passed = kept_forward[layer, "attn"][3]
        rows = kept_forward[layer, "rows"]
        made = mlp_forward(
            side, rows, passed, small[layer], slabs[layer, "mlp"], places[layer], kind
        )
        kept_forward[layer, "mlp"] = made
        return made

    def mlp_back(layer, grad):
        rows = kept_forward[layer, "rows"]
        return mlp_backward(
            side, rows, grad, small[layer], kept_forward[layer, "mlp"][:2],
            slabs[layer, "mlp"], places[layer],
        )

    def attn_back(layer, grad, grad_mlp, kind):
        return attn_backward(
            side, kept_forward[layer, "rows"], grad, tables, mask, small[layer],
            kept_forward[layer, "attn"][:3], grad_mlp, *slabs[layer, "narrow"], kind,
        )

    def vector_of(bias_qkv, bias_up, sums):
        parts = [
            bias_qkv[half : half + 1, part * width : (part + 1) * width]
            for part in range(3)
            for half in range(2)
        ]
        order = (4, 4, 0, 1, 2, 3)
        parts += [bias_up] + [sums[index : index + 1] for index in order]
        return jnp.concatenate(parts, axis=1)

    small = []

    def spread_out(rows):
        spread = spread_small(side, rows, shards, features)
        for layer in range(2):
            made = (part[layer] for part in spread)
            small.append(dict(zip(("qkv", "up", "out", "norms"), made)))

    places = ((TILES, 0), (TILES, 1))
    if small_slice():
        narrow, up, down = pieces
        wide = [jnp.concatenate([narrow[layer], up[layer]], axis=1) for layer in range(2)]
        deep = jnp.concatenate([folded(down[layer], 1) for layer in range(2)], axis=1)
        whole_b = gather_whole(deep)
        ring_a = ring_moved(wide[0])
        line = small_both[None]
        ring_s = ring_moved(line)
        column_s = line_placed(ring_order(), [line] + ring_s)
        column_a = column_of(wide[0], ring_a)
        column_a, next_c, column_s = after((column_a, wide[1], column_s), (ring_a, ring_s))
        near_a = near_moved(column_a)
        square_s = square_moved(column_s)
        ring_c = ring_moved(next_c)
        column_c = column_of(next_c, ring_c)
        lows, column_c, square_s = after(
            (cut_near(near_a), column_c, square_s), (near_a, ring_c, square_s)
        )
        far_a = far_moved(lows)
        near_c = near_moved(column_c)
        rows_s = line_placed(square_order(), [column_s] + square_s)
        spread_out(rows_s.transpose(1, 0, 2, 3).reshape(PARTS, -1))
        whole_a = place_blocks((column_a,) + near_a + far_a)
        lows, whole_a = after((cut_near(near_c), whole_a), (far_a, near_c, small))
        far_c = far_moved(lows)
        swapped_a = swap_cores(whole_a)
        slabs[0, "narrow"] = (whole_a, swapped_a)
        whole_b = after(whole_b, far_a)
        swapped_b = swap_cores(whole_b)
        slabs[0, "mlp"] = (whole_a, swapped_a, whole_b, swapped_b)
        attn_step(0, entry)
        mlp_step(0, jnp.bfloat16)
        whole_c = place_blocks((column_c,) + near_c + far_c)
        swapped_c = swap_cores(whole_c)
        slabs[1, "narrow"] = (whole_c, swapped_c)
        slabs[1, "mlp"] = (whole_c, swapped_c, whole_b, swapped_b)
        attn_step(1, kept_forward[0, "mlp"][2])
        mlp_step(1, jnp.float32)
    else:
        spread_out(gather_whole(small_both[None]))
        whole_b = jnp.concatenate(
            [folded(gather_whole(pieces[2][layer]), PARTS) for layer in range(2)], axis=1
        )
        second = (whole_b, swap_cores(whole_b))
        for layer in range(2):
            narrow, up = (gather_whole(piece[layer]) for piece in pieces[:2])
            wide = jnp.concatenate([narrow, up], axis=1)
            slabs[layer, "narrow"] = (wide, swap_cores(wide))
            slabs[layer, "mlp"] = slabs[layer, "narrow"] + second
        attn_step(0, entry)
        mlp_step(0, jnp.bfloat16)
        attn_step(1, kept_forward[0, "mlp"][2])
        mlp_step(1, jnp.float32)
    produced = kept_forward[1, "mlp"][2]

    def mlp_pairs(made):
        return (made[0], swap_cores(made[1]), made[2], swap_cores(made[3]))

    if small_slice():
        upper = mlp_back(1, cotangent)
        pairs_a = mlp_pairs(upper)
        upper_attn = attn_back(1, cotangent, upper[5], jnp.bfloat16)
        leaving_a = far_blocks(after(pairs_a, upper_attn[2]))
        far_a = sent_both(leaving_a)
        grad_middle = after(upper_attn[4], leaving_a)
        received_b = swap_cores(upper_attn[1])
        lower = mlp_back(0, grad_middle)
        leaving_a = near_blocks(pairs_a, after(far_a, lower[4]))
        near_a = sent_both(leaving_a)
        steps_b = ring_steps(upper_attn[0], after(received_b, lower[4]))
        moved_b = next(steps_b)
        pairs_c = mlp_pairs(lower)
        lower_attn = attn_back(
            0, grad_middle, after(lower[5], (leaving_a, received_b)), jnp.float32
        )
        pairs_d = (lower_attn[0], swap_cores(lower_attn[1]))
        moved_b = next(steps_b)
        pairs_c = after(pairs_c, (lower_attn[2], near_a))
        far_c = sent_both(far_blocks(pairs_c))
        pairs_d = after(pairs_d, near_a)
        far_d = sent_both(far_blocks(pairs_d))
        moved_b = next(steps_b)
        parts_a = column_sent(pairs_a, after(near_a, far_c))
        near_c = sent_both(near_blocks(pairs_c, after(far_c, far_d)))
        blocks_b = next(steps_b)
        near_d = sent_both(near_blocks(pairs_d, after(far_d, near_c)))
        parts_c = column_sent(pairs_c, near_c)
        parts_b = square_sent(after(blocks_b, near_c))
        parts_d = column_sent(pairs_d, after(near_d, near_c))
        reduced = (
            (total_of(parts_d), total_of(parts_b)),
            (total_of(parts_c), total_of(parts_a)),
        )
    else:
        upper = mlp_back(1, cotangent)
        upper_attn = attn_back(1, cotangent, upper[5], jnp.bfloat16)
        lower = mlp_back(0, upper_attn[4])
        lower_attn = attn_back(0, upper_attn[4], lower[5], jnp.float32)

        def spread(kept, received):
            summed = kept.astype(jnp.float32) + received.astype(jnp.float32)
            return lax.psum_scatter(summed, "dp", scatter_dimension=0, tiled=True)

        def spread_mlp(made):
            up_kept, up_got, down_kept, down_got = mlp_pairs(made)
            down = spread(unfolded_rows(down_kept, PARTS), unfolded_rows(down_got, PARTS))
            return jnp.concatenate([spread(up_kept, up_got), folded(down, 1)], axis=1)

        reduced = (
            tuple(spread(made[0], swap_cores(made[1])) for made in (lower_attn, upper_attn)),
            tuple(spread_mlp(made) for made in (lower, upper)),
        )
    grad_entry = lower_attn[4]
    def finish(lower, upper):
        mine, leaving = ordered(is_first, lower, upper)
        return ordered(is_first, mine, swap_cores(leaving))

    narrow_halves, mlp_halves = (finish(*pair) for pair in reduced)
    up_width = up_weight.shape[2] // 2
    total_up = jnp.concatenate([part[:, :up_width] for part in mlp_halves], axis=1)
    total_down = jnp.concatenate(
        [unfolded_rows(part[:, up_width:], 1) for part in mlp_halves], axis=1
    )
    total_qkv = jnp.concatenate(
        [
            part[:, at * width : (at + 1) * width]
            for at in range(3)
            for part in narrow_halves
        ],
        axis=1,
    )
    total_out = jnp.concatenate([part[:, 3 * width :] for part in narrow_halves], axis=1)

    vectors = [
        vector_of(attn[2], mlp[4], attn[3])
        for mlp, attn in ((lower, lower_attn), (upper, upper_attn))
    ]
    vector_kept, vector_sent = ordered(is_first, *vectors)
    if small_slice():
        vector = vector_kept + swap_cores(vector_sent)
        vector = total_of([vector] + square_moved(vector))
        vector = total_of([vector] + ring_moved(after(vector, near_c)))
    else:
        vector = lax.psum(vector_kept + swap_cores(vector_sent), "dp")
    place = lax.axis_index("dp")
    small_outs = []
    at = 0
    for shape in small_shapes:
        lead, size = (1,) if len(shape) == 1 else (shape[0],), shape[-1]
        rows = vector[0, at : at + lead[0] * size * count].reshape(lead[0], count * size)
        at += lead[0] * size * count
        part = lax.dynamic_slice_in_dim(rows, place * size, size, 1)
        small_outs.append(part.reshape((1,) + shape))

    staying, leaving = ordered(is_first, grad_entry, produced)
    ends_out = jnp.concatenate(ordered(is_first, staying, swap_cores(leaving)))
    return (
        ends_out[None],
        total_qkv[None],
        small_outs[0],
        total_out[None],
        total_up[None],
        small_outs[1],
        total_down[None],
        small_outs[2],
        small_outs[3],
        small_outs[4],
    )


def solution(mesh):
    return jax.shard_map(
        on_device,
        mesh=mesh,
        in_specs=(
            P("section", "dp", None),
            P("dp", None),
            P("section", "dp", None),
            P("section", "dp"),
            P("section", "dp", None),
            P("section", "dp", None),
            P("section", "dp"),
            P("section", "dp", None),
            P("section", None, "dp"),
            P("section", None, "dp"),
            P("section", None, "dp"),
        ),
        out_specs=(
            P("section", "dp", None),
            P("section", "dp", None),
            P("section", "dp"),
            P("section", "dp", None),
            P("section", "dp", None),
            P("section", "dp"),
            P("section", "dp", None),
            P("section", None, "dp"),
            P("section", None, "dp"),
            P("section", None, "dp"),
        ),
        check_vma=False,
    )
```

```python
import math

import jax
import jax.numpy as jnp
import numpy as np
from jax import lax
from jax.experimental import pallas as pl
from jax.experimental.pallas import tpu as pltpu
from jax.sharding import PartitionSpec as P

HD = 64
ROT = 16
LANES = 128
TILES = 2
FOLD = 4
PARTS = 16


eps = 1e-05
masked_score = -1e30
vmem_bytes = 48 * 1024 * 1024


def product(left, right):
    return jnp.dot(left, right, preferred_element_type=jnp.float32)


def product_transposed(left, right):
    return lax.dot_general(
        left, right, (((1,), (1,)), ((), ())), preferred_element_type=jnp.float32
    )


def layouts(lengths, slot_count):
    ends_at = jnp.cumsum(lengths)
    indices = jnp.arange(slot_count, dtype=jnp.int32)
    passed = indices[:, None] >= ends_at[None, :]
    segments = jnp.sum(passed.astype(jnp.int32), axis=1)
    starts = jnp.sum(jnp.where(passed, lengths[None, :], 0), axis=1)
    return (segments, indices - starts)


def rotary_tables(positions):
    lane = jnp.arange(LANES, dtype=jnp.int32) % HD
    half = ROT // 2
    freqs = 10000.0 ** (-2.0 * (lane % half).astype(jnp.float32) / ROT)
    angles = positions.astype(jnp.float32)[:, None] * freqs[None, :]
    cosine = jnp.where(lane < ROT, jnp.cos(angles), 1.0)
    sine = jnp.sin(angles)
    ahead = jnp.where(lane < half, -sine, 0.0)
    behind = jnp.where((lane >= half) & (lane < ROT), sine, 0.0)
    return jnp.stack([cosine, ahead, behind])


def allowed_transposed(segment):
    indices = jnp.arange(segment.shape[0], dtype=jnp.int32)
    allowed = (segment[:, None] == segment[None, :]) & (indices[:, None] <= indices[None, :])
    return allowed.astype(jnp.float32)


def turned(values, tables, back):
    half = ROT // 2
    parts = []
    for at in range(0, values.shape[1], LANES):
        part = values[:, at : at + LANES]
        moved = (
            pltpu.roll(part, LANES - half, 1) * tables[1] + pltpu.roll(part, half, 1) * tables[2]
        )
        kept = part * tables[0]
        parts.append(kept - moved if back else kept + moved)
    return jnp.concatenate(parts, axis=1)


def unit_rows(rows):
    centred = rows - jnp.mean(rows, axis=-1, keepdims=True)
    spread = jnp.mean(centred * centred, axis=-1, keepdims=True)
    scale = lax.rsqrt(spread + eps)
    return (centred * scale, scale)


def lane_half(which, width):
    return pl.ds(pl.multiple_of(which * width, LANES), width)


def head_lanes(values, which):
    lane = lax.broadcasted_iota(jnp.int32, values.shape, 1)
    return jnp.where((lane < HD) == (which == 0), values, jnp.zeros_like(values))


def scores_of(key_pair, query_pair, which, allowed):
    scores = product_transposed(head_lanes(key_pair, which), query_pair) * (1.0 / math.sqrt(HD))
    return jnp.where(allowed, scores, masked_score)


def attn_forward_kernel(
    side, rows, tables, mask, norms, bias_qkv, bias_out, mine, other, qkv, logs, attended, passed
):
    width = mine.shape[1] // 4
    entry = rows[...].astype(jnp.float32)
    unit, _ = unit_rows(entry)
    normed = (unit * norms[0:1] + norms[2:3]).astype(jnp.bfloat16)
    allowed = mask[...] > 0.5
    for at, weight in enumerate((mine, other)):
        half = side[0] if at == 0 else 1 - side[0]
        parts = []
        for part in range(3):
            cut = slice(part * width, (part + 1) * width)
            value = product(normed, weight[:, cut]) + bias_qkv[at : at + 1, cut]
            if part < 2:
                value = turned(value, tables, False)
            value = value.astype(jnp.bfloat16)
            qkv[at, :, cut] = value
            parts.append(value)
        queries, keys, values = parts
        values = values.T
        outs = []
        for pair in range(width // LANES):
            cut = slice(pair * LANES, (pair + 1) * LANES)
            for which in range(2):
                head = 2 * pair + which
                scores = scores_of(keys[:, cut], queries[:, cut], which, allowed)
                peak = jnp.max(scores, axis=0, keepdims=True)
                raised = jnp.exp(scores - peak)
                total = jnp.sum(raised, axis=0, keepdims=True)
                chances = (raised * (1.0 / total)).astype(jnp.bfloat16)
                outs.append(product(values[head * HD : (head + 1) * HD], chances))
                logs[at, head : head + 1, :] = peak + jnp.log(total)
        mixed = jnp.concatenate(outs, axis=0).T.astype(jnp.bfloat16)
        attended[:, lane_half(half, width)] = mixed
    mixed = attended[...]
    for at, weight in enumerate((mine, other)):
        half = side[0] if at == 0 else 1 - side[0]
        lanes = lane_half(half, width)
        passed[:, lanes] = (
            rows[:, lanes].astype(jnp.float32)
            + product(mixed, weight[:, 3 * width :])
            + bias_out[0:1, lanes]
        )


def fixed(*shape):
    return pl.BlockSpec(shape, lambda *at: (0,) * len(shape))


def fixed_like(*arrays):
    return [fixed(*array.shape) for array in arrays]


def attn_forward(side, rows, tables, mask, small, mine, other):
    length, features = rows.shape
    width = features // 2
    heads = width // HD
    return pl.pallas_call(
        attn_forward_kernel,
        out_shape=(
            jax.ShapeDtypeStruct((2, length, 3 * width), jnp.bfloat16),
            jax.ShapeDtypeStruct((2, heads, length), jnp.float32),
            jax.ShapeDtypeStruct((length, features), jnp.bfloat16),
            jax.ShapeDtypeStruct((length, features), jnp.float32),
        ),
        grid=(1,),
        in_specs=[pl.BlockSpec(memory_space=pltpu.SMEM)]
        + fixed_like(rows, tables, mask, small["norms"], small["qkv"], small["out"])
        + [fixed(features, 4 * width)] * 2,
        out_specs=(
            fixed(2, length, 3 * width),
            fixed(2, heads, length),
            fixed(length, features),
            fixed(length, features),
        ),
        compiler_params=pltpu.CompilerParams(vmem_limit_bytes=vmem_bytes),
        cost_estimate=pl.CostEstimate(
            flops=2 * length * features * features * 30,
            bytes_accessed=8 * features * features,
            transcendentals=length * length * features // HD,
        ),
        name="attn_forward",
    )(side, rows, tables, mask, small["norms"], small["qkv"], small["out"], mine, other)


def tile_of(step, side):
    half = jnp.where(step < TILES, side[0], 1 - side[0])
    return half * TILES + step % TILES


def first_tile(step):
    return jnp.minimum(step, TILES - 1)


def second_tile(step):
    return jnp.maximum(step - TILES, 0)


def folded_cuts(shape, width):
    rows = 2 * width // PARTS
    for part in range(shape[0] // rows):
        for column in range(shape[1] // width):
            yield (
                slice(part * rows, (part + 1) * rows),
                slice(column * width, (column + 1) * width),
            )


def unfolded(block, width):
    return jnp.concatenate([block[cut] for cut in folded_cuts(block.shape, width)], axis=0)


def down_joined(mine, other, width):
    return jnp.concatenate([unfolded(mine, width), unfolded(other, width)], axis=1)


def mlp_forward_kernel(
    side, rows, passed, norms, bias_up, bias_out, up_mine, up_other, down_mine, down_other,
    active, slope, produced, normed, total
):
    step = pl.program_id(0)

    @pl.when(step == 0)
    def _():
        unit, _ = unit_rows(rows[...].astype(jnp.float32))
        normed[...] = (unit * norms[1:2] + norms[3:4]).astype(jnp.bfloat16)
        total[...] = jnp.zeros_like(total)

    weight = jnp.where(step < TILES, up_mine[...], up_other[...])
    hidden = product(normed[...], weight) + bias_up[...]
    bell = 0.5 * (1.0 + lax.erf(hidden * (1.0 / math.sqrt(2.0))))
    density = jnp.exp(-0.5 * hidden * hidden) * (1.0 / math.sqrt(2.0 * math.pi))
    slope[...] = bell + hidden * density
    lit = (hidden * bell).astype(jnp.bfloat16)
    active[...] = lit
    width = total.shape[1] // 2
    total[...] += product(lit, down_joined(down_mine, down_other, width))

    @pl.when(step == 2 * TILES - 1)
    def _():
        for at, half in enumerate((side[0], 1 - side[0])):
            lanes = lane_half(half, width)
            part = total[:, at * width : (at + 1) * width]
            produced[:, lanes] = (
                passed[:, lanes] + part + bias_out[1:2, lanes]
            ).astype(produced.dtype)


def mlp_forward(side, rows, passed, small, weights, places, kind):
    up_mine, up_other, down_mine, down_other = weights
    up_at, down_at = places
    length, features = rows.shape
    width = features // 2
    tile = FOLD * width // TILES
    hidden = 2 * TILES * tile
    folded = features // (2 * TILES)
    tiled = pl.BlockSpec((length, tile), lambda step, side: (0, tile_of(step, side)))
    down_spec = pl.BlockSpec(
        (folded, FOLD * width), lambda step, side: (tile_of(step, side), down_at)
    )
    return pl.pallas_call(
        mlp_forward_kernel,
        out_shape=(
            jax.ShapeDtypeStruct((length, hidden), jnp.bfloat16),
            jax.ShapeDtypeStruct((length, hidden), jnp.float32),
            jax.ShapeDtypeStruct((length, features), kind),
        ),
        grid_spec=pltpu.PrefetchScalarGridSpec(
            num_scalar_prefetch=1,
            grid=(2 * TILES,),
            in_specs=[
                fixed(length, features),
                fixed(length, features),
                fixed(4, features),
                pl.BlockSpec((1, tile), lambda step, side: (0, tile_of(step, side))),
                fixed(2, features),
                pl.BlockSpec((features, tile), lambda step, side: (0, up_at + first_tile(step))),
                pl.BlockSpec((features, tile), lambda step, side: (0, up_at + second_tile(step))),
                down_spec,
                down_spec,
            ],
            out_specs=(tiled, tiled, fixed(length, features)),
            scratch_shapes=[
                pltpu.VMEM((length, features), jnp.bfloat16),
                pltpu.VMEM((length, features), jnp.float32),
            ],
        ),
        compiler_params=pltpu.CompilerParams(vmem_limit_bytes=vmem_bytes),
        cost_estimate=pl.CostEstimate(
            flops=20 * length * features * hidden,
            bytes_accessed=4 * features * hidden + 6 * length * hidden,
            transcendentals=2 * length * hidden,
        ),
        name="mlp_forward",
    )(
        side, rows, passed, small["norms"], small["up"], small["out"],
        up_mine, up_other, down_mine, down_other,
    )


def mlp_backward_kernel(
    side, rows, grad, norms, active, slope, up_mine, up_other, down_mine, down_other,
    up_kept, up_sent, down_kept, down_sent, bias_grad, grad_normed, normed, grads
):
    step = pl.program_id(0)
    width = grad.shape[1] // 2
    cuts = list(folded_cuts(down_mine.shape, width))

    @pl.when(step == 0)
    def _():
        unit, _ = unit_rows(rows[...].astype(jnp.float32))
        normed[...] = (unit * norms[1:2] + norms[3:4]).T.astype(jnp.bfloat16)
        grad_normed[...] = jnp.zeros_like(grad_normed)
        grads[:, :width] = grad[:, lane_half(side[0], width)]
        grads[:, width:] = grad[:, lane_half(1 - side[0], width)]

    weight = jnp.where(step < TILES, up_mine[...], up_other[...])
    lit = active[...].T
    made = product(lit, grads[...]).astype(jnp.bfloat16)
    rows_each = made.shape[0] // len(cuts)
    for index, cut in enumerate(cuts):
        part = made[index * rows_each : (index + 1) * rows_each]
        down_kept[cut] = part[:, :width]
        down_sent[cut] = part[:, width:]
    back = product_transposed(grads[...], down_joined(down_mine, down_other, width))
    back = (back * slope[...]).astype(jnp.bfloat16)
    bias_grad[...] = jnp.sum(back.astype(jnp.float32), axis=0, keepdims=True)
    up_grad = product(normed[...], back).astype(jnp.bfloat16)

    @pl.when(step < TILES)
    def _():
        up_kept[...] = up_grad

    @pl.when(step >= TILES)
    def _():
        up_sent[...] = up_grad

    grad_normed[...] += product_transposed(back, weight)


def mlp_backward(side, rows, grad, small, saved, weights, places):
    active, slope = saved
    up_mine, up_other, down_mine, down_other = weights
    up_at, down_at = places
    length, features = rows.shape
    width = features // 2
    tile = FOLD * width // TILES
    hidden = 2 * TILES * tile
    folded = features // (2 * TILES)
    tiled = pl.BlockSpec((length, tile), lambda step, side: (0, tile_of(step, side)))
    down_spec = pl.BlockSpec(
        (folded, FOLD * width), lambda step, side: (tile_of(step, side), down_at)
    )
    up_first = pl.BlockSpec((features, tile), lambda step, side: (0, first_tile(step)))
    up_second = pl.BlockSpec((features, tile), lambda step, side: (0, second_tile(step)))
    down_out = pl.BlockSpec(
        (folded, FOLD * width), lambda step, side: (tile_of(step, side), 0)
    )
    return pl.pallas_call(
        mlp_backward_kernel,
        out_shape=(
            jax.ShapeDtypeStruct((features, hidden // 2), jnp.bfloat16),
            jax.ShapeDtypeStruct((features, hidden // 2), jnp.bfloat16),
            jax.ShapeDtypeStruct((features, FOLD * width), jnp.bfloat16),
            jax.ShapeDtypeStruct((features, FOLD * width), jnp.bfloat16),
            jax.ShapeDtypeStruct((1, hidden), jnp.float32),
            jax.ShapeDtypeStruct((length, features), jnp.float32),
        ),
        grid_spec=pltpu.PrefetchScalarGridSpec(
            num_scalar_prefetch=1,
            grid=(2 * TILES,),
            in_specs=[
                fixed(length, features),
                fixed(length, features),
                fixed(4, features),
                tiled,
                tiled,
                pl.BlockSpec((features, tile), lambda step, side: (0, up_at + first_tile(step))),
                pl.BlockSpec((features, tile), lambda step, side: (0, up_at + second_tile(step))),
                down_spec,
                down_spec,
            ],
            out_specs=(
                up_first,
                up_second,
                down_out,
                down_out,
                pl.BlockSpec((1, tile), lambda step, side: (0, tile_of(step, side))),
                fixed(length, features),
            ),
            scratch_shapes=[
                pltpu.VMEM((features, length), jnp.bfloat16),
                pltpu.VMEM((length, features), jnp.bfloat16),
            ],
        ),
        compiler_params=pltpu.CompilerParams(vmem_limit_bytes=vmem_bytes),
        cost_estimate=pl.CostEstimate(
            flops=32 * length * features * hidden,
            bytes_accessed=8 * features * hidden + 6 * length * hidden,
            transcendentals=0,
        ),
        name="mlp_backward",
    )(
        side, rows, grad, small["norms"], active, slope,
        up_mine, up_other, down_mine, down_other,
    )


def attn_backward_kernel(
    side, rows, grad, tables, mask, norms, qkv, logs, attended, grad_mlp, mine, other,
    kept, sent, bias_grad, sums, passed, mixed_back
):
    width = mine.shape[1] // 4
    unit, scale = unit_rows(rows[...].astype(jnp.float32))
    normed = (unit * norms[0:1] + norms[2:3]).T.astype(jnp.bfloat16)
    allowed = mask[...] > 0.5
    mixed = attended[...].T
    back = None
    for at, (weight, result) in enumerate(((mine, kept), (other, sent))):
        half = side[0] if at == 0 else 1 - side[0]
        part = grad[:, lane_half(half, width)]
        result[:, 3 * width :] = product(mixed, part).astype(jnp.bfloat16)
        term = product_transposed(part, weight[:, 3 * width :])
        back = term if back is None else back + term
    mixed_back[...] = back.astype(jnp.bfloat16)
    grad_attn = None
    for at, (weight, result) in enumerate(((mine, kept), (other, sent))):
        half = side[0] if at == 0 else 1 - side[0]
        queries = qkv[at, :, 0:width]
        keys = qkv[at, :, width : 2 * width]
        values = qkv[at, :, 2 * width :]
        keys_turned = keys.T
        grad_out = mixed_back[:, lane_half(half, width)]
        query_grads, key_grads, value_grads = [], [], []
        for pair in range(width // LANES):
            cut = slice(pair * LANES, (pair + 1) * LANES)
            key_pair, value_pair = [], []
            for which in range(2):
                head = 2 * pair + which
                scores = scores_of(keys[:, cut], queries[:, cut], which, allowed)
                chances = jnp.exp(scores - logs[at, head : head + 1, :])
                value_pair.append(product(chances.astype(jnp.bfloat16), grad_out[:, cut]))
                slopes = product_transposed(head_lanes(values[:, cut], which), grad_out[:, cut])
                inner = jnp.sum(slopes * chances, axis=0, keepdims=True)
                slopes = (chances * (slopes - inner)).astype(jnp.bfloat16)
                key_pair.append(product(slopes, queries[:, cut]))
                query_grads.append(product(keys_turned[head * HD : (head + 1) * HD], slopes))
            lane = lax.broadcasted_iota(jnp.int32, key_pair[0].shape, 1)
            key_grads.append(jnp.where(lane < HD, key_pair[0], key_pair[1]))
            value_grads.append(jnp.where(lane < HD, value_pair[0], value_pair[1]))
        factor = 1.0 / math.sqrt(HD)
        query_grad = turned(jnp.concatenate(query_grads, axis=0).T * factor, tables, True)
        key_grad = turned(jnp.concatenate(key_grads, axis=1) * factor, tables, True)
        value_grad = jnp.concatenate(value_grads, axis=1)
        for index, part in enumerate((query_grad, key_grad, value_grad)):
            cut = slice(index * width, (index + 1) * width)
            part = part.astype(jnp.bfloat16)
            bias_grad[pl.ds(half, 1), cut] = jnp.sum(
                part.astype(jnp.float32), axis=0, keepdims=True
            )
            result[:, cut] = product(normed, part).astype(jnp.bfloat16)
            term = product_transposed(part, weight[:, cut])
            grad_attn = term if grad_attn is None else grad_attn + term
    grad_up = grad_mlp[...]
    grad_rows = grad[...].astype(jnp.float32)
    sums[0:1] = jnp.sum(unit * grad_attn, axis=0, keepdims=True)
    sums[1:2] = jnp.sum(unit * grad_up, axis=0, keepdims=True)
    sums[2:3] = jnp.sum(grad_attn, axis=0, keepdims=True)
    sums[3:4] = jnp.sum(grad_up, axis=0, keepdims=True)
    sums[4:5] = jnp.sum(grad_rows, axis=0, keepdims=True)
    inward = grad_attn * norms[0:1] + grad_up * norms[1:2]
    level = jnp.mean(inward, axis=-1, keepdims=True)
    along = jnp.mean(inward * unit, axis=-1, keepdims=True)
    passed[...] = (grad_rows + (inward - level - unit * along) * scale).astype(passed.dtype)


def attn_backward(side, rows, grad, tables, mask, small, saved, grad_mlp, mine, other, kind):
    qkv, logs, attended = saved
    length, features = rows.shape
    return pl.pallas_call(
        attn_backward_kernel,
        out_shape=(
            jax.ShapeDtypeStruct((features, 2 * features), jnp.bfloat16),
            jax.ShapeDtypeStruct((features, 2 * features), jnp.bfloat16),
            jax.ShapeDtypeStruct((2, 3 * features // 2), jnp.float32),
            jax.ShapeDtypeStruct((5, features), jnp.float32),
            jax.ShapeDtypeStruct((length, features), kind),
        ),
        grid=(1,),
        in_specs=[pl.BlockSpec(memory_space=pltpu.SMEM)]
        + fixed_like(rows, grad, tables, mask, small["norms"], qkv, logs, attended, grad_mlp)
        + [fixed(features, 2 * features)] * 2,
        out_specs=(
            fixed(features, 2 * features),
            fixed(features, 2 * features),
            fixed(2, 3 * features // 2),
            fixed(5, features),
            fixed(length, features),
        ),
        scratch_shapes=[pltpu.VMEM((length, features), jnp.bfloat16)],
        compiler_params=pltpu.CompilerParams(vmem_limit_bytes=vmem_bytes),
        cost_estimate=pl.CostEstimate(
            flops=2 * length * features * features * 48,
            bytes_accessed=16 * features * features,
            transcendentals=length * length * features // HD,
        ),
        name="attn_backward",
    )(
        side, rows, grad, tables, mask, small["norms"], qkv, logs, attended, grad_mlp, mine, other
    )


SQUARE = 4
RING = 4


def swap_cores(value):
    return lax.ppermute(value, "section", [(0, 1), (1, 0)])


def swap_square(value, bit):
    count = lax.axis_size("dp")
    return lax.ppermute(value, "dp", [(i, i ^ bit) for i in range(count)])


def shift_ring(value, steps):
    count = lax.axis_size("dp")
    pairs = [(i, (i + SQUARE * steps) % count) for i in range(count)]
    return lax.ppermute(value, "dp", pairs)


def small_slice():
    return lax.axis_size("dp") == SQUARE * RING


def after(values, earlier):
    flat, shape = jax.tree.flatten(values)
    waited = jax.tree.leaves(earlier)
    tied = lax.optimization_barrier(tuple(flat) + tuple(waited))
    return jax.tree.unflatten(shape, tied[: len(flat)])


def own_place():
    place = lax.axis_index("dp").astype(jnp.int32)
    return (place // SQUARE, place % SQUARE)


def any_space(count):
    return [pl.BlockSpec(memory_space=pl.ANY)] * count


def place_kernel(spot_ref, *refs):
    blocks, outs, sems = refs[:5], refs[5:-1], refs[-1]
    own, first, second, far_low, far_high = blocks
    spot = spot_ref[0]
    half = RING // 2
    copies = []
    at = 0
    for index, out in enumerate(outs):
        lanes = pl.ds(at, out.shape[3])
        at += out.shape[3]
        pairs = (
            (own, out.at[:, spot]),
            (first, out.at[:, spot ^ 1]),
            (second, out.at[:, spot ^ 2]),
            (far_low, out.at[pl.ds(0, half), spot ^ 3]),
            (far_high, out.at[pl.ds(half, half), spot ^ 3]),
        )
        for place, (block, target) in enumerate(pairs):
            copies.append(
                pltpu.make_async_copy(
                    block.at[:, :, lanes], target, sems.at[5 * index + place]
                )
            )
    for copy in copies:
        copy.start()
    for copy in copies:
        copy.wait()


def place_blocks(blocks, widths):
    spot = own_place()[1].reshape(1)
    rows = blocks[0].shape[1]
    placed = pl.pallas_call(
        place_kernel,
        out_shape=tuple(
            jax.ShapeDtypeStruct((RING, SQUARE, rows, columns), blocks[0].dtype)
            for columns in widths
        ),
        in_specs=[pl.BlockSpec(memory_space=pltpu.SMEM)] + any_space(5),
        out_specs=tuple([pl.BlockSpec(memory_space=pltpu.VMEM)] * len(widths)),
        scratch_shapes=[pltpu.SemaphoreType.DMA((5 * len(widths),))],
        compiler_params=pltpu.CompilerParams(vmem_limit_bytes=vmem_bytes),
        name="place_blocks",
    )(spot, *blocks)
    return [part.reshape(PARTS * rows, -1) for part in placed]


def line_kernel(order_ref, *refs):
    held, out, sems = refs[:-2], refs[-2], refs[-1]
    copies = [
        pltpu.make_async_copy(part, out.at[order_ref[at]], sems.at[at])
        for at, part in enumerate(held)
    ]
    for copy in copies:
        copy.start()
    for copy in copies:
        copy.wait()


def line_placed(order, held):
    return pl.pallas_call(
        line_kernel,
        out_shape=jax.ShapeDtypeStruct((len(held),) + held[0].shape, held[0].dtype),
        in_specs=[pl.BlockSpec(memory_space=pltpu.SMEM)] + any_space(len(held)),
        out_specs=pl.BlockSpec(memory_space=pltpu.VMEM),
        scratch_shapes=[pltpu.SemaphoreType.DMA((len(held),))],
        compiler_params=pltpu.CompilerParams(vmem_limit_bytes=vmem_bytes),
        name="place_line",
    )(order, *held)


def ring_order():
    return (own_place()[0] + RING - jnp.arange(RING, dtype=jnp.int32)) % RING


def square_order():
    return own_place()[1] ^ jnp.arange(SQUARE, dtype=jnp.int32)


def gather_whole(piece):
    return lax.all_gather(piece, "dp", axis=0, tiled=True)


def ring_moved(piece):
    return [shift_ring(piece, steps) for steps in range(1, RING)]


def square_moved(piece):
    return [swap_square(piece, bit) for bit in range(1, SQUARE)]


def column_of(piece, moved):
    return line_placed(ring_order(), [piece] + moved)


def near_moved(column):
    return (swap_square(column, 1), swap_square(column, 2))


def cut_near(near):
    half = RING // 2
    return (near[0][:half], near[1][half:])


def far_moved(lows):
    return (swap_square(lows[0], 2), swap_square(lows[1], 1))


def ring_around(blocks):
    held = [blocks]
    for _ in range(RING - 1):
        held.append(shift_ring(held[-1], 1))
    return held


def spread_kernel(side, rows, *refs):
    picks, outs = refs[:6], refs[6:]
    count = rows.shape[0]
    width = outs[0].shape[2] // 3
    size = rows.shape[1] // 2

    def row(at, which):
        pick, keep = picks[2 * which], picks[2 * which + 1]
        found = product(rows[:, at : at + pick.shape[0]], pick[...])
        return jnp.sum(found * keep[...], axis=0, keepdims=True)

    for layer in range(2):
        at = layer * size
        found = row(at, 0)
        for half in range(2):
            parts = [
                found[:, (2 * part + half) * width : (2 * part + half + 1) * width]
                for part in range(3)
            ]
            outs[0][layer, pl.ds(half ^ side[0], 1), :] = jnp.concatenate(parts, axis=1)
        at += picks[0].shape[0]
        outs[1][layer] = row(at, 1)
        at += picks[2].shape[0]
        step = picks[4].shape[0]
        for index in range(2):
            outs[2][layer, index : index + 1, :] = row(at + index * step, 2)
        for index in range(4):
            outs[3][layer, index : index + 1, :] = row(at + (2 + index) * step, 2)


def spread_small(side, rows, shards, features):
    count = rows.shape[0]
    picks = []
    for shard in shards:
        lane = np.arange(count * shard)
        picks.append(jnp.asarray(np.arange(shard)[:, None] == lane % shard, jnp.bfloat16))
        picks.append(jnp.asarray(np.arange(count)[:, None] == lane // shard, jnp.float32))
    shapes = (
        (2, 2, 3 * features // 2),
        (2, 1, count * shards[1]),
        (2, 2, features),
        (2, 4, features),
    )
    outs = [jax.ShapeDtypeStruct(shape, jnp.float32) for shape in shapes]
    return pl.pallas_call(
        spread_kernel,
        out_shape=tuple(outs),
        grid=(1,),
        in_specs=[pl.BlockSpec(memory_space=pltpu.SMEM)] + fixed_like(rows, *picks),
        out_specs=tuple(fixed_like(*outs)),
        compiler_params=pltpu.CompilerParams(vmem_limit_bytes=vmem_bytes),
        name="spread_small",
    )(side, rows, *picks)


def far_kernel(place_ref, *refs):
    pairs, (low, high) = refs[:-2], refs[-2:]
    half = RING // 2
    columns = pairs[0].shape[-1]
    for at in range(0, len(pairs), 2):
        cut = slice(at // 2 * columns, (at // 2 + 1) * columns)
        total = pairs[at][...].astype(jnp.float32) + pairs[at + 1][...].astype(jnp.float32)
        total = total[:, 0].astype(low.dtype)
        low[:, :, cut] = total[:half]
        high[:, :, cut] = total[half:]


def near_kernel(place_ref, *refs):
    pairs, (far_low, far_high), (first, second) = refs[:-4], refs[-4:-2], refs[-2:]
    half = RING // 2
    columns = pairs[0].shape[-1]
    for at in range(0, len(pairs), 4):
        cut = slice(at // 4 * columns, (at // 4 + 1) * columns)
        one, two, three, four = (pair[...].astype(jnp.float32)[:, 0] for pair in pairs[at : at + 4])
        total = one + two
        first[:half, :, cut] = total[:half].astype(first.dtype)
        high = far_high[:, :, cut].astype(jnp.float32)
        first[half:, :, cut] = (total[half:] + high).astype(first.dtype)
        total = three + four
        low = far_low[:, :, cut].astype(jnp.float32)
        second[:half, :, cut] = (total[:half] + low).astype(first.dtype)
        second[half:, :, cut] = total[half:].astype(first.dtype)


def column_kernel(place_ref, *refs):
    pairs, (first, second), outs = refs[: -2 - RING], refs[-2 - RING : -RING], refs[-RING:]
    columns = pairs[0].shape[-1]
    for steps, out in enumerate(outs):
        level = lax.rem(place_ref[0] + steps, RING)
        for at in range(0, len(pairs), 2):
            cut = slice(at // 2 * columns, (at // 2 + 1) * columns)
            total = pairs[at][level, 0].astype(jnp.float32)
            total += pairs[at + 1][level, 0].astype(jnp.float32)
            total += first[level, :, cut].astype(jnp.float32)
            total += second[level, :, cut].astype(jnp.float32)
            out[:, cut] = total.astype(out.dtype)


def block_spec(rows, columns, bit):
    return pl.BlockSpec(
        (RING, 1, rows, columns), lambda step, place: (0, place[1] ^ bit, 0, 0)
    )


def scatter_call(body, name, pairs, bits, extra, outs):
    rows, columns = pairs[0].shape[0] // PARTS, pairs[0].shape[1]
    blocks, specs = [], []
    for at in range(0, len(pairs), 2):
        for bit in bits:
            for array in pairs[at : at + 2]:
                blocks.append(array.reshape(RING, SQUARE, rows, columns))
                specs.append(block_spec(rows, columns, bit))
    return pl.pallas_call(
        body,
        out_shape=tuple(outs),
        grid_spec=pltpu.PrefetchScalarGridSpec(
            num_scalar_prefetch=1,
            grid=(1,),
            in_specs=specs + fixed_like(*extra),
            out_specs=tuple(fixed_like(*outs)),
        ),
        compiler_params=pltpu.CompilerParams(vmem_limit_bytes=vmem_bytes),
        name=name,
    )(jnp.stack(own_place()), *blocks, *extra)


def wide_shape(pairs, count, kind=jnp.bfloat16):
    rows, columns = pairs[0].shape[0] // PARTS, pairs[0].shape[1] * len(pairs) // 2
    lead = (count,) if count else ()
    return jax.ShapeDtypeStruct(lead + (rows, columns), kind)


def far_blocks(pairs):
    half = wide_shape(pairs, RING // 2)
    return scatter_call(far_kernel, "far_blocks", pairs, (3,), (), [half, half])


def near_blocks(pairs, far):
    full = wide_shape(pairs, RING)
    return scatter_call(near_kernel, "near_blocks", pairs, (1, 2), far, [full, full])


def sent_both(blocks):
    return (swap_square(blocks[0], 1), swap_square(blocks[1], 2))


def column_sent(pairs, near):
    outs = [wide_shape(pairs, 0, jnp.float32)] + [wide_shape(pairs, 0)] * (RING - 1)
    own, *leaving = scatter_call(column_kernel, "column_blocks", pairs, (0,), near, outs)
    return [own] + [shift_ring(part, steps + 1) for steps, part in enumerate(leaving)]


def total_of(parts):
    total = parts[0].astype(jnp.float32)
    for part in parts[1:]:
        total = total + part.astype(jnp.float32)
    return total


def ring_steps(kept, received):
    rows, columns = kept.shape[0] // PARTS, kept.shape[1]
    kept = kept.reshape(RING, SQUARE, rows, columns)
    received = received.reshape(RING, SQUARE, rows, columns)
    level, _ = own_place()

    def rung(back):
        index = (level + RING - back) % RING
        parts = [lax.dynamic_index_in_dim(array, index, 0, False) for array in (kept, received)]
        return total_of(parts)

    moving = rung(1).astype(jnp.bfloat16)
    for step in range(1, RING):
        moved = shift_ring(moving, 1)
        yield moved
        total = moved.astype(jnp.float32) + rung(step + 1)
        moving = total.astype(jnp.bfloat16)
    yield total


def square_sent(blocks):
    _, spot = own_place()

    def block(index):
        return lax.dynamic_index_in_dim(blocks, index, 0, keepdims=False)

    moved = [
        swap_square(block(spot ^ bit).astype(jnp.bfloat16), bit) for bit in range(1, SQUARE)
    ]
    return [block(spot)] + moved


def folded(rows, parts):
    width = rows.shape[1]
    split = rows.reshape(parts, FOLD, -1, width).transpose(0, 2, 1, 3)
    return split.reshape(-1, FOLD * width)


def unfolded_rows(rows, parts):
    width = rows.shape[1] // FOLD
    split = rows.reshape(parts, -1, FOLD, width).transpose(0, 2, 1, 3)
    return split.reshape(-1, width)


def half_of(array, which):
    width = array.shape[1] // 2
    return lax.dynamic_slice_in_dim(array, which * width, width, 1)


def half_slots(array, which):
    length = array.shape[0] // 2
    return lax.dynamic_slice_in_dim(array, which * length, length, 0)


def ordered(is_first, mine, other):
    return (jnp.where(is_first, mine, other), jnp.where(is_first, other, mine))


def on_device(
    ends_in,
    lengths,
    qkv_weight,
    qkv_bias,
    out_weight,
    up_weight,
    up_bias,
    down_weight,
    out_biases,
    norm_gains,
    norm_biases,
):
    section_index = lax.axis_index("section")
    is_first = section_index == 0
    side = section_index.astype(jnp.int32).reshape(1)
    features = ends_in.shape[2]
    width = features // 2
    count = lax.axis_size("dp")
    own_rows = ends_in[0]
    slot_count = own_rows.shape[0] // 2
    kept_rows = half_slots(own_rows, section_index)
    other_rows = swap_cores(half_slots(own_rows, 1 - section_index))
    entry, cotangent = ordered(is_first, kept_rows, other_rows)
    segment, position = layouts(
        lax.dynamic_index_in_dim(lengths, section_index, 0, keepdims=False), slot_count
    )
    tables = rotary_tables(position)
    mask = allowed_transposed(segment)

    def both(take):
        kept = take(section_index)
        other = swap_cores(take(1 - section_index))
        return ordered(is_first, kept, other)

    def take_narrow(which):
        thirds = [
            qkv_weight[0, :, part * features : (part + 1) * features] for part in range(3)
        ]
        return jnp.concatenate([half_of(part, which) for part in thirds + [out_weight[0]]], axis=1)

    pieces = (
        both(take_narrow),
        both(lambda which: half_of(up_weight[0], which)),
        both(lambda which: half_of(down_weight[0], which)),
    )

    small_shapes = [
        (qkv_bias.shape[1],),
        (up_bias.shape[1],),
        out_biases.shape[1:],
        norm_gains.shape[1:],
        norm_biases.shape[1:],
    ]
    small_own = jnp.concatenate(
        [a[0].reshape(-1) for a in (qkv_bias, up_bias, out_biases, norm_gains, norm_biases)]
    )
    small_both = jnp.concatenate(ordered(is_first, small_own, swap_cores(small_own)))
    shards = (qkv_bias.shape[1], up_bias.shape[1], norm_gains.shape[2])
    kept_forward = {}
    slabs = {}

    def attn_step(layer, rows):
        kept_forward[layer, "rows"] = rows
        made = attn_forward(side, rows, tables, mask, small[layer], *slabs[layer, "narrow"])
        kept_forward[layer, "attn"] = made
        return made

    def mlp_step(layer, kind):
        passed = kept_forward[layer, "attn"][3]
        rows = kept_forward[layer, "rows"]
        made = mlp_forward(
            side, rows, passed, small[layer], slabs[layer, "mlp"], places[layer], kind
        )
        kept_forward[layer, "mlp"] = made
        return made

    def mlp_back(layer, grad):
        rows = kept_forward[layer, "rows"]
        return mlp_backward(
            side, rows, grad, small[layer], kept_forward[layer, "mlp"][:2],
            slabs[layer, "mlp"], places[layer],
        )

    def attn_back(layer, grad, grad_mlp, kind):
        return attn_backward(
            side, kept_forward[layer, "rows"], grad, tables, mask, small[layer],
            kept_forward[layer, "attn"][:3], grad_mlp, *slabs[layer, "narrow"], kind,
        )

    def vector_of(bias_qkv, bias_up, sums):
        parts = [
            bias_qkv[half : half + 1, part * width : (part + 1) * width]
            for part in range(3)
            for half in range(2)
        ]
        order = (4, 4, 0, 1, 2, 3)
        parts += [bias_up] + [sums[index : index + 1] for index in order]
        return jnp.concatenate(parts, axis=1)

    small = []

    def spread_out(rows):
        spread = spread_small(side, rows, shards, features)
        for layer in range(2):
            made = (part[layer] for part in spread)
            small.append(dict(zip(("qkv", "up", "out", "norms"), made)))

    places = ((0, 1), (0, 1))
    if small_slice():
        narrow, up, down = pieces
        wide = [
            jnp.concatenate([up[layer], folded(down[layer], 1)], axis=1) for layer in range(2)
        ]
        lower = jnp.concatenate([narrow[0], wide[0]], axis=1)
        columns = narrow[0].shape[1]
        whole_b = gather_whole(wide[1])
        ring_a = ring_moved(lower)
        line = small_both[None]
        ring_s = ring_moved(line)
        column_s = line_placed(ring_order(), [line] + ring_s)
        column_a = column_of(lower, ring_a)
        column_a, next_c, column_s, entry, cotangent = after(
            (column_a, narrow[1], column_s, entry, cotangent), (ring_a, ring_s)
        )
        near_a = near_moved(column_a)
        square_s = square_moved(column_s)
        ring_c = ring_moved(next_c)
        column_c = column_of(next_c, ring_c)
        lows, column_c, square_s = after(
            (cut_near(near_a), column_c, square_s), (near_a, ring_c, square_s)
        )
        far_a = far_moved(lows)
        near_c = near_moved(column_c)
        rows_s = line_placed(square_order(), [column_s] + square_s)
        spread_out(rows_s.transpose(1, 0, 2, 3).reshape(PARTS, -1))
        parts_a = (column_a,) + near_a + far_a
        lows, parts_a, small = after(
            (cut_near(near_c), parts_a, small), (far_a, near_c, small, whole_b)
        )
        whole_a = place_blocks(parts_a, (columns, 2 * columns))
        far_c = far_moved(lows)
        slabs[0, "narrow"] = (whole_a[0], swap_cores(whole_a[0]))
        swapped_a = swap_cores(whole_a[1])
        slabs[0, "mlp"] = (whole_a[1], swapped_a) * 2
        attn_step(0, entry)
        (whole_c,) = place_blocks((column_c,) + near_c + far_c, (columns,))
        slabs[1, "narrow"] = (whole_c, swap_cores(whole_c))
        swapped_b = swap_cores(whole_b)
        slabs[1, "mlp"] = (whole_b, swapped_b) * 2
        mlp_step(0, jnp.bfloat16)
        attn_step(1, kept_forward[0, "mlp"][2])
        mlp_step(1, jnp.float32)
    else:
        spread_out(gather_whole(small_both[None]))
        for layer in range(2):
            narrow, up, down = (gather_whole(piece[layer]) for piece in pieces)
            wide = jnp.concatenate([up, folded(down, PARTS)], axis=1)
            slabs[layer, "narrow"] = (narrow, swap_cores(narrow))
            slabs[layer, "mlp"] = (wide, swap_cores(wide)) * 2
        attn_step(0, entry)
        mlp_step(0, jnp.bfloat16)
        attn_step(1, kept_forward[0, "mlp"][2])
        mlp_step(1, jnp.float32)
    produced = kept_forward[1, "mlp"][2]

    def mlp_pairs(made):
        return (made[0], swap_cores(made[1]), made[2], swap_cores(made[3]))

    if small_slice():
        upper = mlp_back(1, cotangent)
        pairs_a = mlp_pairs(upper)
        upper_attn = attn_back(1, cotangent, upper[5], jnp.bfloat16)
        leaving_a = far_blocks(after(pairs_a, upper_attn[2]))
        far_a = sent_both(leaving_a)
        grad_middle = after(upper_attn[4], leaving_a)
        received_b = swap_cores(upper_attn[1])
        lower = mlp_back(0, grad_middle)
        leaving_a = near_blocks(pairs_a, after(far_a, lower[4]))
        near_a = sent_both(leaving_a)
        steps_b = ring_steps(upper_attn[0], after(received_b, lower[4]))
        moved_b = next(steps_b)
        pairs_c = mlp_pairs(lower)
        lower_attn = attn_back(
            0, grad_middle, after(lower[5], (leaving_a, received_b)), jnp.float32
        )
        pairs_d = (lower_attn[0], swap_cores(lower_attn[1]))
        moved_b = next(steps_b)
        pairs_c = after(pairs_c, (lower_attn[2], near_a))
        far_c = sent_both(far_blocks(pairs_c))
        pairs_d = after(pairs_d, near_a)
        far_d = sent_both(far_blocks(pairs_d))
        moved_b = next(steps_b)
        parts_a = column_sent(pairs_a, after(near_a, far_c))
        near_c = sent_both(near_blocks(pairs_c, after(far_c, far_d)))
        blocks_b = next(steps_b)
        near_d = sent_both(near_blocks(pairs_d, after(far_d, near_c)))
        parts_c = column_sent(pairs_c, near_c)
        parts_b = square_sent(after(blocks_b, near_c))
        parts_d = column_sent(pairs_d, after(near_d, near_c))
        reduced = (
            (total_of(parts_d), total_of(parts_b)),
            (total_of(parts_c), total_of(parts_a)),
        )
    else:
        upper = mlp_back(1, cotangent)
        upper_attn = attn_back(1, cotangent, upper[5], jnp.bfloat16)
        lower = mlp_back(0, upper_attn[4])
        lower_attn = attn_back(0, upper_attn[4], lower[5], jnp.float32)

        def spread(kept, received):
            summed = kept.astype(jnp.float32) + received.astype(jnp.float32)
            return lax.psum_scatter(summed, "dp", scatter_dimension=0, tiled=True)

        def spread_mlp(made):
            up_kept, up_got, down_kept, down_got = mlp_pairs(made)
            down = spread(unfolded_rows(down_kept, PARTS), unfolded_rows(down_got, PARTS))
            return jnp.concatenate([spread(up_kept, up_got), folded(down, 1)], axis=1)

        reduced = (
            tuple(spread(made[0], swap_cores(made[1])) for made in (lower_attn, upper_attn)),
            tuple(spread_mlp(made) for made in (lower, upper)),
        )
    grad_entry = lower_attn[4]
    def finish(lower, upper):
        mine, leaving = ordered(is_first, lower, upper)
        return ordered(is_first, mine, swap_cores(leaving))

    narrow_halves, mlp_halves = (finish(*pair) for pair in reduced)
    up_width = up_weight.shape[2] // 2
    total_up = jnp.concatenate([part[:, :up_width] for part in mlp_halves], axis=1)
    total_down = jnp.concatenate(
        [unfolded_rows(part[:, up_width:], 1) for part in mlp_halves], axis=1
    )
    total_qkv = jnp.concatenate(
        [
            part[:, at * width : (at + 1) * width]
            for at in range(3)
            for part in narrow_halves
        ],
        axis=1,
    )
    total_out = jnp.concatenate([part[:, 3 * width :] for part in narrow_halves], axis=1)

    vectors = [
        vector_of(attn[2], mlp[4], attn[3])
        for mlp, attn in ((lower, lower_attn), (upper, upper_attn))
    ]
    vector_kept, vector_sent = ordered(is_first, *vectors)
    if small_slice():
        vector = vector_kept + swap_cores(vector_sent)
        vector = total_of([vector] + square_moved(vector))
        vector = total_of([vector] + ring_moved(after(vector, near_c)))
    else:
        vector = lax.psum(vector_kept + swap_cores(vector_sent), "dp")
    place = lax.axis_index("dp")
    small_outs = []
    at = 0
    for shape in small_shapes:
        lead, size = (1,) if len(shape) == 1 else (shape[0],), shape[-1]
        rows = vector[0, at : at + lead[0] * size * count].reshape(lead[0], count * size)
        at += lead[0] * size * count
        part = lax.dynamic_slice_in_dim(rows, place * size, size, 1)
        small_outs.append(part.reshape((1,) + shape))

    staying, leaving = ordered(is_first, grad_entry, produced)
    ends_out = jnp.concatenate(ordered(is_first, staying, swap_cores(leaving)))
    return (
        ends_out[None],
        total_qkv[None],
        small_outs[0],
        total_out[None],
        total_up[None],
        small_outs[1],
        total_down[None],
        small_outs[2],
        small_outs[3],
        small_outs[4],
    )


def solution(mesh):
    return jax.shard_map(
        on_device,
        mesh=mesh,
        in_specs=(
            P("section", "dp", None),
            P("dp", None),
            P("section", "dp", None),
            P("section", "dp"),
            P("section", "dp", None),
            P("section", "dp", None),
            P("section", "dp"),
            P("section", "dp", None),
            P("section", None, "dp"),
            P("section", None, "dp"),
            P("section", None, "dp"),
        ),
        out_specs=(
            P("section", "dp", None),
            P("section", "dp", None),
            P("section", "dp"),
            P("section", "dp", None),
            P("section", "dp", None),
            P("section", "dp"),
            P("section", "dp", None),
            P("section", None, "dp"),
            P("section", None, "dp"),
            P("section", None, "dp"),
        ),
        check_vma=False,
    )
```

```python
import math

import jax
import jax.numpy as jnp
import numpy as np
from jax import lax
from jax.experimental import pallas as pl
from jax.experimental.pallas import tpu as pltpu
from jax.sharding import PartitionSpec as P

HD = 64
ROT = 16
LANES = 128
TILES = 2
FOLD = 4
PARTS = 16


eps = 1e-05
masked_score = -1e30
vmem_bytes = 48 * 1024 * 1024


def product(left, right):
    return jnp.dot(left, right, preferred_element_type=jnp.float32)


def product_transposed(left, right):
    return lax.dot_general(
        left, right, (((1,), (1,)), ((), ())), preferred_element_type=jnp.float32
    )


def layouts(lengths, slot_count):
    ends_at = jnp.cumsum(lengths)
    indices = jnp.arange(slot_count, dtype=jnp.int32)
    passed = indices[:, None] >= ends_at[None, :]
    segments = jnp.sum(passed.astype(jnp.int32), axis=1)
    starts = jnp.sum(jnp.where(passed, lengths[None, :], 0), axis=1)
    return (segments, indices - starts)


def rotary_tables(positions):
    lane = jnp.arange(LANES, dtype=jnp.int32) % HD
    half = ROT // 2
    freqs = 10000.0 ** (-2.0 * (lane % half).astype(jnp.float32) / ROT)
    angles = positions.astype(jnp.float32)[:, None] * freqs[None, :]
    cosine = jnp.where(lane < ROT, jnp.cos(angles), 1.0)
    sine = jnp.sin(angles)
    ahead = jnp.where(lane < half, -sine, 0.0)
    behind = jnp.where((lane >= half) & (lane < ROT), sine, 0.0)
    return jnp.stack([cosine, ahead, behind])


def allowed_transposed(segment):
    indices = jnp.arange(segment.shape[0], dtype=jnp.int32)
    allowed = (segment[:, None] == segment[None, :]) & (indices[:, None] <= indices[None, :])
    return allowed.astype(jnp.float32)


def turned(values, tables, back):
    half = ROT // 2
    parts = []
    for at in range(0, values.shape[1], LANES):
        part = values[:, at : at + LANES]
        moved = (
            pltpu.roll(part, LANES - half, 1) * tables[1] + pltpu.roll(part, half, 1) * tables[2]
        )
        kept = part * tables[0]
        parts.append(kept - moved if back else kept + moved)
    return jnp.concatenate(parts, axis=1)


def unit_rows(rows):
    centred = rows - jnp.mean(rows, axis=-1, keepdims=True)
    spread = jnp.mean(centred * centred, axis=-1, keepdims=True)
    scale = lax.rsqrt(spread + eps)
    return (centred * scale, scale)


def lane_half(which, width):
    return pl.ds(pl.multiple_of(which * width, LANES), width)


def head_lanes(values, which):
    lane = lax.broadcasted_iota(jnp.int32, values.shape, 1)
    return jnp.where((lane < HD) == (which == 0), values, jnp.zeros_like(values))


def scores_of(key_pair, query_pair, which, allowed):
    scores = product_transposed(head_lanes(key_pair, which), query_pair) * (1.0 / math.sqrt(HD))
    return jnp.where(allowed, scores, masked_score)


def attn_forward_kernel(
    side, rows, tables, mask, norms, bias_qkv, bias_out, mine, other, qkv, logs, attended, passed
):
    width = mine.shape[1] // 4
    entry = rows[...].astype(jnp.float32)
    unit, _ = unit_rows(entry)
    normed = (unit * norms[0:1] + norms[2:3]).astype(jnp.bfloat16)
    allowed = mask[...] > 0.5
    for at, weight in enumerate((mine, other)):
        half = side[0] if at == 0 else 1 - side[0]
        parts = []
        for part in range(3):
            cut = slice(part * width, (part + 1) * width)
            value = product(normed, weight[:, cut]) + bias_qkv[at : at + 1, cut]
            if part < 2:
                value = turned(value, tables, False)
            value = value.astype(jnp.bfloat16)
            qkv[at, :, cut] = value
            parts.append(value)
        queries, keys, values = parts
        values = values.T
        outs = []
        for pair in range(width // LANES):
            cut = slice(pair * LANES, (pair + 1) * LANES)
            for which in range(2):
                head = 2 * pair + which
                scores = scores_of(keys[:, cut], queries[:, cut], which, allowed)
                peak = jnp.max(scores, axis=0, keepdims=True)
                raised = jnp.exp(scores - peak)
                total = jnp.sum(raised, axis=0, keepdims=True)
                chances = (raised * (1.0 / total)).astype(jnp.bfloat16)
                outs.append(product(values[head * HD : (head + 1) * HD], chances))
                logs[at, head : head + 1, :] = peak + jnp.log(total)
        mixed = jnp.concatenate(outs, axis=0).T.astype(jnp.bfloat16)
        attended[:, lane_half(half, width)] = mixed
    mixed = attended[...]
    for at, weight in enumerate((mine, other)):
        half = side[0] if at == 0 else 1 - side[0]
        lanes = lane_half(half, width)
        passed[:, lanes] = (
            rows[:, lanes].astype(jnp.float32)
            + product(mixed, weight[:, 3 * width :])
            + bias_out[0:1, lanes]
        )


def fixed(*shape):
    return pl.BlockSpec(shape, lambda *at: (0,) * len(shape))


def fixed_like(*arrays):
    return [fixed(*array.shape) for array in arrays]


def attn_forward(side, rows, tables, mask, small, mine, other):
    length, features = rows.shape
    width = features // 2
    heads = width // HD
    return pl.pallas_call(
        attn_forward_kernel,
        out_shape=(
            jax.ShapeDtypeStruct((2, length, 3 * width), jnp.bfloat16),
            jax.ShapeDtypeStruct((2, heads, length), jnp.float32),
            jax.ShapeDtypeStruct((length, features), jnp.bfloat16),
            jax.ShapeDtypeStruct((length, features), jnp.float32),
        ),
        grid=(1,),
        in_specs=[pl.BlockSpec(memory_space=pltpu.SMEM)]
        + fixed_like(rows, tables, mask, small["norms"], small["qkv"], small["out"])
        + [fixed(features, 4 * width)] * 2,
        out_specs=(
            fixed(2, length, 3 * width),
            fixed(2, heads, length),
            fixed(length, features),
            fixed(length, features),
        ),
        compiler_params=pltpu.CompilerParams(vmem_limit_bytes=vmem_bytes),
        cost_estimate=pl.CostEstimate(
            flops=2 * length * features * features * 30,
            bytes_accessed=8 * features * features,
            transcendentals=length * length * features // HD,
        ),
        name="attn_forward",
    )(side, rows, tables, mask, small["norms"], small["qkv"], small["out"], mine, other)


def tile_of(step, side):
    half = jnp.where(step < TILES, side[0], 1 - side[0])
    return half * TILES + step % TILES


def first_tile(step):
    return jnp.minimum(step, TILES - 1)


def second_tile(step):
    return jnp.maximum(step - TILES, 0)


def folded_cuts(shape, width):
    rows = 2 * width // PARTS
    for part in range(shape[0] // rows):
        for column in range(shape[1] // width):
            yield (
                slice(part * rows, (part + 1) * rows),
                slice(column * width, (column + 1) * width),
            )


def unfolded(block, width):
    return jnp.concatenate([block[cut] for cut in folded_cuts(block.shape, width)], axis=0)


def down_joined(mine, other, width):
    return jnp.concatenate([unfolded(mine, width), unfolded(other, width)], axis=1)


def mlp_forward_kernel(
    side, rows, passed, norms, bias_up, bias_out, up_mine, up_other, down_mine, down_other,
    active, slope, produced, normed, total
):
    step = pl.program_id(0)

    @pl.when(step == 0)
    def _():
        unit, _ = unit_rows(rows[...].astype(jnp.float32))
        normed[...] = (unit * norms[1:2] + norms[3:4]).astype(jnp.bfloat16)
        total[...] = jnp.zeros_like(total)

    weight = jnp.where(step < TILES, up_mine[...], up_other[...])
    hidden = product(normed[...], weight) + bias_up[...]
    bell = 0.5 * (1.0 + lax.erf(hidden * (1.0 / math.sqrt(2.0))))
    density = jnp.exp(-0.5 * hidden * hidden) * (1.0 / math.sqrt(2.0 * math.pi))
    slope[...] = bell + hidden * density
    lit = (hidden * bell).astype(jnp.bfloat16)
    active[...] = lit
    width = total.shape[1] // 2
    total[...] += product(lit, down_joined(down_mine, down_other, width))

    @pl.when(step == 2 * TILES - 1)
    def _():
        for at, half in enumerate((side[0], 1 - side[0])):
            lanes = lane_half(half, width)
            part = total[:, at * width : (at + 1) * width]
            produced[:, lanes] = (
                passed[:, lanes] + part + bias_out[1:2, lanes]
            ).astype(produced.dtype)


def mlp_forward(side, rows, passed, small, weights, places, kind):
    up_mine, up_other, down_mine, down_other = weights
    up_at, down_at = places
    length, features = rows.shape
    width = features // 2
    tile = FOLD * width // TILES
    hidden = 2 * TILES * tile
    folded = features // (2 * TILES)
    tiled = pl.BlockSpec((length, tile), lambda step, side: (0, tile_of(step, side)))
    down_spec = pl.BlockSpec(
        (folded, FOLD * width), lambda step, side: (tile_of(step, side), down_at)
    )
    return pl.pallas_call(
        mlp_forward_kernel,
        out_shape=(
            jax.ShapeDtypeStruct((length, hidden), jnp.bfloat16),
            jax.ShapeDtypeStruct((length, hidden), jnp.float32),
            jax.ShapeDtypeStruct((length, features), kind),
        ),
        grid_spec=pltpu.PrefetchScalarGridSpec(
            num_scalar_prefetch=1,
            grid=(2 * TILES,),
            in_specs=[
                fixed(length, features),
                fixed(length, features),
                fixed(4, features),
                pl.BlockSpec((1, tile), lambda step, side: (0, tile_of(step, side))),
                fixed(2, features),
                pl.BlockSpec((features, tile), lambda step, side: (0, up_at + first_tile(step))),
                pl.BlockSpec((features, tile), lambda step, side: (0, up_at + second_tile(step))),
                down_spec,
                down_spec,
            ],
            out_specs=(tiled, tiled, fixed(length, features)),
            scratch_shapes=[
                pltpu.VMEM((length, features), jnp.bfloat16),
                pltpu.VMEM((length, features), jnp.float32),
            ],
        ),
        compiler_params=pltpu.CompilerParams(vmem_limit_bytes=vmem_bytes),
        cost_estimate=pl.CostEstimate(
            flops=20 * length * features * hidden,
            bytes_accessed=4 * features * hidden + 6 * length * hidden,
            transcendentals=2 * length * hidden,
        ),
        name="mlp_forward",
    )(
        side, rows, passed, small["norms"], small["up"], small["out"],
        up_mine, up_other, down_mine, down_other,
    )


def mlp_backward_kernel(
    side, rows, grad, norms, active, slope, up_mine, up_other, down_mine, down_other,
    up_kept, up_sent, down_kept, down_sent, bias_grad, grad_normed, normed, grads
):
    step = pl.program_id(0)
    width = grad.shape[1] // 2
    cuts = list(folded_cuts(down_mine.shape, width))

    @pl.when(step == 0)
    def _():
        unit, _ = unit_rows(rows[...].astype(jnp.float32))
        normed[...] = (unit * norms[1:2] + norms[3:4]).T.astype(jnp.bfloat16)
        grad_normed[...] = jnp.zeros_like(grad_normed)
        grads[:, :width] = grad[:, lane_half(side[0], width)]
        grads[:, width:] = grad[:, lane_half(1 - side[0], width)]

    weight = jnp.where(step < TILES, up_mine[...], up_other[...])
    lit = active[...].T
    made = product(lit, grads[...]).astype(jnp.bfloat16)
    rows_each = made.shape[0] // len(cuts)
    for index, cut in enumerate(cuts):
        part = made[index * rows_each : (index + 1) * rows_each]
        down_kept[cut] = part[:, :width]
        down_sent[cut] = part[:, width:]
    back = product_transposed(grads[...], down_joined(down_mine, down_other, width))
    back = (back * slope[...]).astype(jnp.bfloat16)
    bias_grad[...] = jnp.sum(back.astype(jnp.float32), axis=0, keepdims=True)
    up_grad = product(normed[...], back).astype(jnp.bfloat16)

    @pl.when(step < TILES)
    def _():
        up_kept[...] = up_grad

    @pl.when(step >= TILES)
    def _():
        up_sent[...] = up_grad

    grad_normed[...] += product_transposed(back, weight)


def mlp_backward(side, rows, grad, small, saved, weights, places):
    active, slope = saved
    up_mine, up_other, down_mine, down_other = weights
    up_at, down_at = places
    length, features = rows.shape
    width = features // 2
    tile = FOLD * width // TILES
    hidden = 2 * TILES * tile
    folded = features // (2 * TILES)
    tiled = pl.BlockSpec((length, tile), lambda step, side: (0, tile_of(step, side)))
    down_spec = pl.BlockSpec(
        (folded, FOLD * width), lambda step, side: (tile_of(step, side), down_at)
    )
    up_first = pl.BlockSpec((features, tile), lambda step, side: (0, first_tile(step)))
    up_second = pl.BlockSpec((features, tile), lambda step, side: (0, second_tile(step)))
    down_out = pl.BlockSpec(
        (folded, FOLD * width), lambda step, side: (tile_of(step, side), 0)
    )
    return pl.pallas_call(
        mlp_backward_kernel,
        out_shape=(
            jax.ShapeDtypeStruct((features, hidden // 2), jnp.bfloat16),
            jax.ShapeDtypeStruct((features, hidden // 2), jnp.bfloat16),
            jax.ShapeDtypeStruct((features, FOLD * width), jnp.bfloat16),
            jax.ShapeDtypeStruct((features, FOLD * width), jnp.bfloat16),
            jax.ShapeDtypeStruct((1, hidden), jnp.float32),
            jax.ShapeDtypeStruct((length, features), jnp.float32),
        ),
        grid_spec=pltpu.PrefetchScalarGridSpec(
            num_scalar_prefetch=1,
            grid=(2 * TILES,),
            in_specs=[
                fixed(length, features),
                fixed(length, features),
                fixed(4, features),
                tiled,
                tiled,
                pl.BlockSpec((features, tile), lambda step, side: (0, up_at + first_tile(step))),
                pl.BlockSpec((features, tile), lambda step, side: (0, up_at + second_tile(step))),
                down_spec,
                down_spec,
            ],
            out_specs=(
                up_first,
                up_second,
                down_out,
                down_out,
                pl.BlockSpec((1, tile), lambda step, side: (0, tile_of(step, side))),
                fixed(length, features),
            ),
            scratch_shapes=[
                pltpu.VMEM((features, length), jnp.bfloat16),
                pltpu.VMEM((length, features), jnp.bfloat16),
            ],
        ),
        compiler_params=pltpu.CompilerParams(vmem_limit_bytes=vmem_bytes),
        cost_estimate=pl.CostEstimate(
            flops=32 * length * features * hidden,
            bytes_accessed=8 * features * hidden + 6 * length * hidden,
            transcendentals=0,
        ),
        name="mlp_backward",
    )(
        side, rows, grad, small["norms"], active, slope,
        up_mine, up_other, down_mine, down_other,
    )


def attn_backward_kernel(
    side, rows, grad, tables, mask, norms, qkv, logs, attended, grad_mlp, mine, other,
    kept, sent, bias_grad, sums, passed, mixed_back
):
    width = mine.shape[1] // 4
    unit, scale = unit_rows(rows[...].astype(jnp.float32))
    normed = (unit * norms[0:1] + norms[2:3]).T.astype(jnp.bfloat16)
    allowed = mask[...] > 0.5
    mixed = attended[...].T
    back = None
    for at, (weight, result) in enumerate(((mine, kept), (other, sent))):
        half = side[0] if at == 0 else 1 - side[0]
        part = grad[:, lane_half(half, width)]
        result[:, 3 * width :] = product(mixed, part).astype(jnp.bfloat16)
        term = product_transposed(part, weight[:, 3 * width :])
        back = term if back is None else back + term
    mixed_back[...] = back.astype(jnp.bfloat16)
    grad_attn = None
    for at, (weight, result) in enumerate(((mine, kept), (other, sent))):
        half = side[0] if at == 0 else 1 - side[0]
        queries = qkv[at, :, 0:width]
        keys = qkv[at, :, width : 2 * width]
        values = qkv[at, :, 2 * width :]
        keys_turned = keys.T
        grad_out = mixed_back[:, lane_half(half, width)]
        query_grads, key_grads, value_grads = [], [], []
        for pair in range(width // LANES):
            cut = slice(pair * LANES, (pair + 1) * LANES)
            key_pair, value_pair = [], []
            for which in range(2):
                head = 2 * pair + which
                scores = scores_of(keys[:, cut], queries[:, cut], which, allowed)
                chances = jnp.exp(scores - logs[at, head : head + 1, :])
                value_pair.append(product(chances.astype(jnp.bfloat16), grad_out[:, cut]))
                slopes = product_transposed(head_lanes(values[:, cut], which), grad_out[:, cut])
                inner = jnp.sum(slopes * chances, axis=0, keepdims=True)
                slopes = (chances * (slopes - inner)).astype(jnp.bfloat16)
                key_pair.append(product(slopes, queries[:, cut]))
                query_grads.append(product(keys_turned[head * HD : (head + 1) * HD], slopes))
            lane = lax.broadcasted_iota(jnp.int32, key_pair[0].shape, 1)
            key_grads.append(jnp.where(lane < HD, key_pair[0], key_pair[1]))
            value_grads.append(jnp.where(lane < HD, value_pair[0], value_pair[1]))
        factor = 1.0 / math.sqrt(HD)
        query_grad = turned(jnp.concatenate(query_grads, axis=0).T * factor, tables, True)
        key_grad = turned(jnp.concatenate(key_grads, axis=1) * factor, tables, True)
        value_grad = jnp.concatenate(value_grads, axis=1)
        for index, part in enumerate((query_grad, key_grad, value_grad)):
            cut = slice(index * width, (index + 1) * width)
            part = part.astype(jnp.bfloat16)
            bias_grad[pl.ds(half, 1), cut] = jnp.sum(
                part.astype(jnp.float32), axis=0, keepdims=True
            )
            result[:, cut] = product(normed, part).astype(jnp.bfloat16)
            term = product_transposed(part, weight[:, cut])
            grad_attn = term if grad_attn is None else grad_attn + term
    grad_up = grad_mlp[...]
    grad_rows = grad[...].astype(jnp.float32)
    sums[0:1] = jnp.sum(unit * grad_attn, axis=0, keepdims=True)
    sums[1:2] = jnp.sum(unit * grad_up, axis=0, keepdims=True)
    sums[2:3] = jnp.sum(grad_attn, axis=0, keepdims=True)
    sums[3:4] = jnp.sum(grad_up, axis=0, keepdims=True)
    sums[4:5] = jnp.sum(grad_rows, axis=0, keepdims=True)
    inward = grad_attn * norms[0:1] + grad_up * norms[1:2]
    level = jnp.mean(inward, axis=-1, keepdims=True)
    along = jnp.mean(inward * unit, axis=-1, keepdims=True)
    passed[...] = (grad_rows + (inward - level - unit * along) * scale).astype(passed.dtype)


def attn_backward(side, rows, grad, tables, mask, small, saved, grad_mlp, mine, other, kind):
    qkv, logs, attended = saved
    length, features = rows.shape
    return pl.pallas_call(
        attn_backward_kernel,
        out_shape=(
            jax.ShapeDtypeStruct((features, 2 * features), jnp.bfloat16),
            jax.ShapeDtypeStruct((features, 2 * features), jnp.bfloat16),
            jax.ShapeDtypeStruct((2, 3 * features // 2), jnp.float32),
            jax.ShapeDtypeStruct((5, features), jnp.float32),
            jax.ShapeDtypeStruct((length, features), kind),
        ),
        grid=(1,),
        in_specs=[pl.BlockSpec(memory_space=pltpu.SMEM)]
        + fixed_like(rows, grad, tables, mask, small["norms"], qkv, logs, attended, grad_mlp)
        + [fixed(features, 2 * features)] * 2,
        out_specs=(
            fixed(features, 2 * features),
            fixed(features, 2 * features),
            fixed(2, 3 * features // 2),
            fixed(5, features),
            fixed(length, features),
        ),
        scratch_shapes=[pltpu.VMEM((length, features), jnp.bfloat16)],
        compiler_params=pltpu.CompilerParams(vmem_limit_bytes=vmem_bytes),
        cost_estimate=pl.CostEstimate(
            flops=2 * length * features * features * 48,
            bytes_accessed=16 * features * features,
            transcendentals=length * length * features // HD,
        ),
        name="attn_backward",
    )(
        side, rows, grad, tables, mask, small["norms"], qkv, logs, attended, grad_mlp, mine, other
    )


SQUARE = 4
RING = 4


def swap_cores(value):
    return lax.ppermute(value, "section", [(0, 1), (1, 0)])


def swap_square(value, bit):
    count = lax.axis_size("dp")
    return lax.ppermute(value, "dp", [(i, i ^ bit) for i in range(count)])


def shift_ring(value, steps):
    count = lax.axis_size("dp")
    pairs = [(i, (i + SQUARE * steps) % count) for i in range(count)]
    return lax.ppermute(value, "dp", pairs)


def small_slice():
    return lax.axis_size("dp") == SQUARE * RING


def after(values, earlier):
    flat, shape = jax.tree.flatten(values)
    waited = jax.tree.leaves(earlier)
    tied = lax.optimization_barrier(tuple(flat) + tuple(waited))
    return jax.tree.unflatten(shape, tied[: len(flat)])


def own_place():
    place = lax.axis_index("dp").astype(jnp.int32)
    return (place // SQUARE, place % SQUARE)


def any_space(count):
    return [pl.BlockSpec(memory_space=pl.ANY)] * count


def place_kernel(spot_ref, *refs):
    blocks, outs, sems = refs[:5], refs[5:-1], refs[-1]
    own, first, second, far_low, far_high = blocks
    spot = spot_ref[0]
    half = RING // 2
    copies = []
    at = 0
    for index, out in enumerate(outs):
        lanes = pl.ds(at, out.shape[3])
        at += out.shape[3]
        pairs = (
            (own, out.at[:, spot]),
            (first, out.at[:, spot ^ 1]),
            (second, out.at[:, spot ^ 2]),
            (far_low, out.at[pl.ds(0, half), spot ^ 3]),
            (far_high, out.at[pl.ds(half, half), spot ^ 3]),
        )
        for place, (block, target) in enumerate(pairs):
            copies.append(
                pltpu.make_async_copy(
                    block.at[:, :, lanes], target, sems.at[5 * index + place]
                )
            )
    for copy in copies:
        copy.start()
    for copy in copies:
        copy.wait()


def place_blocks(blocks, widths):
    spot = own_place()[1].reshape(1)
    rows = blocks[0].shape[1]
    placed = pl.pallas_call(
        place_kernel,
        out_shape=tuple(
            jax.ShapeDtypeStruct((RING, SQUARE, rows, columns), blocks[0].dtype)
            for columns in widths
        ),
        in_specs=[pl.BlockSpec(memory_space=pltpu.SMEM)] + any_space(5),
        out_specs=tuple([pl.BlockSpec(memory_space=pltpu.VMEM)] * len(widths)),
        scratch_shapes=[pltpu.SemaphoreType.DMA((5 * len(widths),))],
        compiler_params=pltpu.CompilerParams(vmem_limit_bytes=vmem_bytes),
        name="place_blocks",
    )(spot, *blocks)
    return [part.reshape(PARTS * rows, -1) for part in placed]


def line_kernel(order_ref, *refs):
    held, out, sems = refs[:-2], refs[-2], refs[-1]
    copies = [
        pltpu.make_async_copy(part, out.at[order_ref[at]], sems.at[at])
        for at, part in enumerate(held)
    ]
    for copy in copies:
        copy.start()
    for copy in copies:
        copy.wait()


def line_placed(order, held):
    return pl.pallas_call(
        line_kernel,
        out_shape=jax.ShapeDtypeStruct((len(held),) + held[0].shape, held[0].dtype),
        in_specs=[pl.BlockSpec(memory_space=pltpu.SMEM)] + any_space(len(held)),
        out_specs=pl.BlockSpec(memory_space=pltpu.VMEM),
        scratch_shapes=[pltpu.SemaphoreType.DMA((len(held),))],
        compiler_params=pltpu.CompilerParams(vmem_limit_bytes=vmem_bytes),
        name="place_line",
    )(order, *held)


def ring_order():
    return (own_place()[0] + RING - jnp.arange(RING, dtype=jnp.int32)) % RING


def square_order():
    return own_place()[1] ^ jnp.arange(SQUARE, dtype=jnp.int32)


def gather_whole(piece):
    return lax.all_gather(piece, "dp", axis=0, tiled=True)


def ring_moved(piece):
    return [shift_ring(piece, steps) for steps in range(1, RING)]


def square_moved(piece):
    return [swap_square(piece, bit) for bit in range(1, SQUARE)]


def column_of(piece, moved):
    return line_placed(ring_order(), [piece] + moved)


def near_moved(column):
    return (swap_square(column, 1), swap_square(column, 2))


def cut_near(near):
    half = RING // 2
    return (near[0][:half], near[1][half:])


def far_moved(lows):
    return (swap_square(lows[0], 2), swap_square(lows[1], 1))


def ring_around(blocks):
    held = [blocks]
    for _ in range(RING - 1):
        held.append(shift_ring(held[-1], 1))
    return held


def spread_kernel(side, rows, *refs):
    picks, outs = refs[:6], refs[6:]
    count = rows.shape[0]
    width = outs[0].shape[2] // 3
    size = rows.shape[1] // 2

    def row(at, which):
        pick, keep = picks[2 * which], picks[2 * which + 1]
        found = product(rows[:, at : at + pick.shape[0]], pick[...])
        return jnp.sum(found * keep[...], axis=0, keepdims=True)

    for layer in range(2):
        at = layer * size
        found = row(at, 0)
        for half in range(2):
            parts = [
                found[:, (2 * part + half) * width : (2 * part + half + 1) * width]
                for part in range(3)
            ]
            outs[0][layer, pl.ds(half ^ side[0], 1), :] = jnp.concatenate(parts, axis=1)
        at += picks[0].shape[0]
        outs[1][layer] = row(at, 1)
        at += picks[2].shape[0]
        step = picks[4].shape[0]
        for index in range(2):
            outs[2][layer, index : index + 1, :] = row(at + index * step, 2)
        for index in range(4):
            outs[3][layer, index : index + 1, :] = row(at + (2 + index) * step, 2)


def spread_small(side, rows, shards, features):
    count = rows.shape[0]
    picks = []
    for shard in shards:
        lane = np.arange(count * shard)
        picks.append(jnp.asarray(np.arange(shard)[:, None] == lane % shard, jnp.bfloat16))
        picks.append(jnp.asarray(np.arange(count)[:, None] == lane // shard, jnp.float32))
    shapes = (
        (2, 2, 3 * features // 2),
        (2, 1, count * shards[1]),
        (2, 2, features),
        (2, 4, features),
    )
    outs = [jax.ShapeDtypeStruct(shape, jnp.float32) for shape in shapes]
    return pl.pallas_call(
        spread_kernel,
        out_shape=tuple(outs),
        grid=(1,),
        in_specs=[pl.BlockSpec(memory_space=pltpu.SMEM)] + fixed_like(rows, *picks),
        out_specs=tuple(fixed_like(*outs)),
        compiler_params=pltpu.CompilerParams(vmem_limit_bytes=vmem_bytes),
        name="spread_small",
    )(side, rows, *picks)


def far_kernel(place_ref, *refs):
    pairs, (low, high) = refs[:-2], refs[-2:]
    half = RING // 2
    columns = pairs[0].shape[-1]
    for at in range(0, len(pairs), 2):
        cut = slice(at // 2 * columns, (at // 2 + 1) * columns)
        total = pairs[at][...].astype(jnp.float32) + pairs[at + 1][...].astype(jnp.float32)
        total = total[:, 0].astype(low.dtype)
        low[:, :, cut] = total[:half]
        high[:, :, cut] = total[half:]


def near_kernel(place_ref, *refs):
    pairs, (far_low, far_high), (first, second) = refs[:-4], refs[-4:-2], refs[-2:]
    half = RING // 2
    columns = pairs[0].shape[-1]
    for at in range(0, len(pairs), 4):
        cut = slice(at // 4 * columns, (at // 4 + 1) * columns)
        one, two, three, four = (pair[...].astype(jnp.float32)[:, 0] for pair in pairs[at : at + 4])
        total = one + two
        first[:half, :, cut] = total[:half].astype(first.dtype)
        high = far_high[:, :, cut].astype(jnp.float32)
        first[half:, :, cut] = (total[half:] + high).astype(first.dtype)
        total = three + four
        low = far_low[:, :, cut].astype(jnp.float32)
        second[:half, :, cut] = (total[:half] + low).astype(first.dtype)
        second[half:, :, cut] = total[half:].astype(first.dtype)


def column_kernel(place_ref, *refs):
    pairs, (first, second), outs = refs[: -2 - RING], refs[-2 - RING : -RING], refs[-RING:]
    columns = pairs[0].shape[-1]
    for steps, out in enumerate(outs):
        level = lax.rem(place_ref[0] + steps, RING)
        for at in range(0, len(pairs), 2):
            cut = slice(at // 2 * columns, (at // 2 + 1) * columns)
            total = pairs[at][level, 0].astype(jnp.float32)
            total += pairs[at + 1][level, 0].astype(jnp.float32)
            total += first[level, :, cut].astype(jnp.float32)
            total += second[level, :, cut].astype(jnp.float32)
            out[:, cut] = total.astype(out.dtype)


def block_spec(rows, columns, bit):
    return pl.BlockSpec(
        (RING, 1, rows, columns), lambda step, place: (0, place[1] ^ bit, 0, 0)
    )


def scatter_call(body, name, pairs, bits, extra, outs):
    rows, columns = pairs[0].shape[0] // PARTS, pairs[0].shape[1]
    blocks, specs = [], []
    for at in range(0, len(pairs), 2):
        for bit in bits:
            for array in pairs[at : at + 2]:
                blocks.append(array.reshape(RING, SQUARE, rows, columns))
                specs.append(block_spec(rows, columns, bit))
    return pl.pallas_call(
        body,
        out_shape=tuple(outs),
        grid_spec=pltpu.PrefetchScalarGridSpec(
            num_scalar_prefetch=1,
            grid=(1,),
            in_specs=specs + fixed_like(*extra),
            out_specs=tuple(fixed_like(*outs)),
        ),
        compiler_params=pltpu.CompilerParams(vmem_limit_bytes=vmem_bytes),
        name=name,
    )(jnp.stack(own_place()), *blocks, *extra)


def wide_shape(pairs, count, kind=jnp.bfloat16):
    rows, columns = pairs[0].shape[0] // PARTS, pairs[0].shape[1] * len(pairs) // 2
    lead = (count,) if count else ()
    return jax.ShapeDtypeStruct(lead + (rows, columns), kind)


def far_blocks(pairs):
    half = wide_shape(pairs, RING // 2)
    return scatter_call(far_kernel, "far_blocks", pairs, (3,), (), [half, half])


def near_blocks(pairs, far):
    full = wide_shape(pairs, RING)
    return scatter_call(near_kernel, "near_blocks", pairs, (1, 2), far, [full, full])


def sent_both(blocks):
    return (swap_square(blocks[0], 1), swap_square(blocks[1], 2))


def column_sent(pairs, near):
    outs = [wide_shape(pairs, 0, jnp.float32)] + [wide_shape(pairs, 0)] * (RING - 1)
    own, *leaving = scatter_call(column_kernel, "column_blocks", pairs, (0,), near, outs)
    return [own] + [shift_ring(part, steps + 1) for steps, part in enumerate(leaving)]


def total_of(parts):
    total = parts[0].astype(jnp.float32)
    for part in parts[1:]:
        total = total + part.astype(jnp.float32)
    return total


def ring_steps(kept, received):
    rows, columns = kept.shape[0] // PARTS, kept.shape[1]
    kept = kept.reshape(RING, SQUARE, rows, columns)
    received = received.reshape(RING, SQUARE, rows, columns)
    level, _ = own_place()

    def rung(back):
        index = (level + RING - back) % RING
        parts = [lax.dynamic_index_in_dim(array, index, 0, False) for array in (kept, received)]
        return total_of(parts)

    moving = rung(1).astype(jnp.bfloat16)
    for step in range(1, RING):
        moved = shift_ring(moving, 1)
        yield moved
        total = moved.astype(jnp.float32) + rung(step + 1)
        moving = total.astype(jnp.bfloat16)
    yield total


def square_sent(blocks):
    _, spot = own_place()

    def block(index):
        return lax.dynamic_index_in_dim(blocks, index, 0, keepdims=False)

    moved = [
        swap_square(block(spot ^ bit).astype(jnp.bfloat16), bit) for bit in range(1, SQUARE)
    ]
    return [block(spot)] + moved


def folded(rows, parts):
    width = rows.shape[1]
    split = rows.reshape(parts, FOLD, -1, width).transpose(0, 2, 1, 3)
    return split.reshape(-1, FOLD * width)


def unfolded_rows(rows, parts):
    width = rows.shape[1] // FOLD
    split = rows.reshape(parts, -1, FOLD, width).transpose(0, 2, 1, 3)
    return split.reshape(-1, width)


def half_of(array, which):
    width = array.shape[1] // 2
    return lax.dynamic_slice_in_dim(array, which * width, width, 1)


def half_slots(array, which):
    length = array.shape[0] // 2
    return lax.dynamic_slice_in_dim(array, which * length, length, 0)


def ordered(is_first, mine, other):
    return (jnp.where(is_first, mine, other), jnp.where(is_first, other, mine))


def on_device(
    ends_in,
    lengths,
    qkv_weight,
    qkv_bias,
    out_weight,
    up_weight,
    up_bias,
    down_weight,
    out_biases,
    norm_gains,
    norm_biases,
):
    section_index = lax.axis_index("section")
    is_first = section_index == 0
    side = section_index.astype(jnp.int32).reshape(1)
    features = ends_in.shape[2]
    width = features // 2
    count = lax.axis_size("dp")
    own_rows = ends_in[0]
    slot_count = own_rows.shape[0] // 2
    kept_rows = half_slots(own_rows, section_index)
    other_rows = swap_cores(half_slots(own_rows, 1 - section_index))
    entry, cotangent = ordered(is_first, kept_rows, other_rows)
    segment, position = layouts(
        lax.dynamic_index_in_dim(lengths, section_index, 0, keepdims=False), slot_count
    )
    tables = rotary_tables(position)
    mask = allowed_transposed(segment)

    def both(take):
        kept = take(section_index)
        other = swap_cores(take(1 - section_index))
        return ordered(is_first, kept, other)

    def take_narrow(which):
        thirds = [
            qkv_weight[0, :, part * features : (part + 1) * features] for part in range(3)
        ]
        return jnp.concatenate([half_of(part, which) for part in thirds + [out_weight[0]]], axis=1)

    pieces = (
        both(take_narrow),
        both(lambda which: half_of(up_weight[0], which)),
        both(lambda which: half_of(down_weight[0], which)),
    )

    small_shapes = [
        (qkv_bias.shape[1],),
        (up_bias.shape[1],),
        out_biases.shape[1:],
        norm_gains.shape[1:],
        norm_biases.shape[1:],
    ]
    small_own = jnp.concatenate(
        [a[0].reshape(-1) for a in (qkv_bias, up_bias, out_biases, norm_gains, norm_biases)]
    )
    small_both = jnp.concatenate(ordered(is_first, small_own, swap_cores(small_own)))
    shards = (qkv_bias.shape[1], up_bias.shape[1], norm_gains.shape[2])
    kept_forward = {}
    slabs = {}

    def attn_step(layer, rows):
        kept_forward[layer, "rows"] = rows
        made = attn_forward(side, rows, tables, mask, small[layer], *slabs[layer, "narrow"])
        kept_forward[layer, "attn"] = made
        return made

    def mlp_step(layer, kind):
        passed = kept_forward[layer, "attn"][3]
        rows = kept_forward[layer, "rows"]
        made = mlp_forward(
            side, rows, passed, small[layer], slabs[layer, "mlp"], places[layer], kind
        )
        kept_forward[layer, "mlp"] = made
        return made

    def mlp_back(layer, grad):
        rows = kept_forward[layer, "rows"]
        return mlp_backward(
            side, rows, grad, small[layer], kept_forward[layer, "mlp"][:2],
            slabs[layer, "mlp"], places[layer],
        )

    def attn_back(layer, grad, grad_mlp, kind):
        return attn_backward(
            side, kept_forward[layer, "rows"], grad, tables, mask, small[layer],
            kept_forward[layer, "attn"][:3], grad_mlp, *slabs[layer, "narrow"], kind,
        )

    def vector_of(bias_qkv, bias_up, sums):
        parts = [
            bias_qkv[half : half + 1, part * width : (part + 1) * width]
            for part in range(3)
            for half in range(2)
        ]
        order = (4, 4, 0, 1, 2, 3)
        parts += [bias_up] + [sums[index : index + 1] for index in order]
        return jnp.concatenate(parts, axis=1)

    small = []

    def spread_out(rows):
        spread = spread_small(side, rows, shards, features)
        for layer in range(2):
            made = (part[layer] for part in spread)
            small.append(dict(zip(("qkv", "up", "out", "norms"), made)))

    places = ((0, 1), (0, 1))
    if small_slice():
        narrow, up, down = pieces
        wide = [
            jnp.concatenate([up[layer], folded(down[layer], 1)], axis=1) for layer in range(2)
        ]
        lower = jnp.concatenate([narrow[0], wide[0]], axis=1)
        columns = narrow[0].shape[1]
        whole_b = gather_whole(wide[1])
        ring_a = ring_moved(lower)
        line = small_both[None]
        column_a = column_of(lower, ring_a)
        column_a, next_c, line, entry, cotangent = after(
            (column_a, narrow[1], line, entry, cotangent), ring_a
        )
        near_a = near_moved(column_a)
        ring_c = ring_moved(next_c)
        ring_s = ring_moved(line)
        column_c = column_of(next_c, ring_c)
        column_s = line_placed(ring_order(), [line] + ring_s)
        lows, column_c, column_s = after(
            (cut_near(near_a), column_c, column_s), (near_a, ring_c, ring_s)
        )
        far_a = far_moved(lows)
        near_c = near_moved(column_c)
        square_s = square_moved(column_s)
        rows_s = line_placed(square_order(), [column_s] + square_s)
        spread_out(rows_s.transpose(1, 0, 2, 3).reshape(PARTS, -1))
        parts_a = (column_a,) + near_a + far_a
        lows, parts_a, small = after(
            (cut_near(near_c), parts_a, small), (far_a, near_c, small, whole_b)
        )
        whole_a = place_blocks(parts_a, (columns, 2 * columns))
        far_c = far_moved(lows)
        slabs[0, "narrow"] = (whole_a[0], swap_cores(whole_a[0]))
        swapped_a = swap_cores(whole_a[1])
        slabs[0, "mlp"] = (whole_a[1], swapped_a) * 2
        attn_step(0, entry)
        (whole_c,) = place_blocks((column_c,) + near_c + far_c, (columns,))
        slabs[1, "narrow"] = (whole_c, swap_cores(whole_c))
        swapped_b = swap_cores(whole_b)
        slabs[1, "mlp"] = (whole_b, swapped_b) * 2
        mlp_step(0, jnp.bfloat16)
        attn_step(1, kept_forward[0, "mlp"][2])
        mlp_step(1, jnp.float32)
    else:
        spread_out(gather_whole(small_both[None]))
        for layer in range(2):
            narrow, up, down = (gather_whole(piece[layer]) for piece in pieces)
            wide = jnp.concatenate([up, folded(down, PARTS)], axis=1)
            slabs[layer, "narrow"] = (narrow, swap_cores(narrow))
            slabs[layer, "mlp"] = (wide, swap_cores(wide)) * 2
        attn_step(0, entry)
        mlp_step(0, jnp.bfloat16)
        attn_step(1, kept_forward[0, "mlp"][2])
        mlp_step(1, jnp.float32)
    produced = kept_forward[1, "mlp"][2]

    def mlp_pairs(made):
        return (made[0], swap_cores(made[1]), made[2], swap_cores(made[3]))

    if small_slice():
        upper = mlp_back(1, cotangent)
        pairs_a = mlp_pairs(upper)
        upper_attn = attn_back(1, cotangent, upper[5], jnp.bfloat16)
        leaving_a = far_blocks(after(pairs_a, upper_attn[2]))
        far_a = sent_both(leaving_a)
        grad_middle = after(upper_attn[4], leaving_a)
        received_b = swap_cores(upper_attn[1])
        lower = mlp_back(0, grad_middle)
        leaving_a = near_blocks(pairs_a, after(far_a, lower[4]))
        near_a = sent_both(leaving_a)
        steps_b = ring_steps(upper_attn[0], after(received_b, lower[4]))
        moved_b = next(steps_b)
        pairs_c = mlp_pairs(lower)
        lower_attn = attn_back(
            0, grad_middle, lower[5], jnp.float32
        )
        pairs_d = (lower_attn[0], swap_cores(lower_attn[1]))
        moved_b = next(steps_b)
        pairs_c = after(pairs_c, (lower_attn[2], near_a))
        far_c = sent_both(far_blocks(pairs_c))
        pairs_d = after(pairs_d, near_a)
        far_d = sent_both(far_blocks(pairs_d))
        moved_b = next(steps_b)
        parts_a = column_sent(pairs_a, after(near_a, far_c))
        near_c = sent_both(near_blocks(pairs_c, after(far_c, far_d)))
        blocks_b = next(steps_b)
        near_d = sent_both(near_blocks(pairs_d, after(far_d, near_c)))
        parts_c = column_sent(pairs_c, near_c)
        parts_b = square_sent(after(blocks_b, near_c))
        parts_d = column_sent(pairs_d, after(near_d, near_c))
        reduced = (
            (total_of(parts_d), total_of(parts_b)),
            (total_of(parts_c), total_of(parts_a)),
        )
    else:
        upper = mlp_back(1, cotangent)
        upper_attn = attn_back(1, cotangent, upper[5], jnp.bfloat16)
        lower = mlp_back(0, upper_attn[4])
        lower_attn = attn_back(0, upper_attn[4], lower[5], jnp.float32)

        def spread(kept, received):
            summed = kept.astype(jnp.float32) + received.astype(jnp.float32)
            return lax.psum_scatter(summed, "dp", scatter_dimension=0, tiled=True)

        def spread_mlp(made):
            up_kept, up_got, down_kept, down_got = mlp_pairs(made)
            down = spread(unfolded_rows(down_kept, PARTS), unfolded_rows(down_got, PARTS))
            return jnp.concatenate([spread(up_kept, up_got), folded(down, 1)], axis=1)

        reduced = (
            tuple(spread(made[0], swap_cores(made[1])) for made in (lower_attn, upper_attn)),
            tuple(spread_mlp(made) for made in (lower, upper)),
        )
    grad_entry = lower_attn[4]
    def finish(lower, upper):
        mine, leaving = ordered(is_first, lower, upper)
        return ordered(is_first, mine, swap_cores(leaving))

    narrow_halves, mlp_halves = (finish(*pair) for pair in reduced)
    up_width = up_weight.shape[2] // 2
    total_up = jnp.concatenate([part[:, :up_width] for part in mlp_halves], axis=1)
    total_down = jnp.concatenate(
        [unfolded_rows(part[:, up_width:], 1) for part in mlp_halves], axis=1
    )
    total_qkv = jnp.concatenate(
        [
            part[:, at * width : (at + 1) * width]
            for at in range(3)
            for part in narrow_halves
        ],
        axis=1,
    )
    total_out = jnp.concatenate([part[:, 3 * width :] for part in narrow_halves], axis=1)

    vectors = [
        vector_of(attn[2], mlp[4], attn[3])
        for mlp, attn in ((lower, lower_attn), (upper, upper_attn))
    ]
    vector_kept, vector_sent = ordered(is_first, *vectors)
    if small_slice():
        vector = vector_kept + swap_cores(vector_sent)
        vector = total_of([vector] + square_moved(vector))
        vector = total_of([vector] + ring_moved(after(vector, near_c)))
    else:
        vector = lax.psum(vector_kept + swap_cores(vector_sent), "dp")
    place = lax.axis_index("dp")
    small_outs = []
    at = 0
    for shape in small_shapes:
        lead, size = (1,) if len(shape) == 1 else (shape[0],), shape[-1]
        rows = vector[0, at : at + lead[0] * size * count].reshape(lead[0], count * size)
        at += lead[0] * size * count
        part = lax.dynamic_slice_in_dim(rows, place * size, size, 1)
        small_outs.append(part.reshape((1,) + shape))

    staying, leaving = ordered(is_first, grad_entry, produced)
    ends_out = jnp.concatenate(ordered(is_first, staying, swap_cores(leaving)))
    return (
        ends_out[None],
        total_qkv[None],
        small_outs[0],
        total_out[None],
        total_up[None],
        small_outs[1],
        total_down[None],
        small_outs[2],
        small_outs[3],
        small_outs[4],
    )


def solution(mesh):
    return jax.shard_map(
        on_device,
        mesh=mesh,
        in_specs=(
            P("section", "dp", None),
            P("dp", None),
            P("section", "dp", None),
            P("section", "dp"),
            P("section", "dp", None),
            P("section", "dp", None),
            P("section", "dp"),
            P("section", "dp", None),
            P("section", None, "dp"),
            P("section", None, "dp"),
            P("section", None, "dp"),
        ),
        out_specs=(
            P("section", "dp", None),
            P("section", "dp", None),
            P("section", "dp"),
            P("section", "dp", None),
            P("section", "dp", None),
            P("section", "dp"),
            P("section", "dp", None),
            P("section", None, "dp"),
            P("section", None, "dp"),
            P("section", None, "dp"),
        ),
        check_vma=False,
    )
```
